32 devices in a mesh: seq: 2 (over x), rows: 16 (over z, y, core).
Axes of the slice: x: 2, y: 2, z: 4, core: 2. Of those that a mesh axis runs over, the one named last changes fastest.
Arguments:
- inputs: bfloat16 [32, 1024, 768], P('rows', 'seq'), may hold values from -6 to 6
- timesteps: int32 [32], P('rows'), may hold values from 0 to 999
- boundary: int32 [16], P('rows'), may hold values from 0 to 1
- step_table: bfloat16 [1000, 768], P(None, ('seq', 'rows')), may hold values from -3 to 3
- w_qkv: bfloat16 [768, 2304], P(('seq', 'rows')), may hold values from -0.21875 to 0.21875
- w_out: bfloat16 [768, 768], P(('seq', 'rows')), may hold values from -0.875 to 0.875
- w_up: bfloat16 [768, 3072], P(('seq', 'rows')), may hold values from -0.21875 to 0.21875
- w_down: bfloat16 [3072, 768], P(('seq', 'rows')), may hold values from -0.109375 to 0.109375
- norm1_gain: bfloat16 [768], P(('seq', 'rows')), may hold values from 0.5 to 1.5
- norm1_shift: bfloat16 [768], P(('seq', 'rows')), may hold values from -1.5 to 1.5
- norm2_gain: bfloat16 [768], P(('seq', 'rows')), may hold values from 0.5 to 1.5
- norm2_shift: bfloat16 [768], P(('seq', 'rows')), may hold values from -1.5 to 1.5
- up_bias: bfloat16 [3072], P(('seq', 'rows')), may hold values from -2.5 to 2.5
- down_bias: bfloat16 [768], P(('seq', 'rows')), may hold values from -1.5 to 1.5
- cotangent: bfloat16 [32, 1024, 768], P('rows', 'seq'), may hold values from -6 to 6
Outputs:
- block_out: bfloat16 [32, 1024, 768], P('rows', 'seq')
- grad_inputs: bfloat16 [32, 1024, 768], P('rows', 'seq')
- grad_step_table: float32 [1000, 768], P(None, ('seq', 'rows'))
- grad_w_qkv: float32 [768, 2304], P(('seq', 'rows'))
- grad_w_out: float32 [768, 768], P(('seq', 'rows'))
- grad_w_up: float32 [768, 3072], P(('seq', 'rows'))
- grad_w_down: float32 [3072, 768], P(('seq', 'rows'))
- grad_norm1_gain: float32 [768], P(('seq', 'rows'))
- grad_norm1_shift: float32 [768], P(('seq', 'rows'))
- grad_norm2_gain: float32 [768], P(('seq', 'rows'))
- grad_norm2_shift: float32 [768], P(('seq', 'rows'))
- grad_up_bias: float32 [3072], P(('seq', 'rows'))
- grad_down_bias: float32 [768], P(('seq', 'rows'))
The draws below stay inside these ranges and needn't reach their ends.
All inputs are finite; a program needn't handle non-finite values.
Results may differ from the reference program's by a relative error of at most 0.008.
Values may be sent and summed in bfloat16 or wider, within the bound.
No kernel may reach another device: no remote copies, remote signals or barrier semaphores. Data moves between devices by JAX's collectives and lax.ppermute only.
A program may use at most 192 MiB of HBM per device.

```python
import math
from functools import partial
import jax
import jax.numpy as jnp
from jax import lax

D = 768
H = 12
HD = 64
FF = 3072
STEPS = 1000
SLOT = 1024
ROWS_DEV = 2
HALF = 512
ROWS = 32
GROUPS = 16


def plant(drawn, rng, smallest, largest):
    index_at = [jax.random.randint(jax.random.fold_in(rng, axis), (), 0, length) for axis, length in enumerate(drawn.shape)]
    widest = drawn.shape.index(max(drawn.shape))
    neighbour = index_at[:widest] + [(index_at[widest] + 1) % drawn.shape[widest]] + index_at[widest + 1:]
    return drawn.at[tuple(index_at)].set(smallest).at[tuple(neighbour)].set(largest)


def level_of(own_key, dims, shards, least, largest):
    def one(axis_at, blocks):
        steps = jax.random.uniform(jax.random.fold_in(jax.random.fold_in(own_key, 6), axis_at), (blocks,), jnp.float32, least / len(shards), largest / len(shards))
        return jnp.repeat(jnp.exp(steps), dims[axis_at] // blocks).reshape((-1,) + (1,) * (len(dims) - axis_at - 1))

    factor_of = one(*shards[0])
    for cut in shards[1:]:
        factor_of = factor_of * one(*cut)
    return factor_of


def bell_draw(key, shape, deviation, reach, cuts=(), kind=jnp.bfloat16):
    values = deviation * jax.random.normal(key, shape, jnp.float32)
    if cuts:
        values = values * level_of(key, shape, cuts, -0.22, 0.18)
    return jnp.clip(values, -reach, reach).astype(kind)


def setup_inputs(seed: int = 0) -> dict:
    key_of = jax.random.split(jax.random.key(seed), 16)
    return {
        "inputs": bell_draw(key_of[0], (ROWS, SLOT, D), 1.0, 6.0, ((0, 16), (1, 2))),
        "timesteps": plant(jax.random.randint(key_of[1], (ROWS,), 0, STEPS), jax.random.fold_in(key_of[1], 1), 0, STEPS - 1).astype(jnp.int32),
        "boundary": plant(jax.random.randint(key_of[2], (GROUPS,), 0, ROWS_DEV), jax.random.fold_in(key_of[2], 1), 0, ROWS_DEV - 1).astype(jnp.int32),
        "step_table": bell_draw(key_of[3], (STEPS, D), 0.5, 3.0, ((1, 32),)),
        "w_qkv": bell_draw(key_of[4], (D, 3 * D), D ** -0.5, 0.21875, ((0, 32),)),
        "w_out": bell_draw(key_of[5], (D, D), (D // 16) ** -0.5, 0.875, ((0, 32),)),
        "w_up": bell_draw(key_of[6], (D, FF), D ** -0.5, 0.21875, ((0, 32),)),
        "w_down": bell_draw(key_of[7], (FF, D), FF ** -0.5, 0.109375, ((0, 32),)),
        "norm1_gain": jnp.clip(1.0 + 0.1 * jax.random.normal(key_of[8], (D,), jnp.float32), 0.5, 1.5).astype(jnp.bfloat16),
        "norm1_shift": bell_draw(key_of[9], (D,), 0.3, 1.5, ((0, 32),)),
        "norm2_gain": jnp.clip(1.0 + 0.1 * jax.random.normal(key_of[10], (D,), jnp.float32), 0.5, 1.5).astype(jnp.bfloat16),
        "norm2_shift": bell_draw(key_of[11], (D,), 0.3, 1.5, ((0, 32),)),
        "up_bias": bell_draw(key_of[12], (FF,), 0.5, 2.5, ((0, 32),)),
        "down_bias": bell_draw(key_of[13], (D,), 0.3, 1.5, ((0, 32),)),
        "cotangent": bell_draw(key_of[14], (ROWS, SLOT, D), 1.0, 6.0, ((0, 16), (1, 2))),
    }


epsilon = 1e-05
highest = lax.Precision.HIGHEST

@jax.custom_vjp
def low(v):
    return lax.optimization_barrier(v.astype(jnp.bfloat16)).astype(jnp.float32)

@jax.custom_vjp
def low_back(v):
    return v

def low_keep(v):
    return (low(v), None)

def low_pass(kept, grad):
    return (grad,)

def back_keep(v):
    return (v, None)

def back_low(kept, grad):
    return (low(grad),)
low.defvjp(low_keep, low_pass)
low_back.defvjp(back_keep, back_low)

def layer_norm(values, norm_gain, norm_shift):
    average = lax.optimization_barrier(jnp.mean(values, axis=-1, keepdims=True))
    centred = values - average
    spread = lax.optimization_barrier(jnp.mean(centred * centred, axis=-1, keepdims=True))
    return centred * lax.rsqrt(spread + epsilon) * norm_gain + norm_shift

def block_rows(weights, hidden, short_rows):
    w_qkv, w_out, w_up, w_down, gain_one, shift_one, gain_two, shift_two, up_shift, down_shift = weights
    count = hidden.shape[0]
    normed = low(layer_norm(hidden, gain_one, shift_one))
    projected = jnp.einsum('bsd,de->bse', normed, w_qkv, precision=highest)
    projected = low_back(low(projected)).reshape(count, SLOT, 3, H, HD)
    query = projected[:, :, 0]
    keys = projected[:, :, 1]
    values = projected[:, :, 2]
    raw = jnp.einsum('bqhe,bkhe->bhqk', query, keys, precision=highest)
    scores = low_back(raw * HD ** (-0.5))
    places = jnp.arange(SLOT)
    same_half = places[:, None] // HALF == places[None, :] // HALF
    allowed = jnp.logical_or(jnp.logical_not(short_rows)[:, None, None], same_half[None])
    scores = jnp.where(allowed[:, None], scores, -1e+30)
    probs = jax.nn.softmax(scores, axis=-1)
    attended = jnp.einsum('bhqk,bkhe->bqhe', low(probs), values, precision=highest).reshape(count, SLOT, D)
    attended = low_back(low(attended))
    middle = hidden + low_back(jnp.einsum('bsd,de->bse', attended, w_out, precision=highest))
    normed_two = low(layer_norm(middle, gain_two, shift_two))
    upper = low_back(jnp.einsum('bsd,df->bsf', normed_two, w_up, precision=highest) + up_shift)
    active = low(jax.nn.gelu(upper, approximate=False))
    return middle + low_back(jnp.einsum('bsf,fd->bsd', active, w_down, precision=highest) + down_shift)

def reference(inputs, timesteps, boundary, step_table, w_qkv, w_out, w_up, w_down, norm1_gain, norm1_shift, norm2_gain, norm2_shift, up_bias, down_bias, cotangent):
    row_index = jnp.arange(ROWS, dtype=jnp.int32)
    short_all = row_index % ROWS_DEV < jnp.take(boundary, row_index // ROWS_DEV)
    per_block = math.gcd(ROWS, max(1, 4096 // SLOT))
    blocks_count = ROWS // per_block
    floats = [piece.astype(jnp.float32) for piece in (inputs, step_table, w_qkv, w_out, w_up, w_down, norm1_gain, norm1_shift, norm2_gain, norm2_shift, up_bias, down_bias)]

    def forward(inputs_f, table_f, *weights):
        base = inputs_f + jnp.take(table_f, timesteps, axis=0)[:, None, :]
        blocked = base.reshape(blocks_count, per_block, SLOT, D)
        flags = short_all.reshape(blocks_count, per_block)
        mapped = jax.checkpoint(partial(block_rows, weights))

        def scan_body(carried, paired):
            return (carried, mapped(paired[0], paired[1]))
        unused, results = lax.scan(scan_body, None, (blocked, flags))
        return results.reshape(ROWS, SLOT, D)
    outputs, pullback = jax.vjp(forward, *floats)
    grads = pullback(cotangent.astype(jnp.float32))
    return (outputs.astype(jnp.bfloat16), grads[0].astype(jnp.bfloat16), grads[1], grads[2], grads[3], grads[4], grads[5], grads[6], grads[7], grads[8], grads[9], grads[10], grads[11])
```

```python
import functools

import jax
import jax.numpy as jnp
from jax import lax
from jax.experimental import pallas as pl
from jax.experimental.pallas import tpu as pltpu
from jax.sharding import PartitionSpec as P

f32 = jnp.float32
bf16 = jnp.bfloat16
HD = 64
EPS = 1e-5
LOG2E = 1.4426950408889634
VMEM = 56 * 1024 * 1024
BOTH = ("seq", "rows")
WEIGHT = 0.02


def nn(a, b):
    return lax.dot_general(a, b, (((1,), (0,)), ((), ())), preferred_element_type=f32)


def nt(a, b):
    return lax.dot_general(a, b, (((1,), (1,)), ((), ())), preferred_element_type=f32)


def tn(a, b):
    return lax.dot_general(a, b, (((0,), (0,)), ((), ())), preferred_element_type=f32)


def sds(shape, dtype):
    return jax.ShapeDtypeStruct(shape, dtype)


def whole(*shape):
    return pl.BlockSpec(shape, lambda *_: (0,) * len(shape))


def params():
    return pltpu.CompilerParams(vmem_limit_bytes=VMEM, dimension_semantics=("arbitrary",))


def cost(flops, nbytes, trans=0):
    return pl.CostEstimate(
        flops=int(flops * WEIGHT), bytes_accessed=int(nbytes * WEIGHT), transcendentals=int(trans * WEIGHT)
    )


def norm_parts(v):
    c = v - jnp.mean(v, axis=1, keepdims=True)
    s = lax.rsqrt(jnp.mean(c * c, axis=1, keepdims=True) + EPS)
    return c * s, s


def norm_back(e, gain, xhat, s):
    f = e * gain
    return s * (
        f
        - jnp.mean(f, axis=1, keepdims=True)
        - xhat * jnp.mean(f * xhat, axis=1, keepdims=True)
    )


def norm_one_kernel(x_ref, row_ref, n_ref):
    xhat, _ = norm_parts(x_ref[...].astype(f32) + row_ref[0:1, :])
    n_ref[...] = (xhat * row_ref[1:2, :] + row_ref[2:3, :]).astype(bf16)


def norm_one(x, rows, tb=256):
    t, d = x.shape
    tok = pl.BlockSpec((tb, d), lambda i: (i, 0))
    return pl.pallas_call(
        norm_one_kernel,
        grid=(t // tb,),
        in_specs=[tok, whole(*rows.shape)],
        out_specs=tok,
        out_shape=sds((t, d), bf16),
        compiler_params=params(),
        cost_estimate=cost(10 * t * d, 4 * t * d),
        name="norm_one",
    )(x, rows)


def attend_kernel(
    short_ref, n_ref, wq_ref, wk_ref, wv_ref, q_ref, k_ref, v_ref, o_ref, lse_ref, *, heads, qb
):
    t = n_ref.shape[0]
    n = n_ref[...]
    q_ref[...] = nn(n, wq_ref[...]).astype(bf16)
    k_ref[...] = nn(n, wk_ref[...]).astype(bf16)
    v_ref[...] = nn(n, wv_ref[...]).astype(bf16)

    def run(parts):
        span = t // parts
        for h in range(heads):
            hs = slice(h * HD, (h + 1) * HD)
            for q0 in range(0, t, qb):
                k0 = (q0 // span) * span
                q = q_ref[q0 : q0 + qb, hs] * bf16(0.125)
                s = nt(k_ref[k0 : k0 + span, hs], q)
                top = jnp.max(s, axis=0, keepdims=True)
                p = jnp.exp2((s - top) * f32(LOG2E))
                total = jnp.sum(p, axis=0, keepdims=True)
                probs = (p * (1.0 / total)).astype(bf16)
                o_ref[q0 : q0 + qb, hs] = tn(probs, v_ref[k0 : k0 + span, hs]).astype(bf16)
                lse_ref[0, h : h + 1, q0 : q0 + qb] = top + jnp.log(total)

    short = short_ref[0]

    @pl.when(short == 0)
    def _():
        run(1)

    @pl.when(short != 0)
    def _():
        run(2)


def attend(short, n, w_qk, w_v, heads=4, qb=256):
    t, d = n.shape
    c = heads * HD
    groups = d // c

    def col(part):
        return pl.BlockSpec((d, c), lambda g, s: (0, part * groups + g))

    tok = pl.BlockSpec((t, c), lambda g, s: (0, g))
    return pl.pallas_call(
        functools.partial(attend_kernel, heads=heads, qb=qb),
        grid_spec=pltpu.PrefetchScalarGridSpec(
            num_scalar_prefetch=1,
            grid=(groups,),
            in_specs=[whole(t, d), col(0), col(1), col(0)],
            out_specs=[tok] * 4 + [pl.BlockSpec((1, heads, t), lambda g, s: (g, 0, 0))],
        ),
        out_shape=[sds((t, d), bf16)] * 4 + [sds((groups, heads, t), f32)],
        compiler_params=params(),
        cost_estimate=cost(6 * t * d * d + 16 * t * t * d, 20 * t * d, t * t * d // HD),
        name="attend",
    )(short, n, w_qk, w_qk, w_v)


def attend_back_kernel(
    short_ref, q_ref, k_ref, v_ref, o_ref, do_ref, lse_ref, dq_ref, dk_ref, dv_ref, *, heads, qb
):
    t = q_ref.shape[0]

    def run(parts):
        span = t // parts
        for h in range(heads):
            hs = slice(h * HD, (h + 1) * HD)
            for b in range(parts):
                ks = slice(b * span, (b + 1) * span)
                k = k_ref[ks, hs]
                v = v_ref[ks, hs]
                dk = dv = None
                for q0 in range(b * span, (b + 1) * span, qb):
                    qs = slice(q0, q0 + qb)
                    q = q_ref[qs, hs] * bf16(0.125)
                    do = do_ref[qs, hs]
                    prod = do.astype(f32) * o_ref[qs, hs].astype(f32)
                    delta = jnp.sum(jnp.transpose(prod), axis=0, keepdims=True)
                    p = jnp.exp2((nt(k, q) - lse_ref[0, h : h + 1, qs]) * f32(LOG2E))
                    ds = (p * (nt(v, do) - delta)).astype(bf16)
                    dv_part = nn(p.astype(bf16), do)
                    dk_part = nn(ds, q)
                    dv = dv_part if dv is None else dv + dv_part
                    dk = dk_part if dk is None else dk + dk_part
                    dq_ref[qs, hs] = (tn(ds, k) * f32(0.125)).astype(bf16)
                dk_ref[ks, hs] = dk.astype(bf16)
                dv_ref[ks, hs] = dv.astype(bf16)

    short = short_ref[0]

    @pl.when(short == 0)
    def _():
        run(1)

    @pl.when(short != 0)
    def _():
        run(2)


def attend_back(short, q, k, v, o, do, lse, part, parts, heads=2, qb=256):
    t, d = q.shape
    c = heads * HD
    count = d // c // parts
    first = part * count
    tok = pl.BlockSpec((t, c), lambda g, s: (0, first + g))
    out = pl.BlockSpec((t, c), lambda g, s: (0, g))
    d = d // parts
    return pl.pallas_call(
        functools.partial(attend_back_kernel, heads=heads, qb=qb),
        grid_spec=pltpu.PrefetchScalarGridSpec(
            num_scalar_prefetch=1,
            grid=(count,),
            in_specs=[tok] * 5 + [pl.BlockSpec((1, heads, t), lambda g, s: (first + g, 0, 0))],
            out_specs=[out] * 3,
        ),
        out_shape=[sds((t, d), bf16)] * 3,
        compiler_params=params(),
        cost_estimate=cost(40 * t * t * d, 16 * t * d, t * t * d // HD),
        name=f"attend_back_{part}",
    )(short, q, k, v, o, do, lse.reshape(-1, heads, t))


def mix_kernel(x_ref, o_ref, w_ref, row_ref, mid_ref, n_ref):
    mid = x_ref[...].astype(f32) + row_ref[0:1, :] + nn(o_ref[...], w_ref[...])
    mid_ref[...] = mid
    xhat, _ = norm_parts(mid)
    n_ref[...] = (xhat * row_ref[3:4, :] + row_ref[4:5, :]).astype(bf16)


def mix(x, o, up_out, rows, tb=256):
    t, d = x.shape
    tok = pl.BlockSpec((tb, d), lambda i: (i, 0))
    last = up_out.shape[1] // d - 1
    return pl.pallas_call(
        mix_kernel,
        grid=(t // tb,),
        in_specs=[tok, tok, pl.BlockSpec((d, d), lambda i: (0, last)), whole(*rows.shape)],
        out_specs=[tok, tok],
        out_shape=[sds((t, d), f32), sds((t, d), bf16)],
        compiler_params=params(),
        cost_estimate=cost(2 * t * d * d, 12 * t * d),
        name="mix",
    )(x, o, up_out, rows)


def gelu_parts(u):
    e = jnp.exp(u * u * f32(-0.5))
    r = pl.reciprocal(1.0 + f32(0.3275911 * 0.7071067811865476) * jnp.abs(u))
    poly = f32(-1.453152027) + r * f32(1.061405429)
    poly = f32(1.421413741) + r * poly
    poly = f32(-0.284496736) + r * poly
    poly = r * (f32(0.254829592) + r * poly)
    tail = f32(0.5) * poly * e
    return jnp.where(u >= 0, 1.0 - tail, tail), e * f32(0.3989422804014327)


def ffn_kernel(
    n_ref, dy_ref, mid_ref, wu_ref, wd_ref, ub_ref, row_ref,
    out_ref, du_ref, gwd_ref, gub_ref, small_ref, acc,
):
    j = pl.program_id(0)

    @pl.when(j == 0)
    def _():
        acc[...] = mid_ref[...] + row_ref[5:6, :]

    dy = dy_ref[...]
    wd = wd_ref[...]
    u = nn(n_ref[...], wu_ref[...]) + ub_ref[...].astype(f32)
    cdf, pdf = gelu_parts(u)
    active = (u * cdf).astype(bf16)
    acc[...] += nn(active, wd)
    gwd_ref[...] = tn(active, dy).astype(bf16)
    du = (nt(dy, wd) * (cdf + u * pdf)).astype(bf16)
    du_ref[...] = du
    gub_ref[...] = jnp.sum(du.astype(f32), axis=0, keepdims=True)

    @pl.when(j == pl.num_programs(0) - 1)
    def _():
        out_ref[...] = acc[...].astype(bf16)
        small_ref[...] = jnp.sum(dy_ref[...].astype(f32), axis=0, keepdims=True)


def ffn(n, dy, mid, up_out, down, up_bias, rows, fb=512):
    t, d = n.shape
    ff = down.shape[0]
    return pl.pallas_call(
        ffn_kernel,
        grid=(ff // fb,),
        in_specs=[
            whole(t, d),
            whole(t, d),
            whole(t, d),
            pl.BlockSpec((d, fb), lambda j: (0, j)),
            pl.BlockSpec((fb, d), lambda j: (j, 0)),
            pl.BlockSpec((1, fb), lambda j: (0, j)),
            whole(*rows.shape),
        ],
        out_specs=[
            whole(t, d),
            pl.BlockSpec((t, fb), lambda j: (0, j)),
            pl.BlockSpec((fb, d), lambda j: (j, 0)),
            pl.BlockSpec((1, fb), lambda j: (0, j)),
            whole(1, d),
        ],
        out_shape=[
            sds((t, d), bf16),
            sds((t, ff), bf16),
            sds((ff, d), bf16),
            sds((1, ff), f32),
            sds((1, d), f32),
        ],
        scratch_shapes=[pltpu.VMEM((t, d), f32)],
        compiler_params=params(),
        cost_estimate=cost(8 * t * d * ff, 20 * t * d + 8 * d * ff, 2 * t * ff),
        name="ffn",
    )(n, dy, mid, up_out, down, up_bias, rows)


def unffn_kernel(
    n_ref, dy_ref, mid_ref, du_ref, wu_ref, wo_ref, o_ref, row_ref,
    dmid_ref, do_ref, gwu_ref, gwo_ref, small_ref, acc, turned,
):
    j = pl.program_id(0)

    @pl.when(j == 0)
    def _():
        acc[...] = jnp.zeros_like(acc)
        turned[...] = n_ref[...].T

    du = du_ref[...]
    gwu_ref[...] = nn(turned[...], du).astype(bf16)
    acc[...] += nt(du, wu_ref[...])

    @pl.when(j == pl.num_programs(0) - 1)
    def _():
        xhat, s = norm_parts(mid_ref[...])
        e = acc[...]
        small_ref[...] = jnp.concatenate(
            [jnp.sum(e * xhat, axis=0, keepdims=True), jnp.sum(e, axis=0, keepdims=True)], axis=0
        )
        dmid = dy_ref[...].astype(f32) + norm_back(e, row_ref[3:4, :], xhat, s)
        dmid_ref[...] = dmid
        db = dmid.astype(bf16)
        do_ref[...] = nt(db, wo_ref[...]).astype(bf16)
        gwo_ref[...] = tn(o_ref[...], db).astype(bf16)


def unffn(n, dy, mid, du, up_out, o, rows, fb=512):
    t, d = n.shape
    ff = du.shape[1]
    last = up_out.shape[1] // d - 1
    return pl.pallas_call(
        unffn_kernel,
        grid=(ff // fb,),
        in_specs=[
            whole(t, d),
            whole(t, d),
            whole(t, d),
            pl.BlockSpec((t, fb), lambda j: (0, j)),
            pl.BlockSpec((d, fb), lambda j: (0, j)),
            pl.BlockSpec((d, d), lambda j: (0, last)),
            whole(t, d),
            whole(*rows.shape),
        ],
        out_specs=[
            whole(t, d),
            whole(t, d),
            pl.BlockSpec((d, fb), lambda j: (0, j)),
            whole(d, d),
            whole(2, d),
        ],
        out_shape=[
            sds((t, d), f32),
            sds((t, d), bf16),
            sds((d, ff), bf16),
            sds((d, d), bf16),
            sds((2, d), f32),
        ],
        scratch_shapes=[pltpu.VMEM((t, d), f32), pltpu.VMEM((d, t), bf16)],
        compiler_params=params(),
        cost_estimate=cost(4 * t * d * (ff + d), 20 * t * d + 8 * d * ff),
        name="unffn",
    )(n, dy, mid, du, up_out, up_out, o, rows)


def unqkv_kernel(
    x_ref, row_ref, n_ref, dmid_ref, wq_ref, wk_ref, wv_ref, dq_ref, dk_ref, dv_ref,
    dx_ref, gq_ref, gk_ref, gv_ref, small_ref, acc, turned,
):
    i = pl.program_id(0)

    @pl.when(i == 0)
    def _():
        turned[...] = n_ref[...].T

    n = turned[...]
    e = None
    for d_ref, w_ref, g_ref in (
        (dq_ref, wq_ref, gq_ref),
        (dk_ref, wk_ref, gk_ref),
        (dv_ref, wv_ref, gv_ref),
    ):
        piece = d_ref[...]
        g_ref[...] = nn(n, piece).astype(bf16)
        part = nt(piece, w_ref[...])
        e = part if e is None else e + part

    @pl.when(i == 0)
    def _():
        acc[...] = e

    @pl.when(i > 0)
    def _():
        acc[...] += e

    @pl.when(i == pl.num_programs(0) - 1)
    def _():
        e = acc[...]
        xhat, s = norm_parts(x_ref[...].astype(f32) + row_ref[0:1, :])
        d_base = dmid_ref[...] + norm_back(e, row_ref[1:2, :], xhat, s)
        dx_ref[...] = d_base.astype(bf16)
        small_ref[...] = jnp.concatenate(
            [
                jnp.sum(d_base, axis=0, keepdims=True),
                jnp.sum(e * xhat, axis=0, keepdims=True),
                jnp.sum(e, axis=0, keepdims=True),
                jnp.zeros((5, e.shape[1]), f32),
            ],
            axis=0,
        )


def unqkv(x, rows, n, dmid, w_qk, w_v, dq, dk, dv, cb=256):
    t, d = x.shape
    count = d // cb

    def col(part):
        return pl.BlockSpec((d, cb), lambda i: (0, part * count + i))

    tok = pl.BlockSpec((t, cb), lambda i: (0, i))
    return pl.pallas_call(
        unqkv_kernel,
        grid=(count,),
        in_specs=[whole(t, d), whole(*rows.shape), whole(t, d), whole(t, d)]
        + [col(0), col(1), col(0)]
        + [tok] * 3,
        out_specs=[whole(t, d)] + [col(0)] * 3 + [whole(8, d)],
        out_shape=[sds((t, d), bf16)] + [sds((d, d), bf16)] * 3 + [sds((8, d), f32)],
        scratch_shapes=[pltpu.VMEM((t, d), f32), pltpu.VMEM((d, t), bf16)],
        compiler_params=params(),
        cost_estimate=cost(12 * t * d * d, 30 * t * d),
        name="unqkv",
    )(x, rows, n, dmid, w_qk, w_qk, w_v, dq, dk, dv)


class Grid:
    def __init__(self, seq, rows):
        self.seq, self.rows = seq, rows
        self.known = seq == 2 and rows == 16
        at = lax.axis_index("rows")
        self.x = lax.axis_index("seq")
        self.z, self.y, self.c = at // 4, (at // 2) % 2, at % 2

    def table(self, move):
        pairs = []
        for x in range(self.seq):
            for z in range(4):
                for y in range(2):
                    for c in range(2):
                        x2, z2, y2, c2 = move(x, z, y, c)
                        pairs.append((x * 16 + z * 4 + y * 2 + c, x2 * 16 + z2 * 4 + y2 * 2 + c2))
        return pairs

    def swap(self, v, axis):
        move = {
            "x": lambda x, z, y, c: (1 - x, z, y, c),
            "y": lambda x, z, y, c: (x, z, 1 - y, c),
            "c": lambda x, z, y, c: (x, z, y, 1 - c),
        }[axis]
        return lax.ppermute(v, BOTH, self.table(move))

    def shift(self, v, by):
        return lax.ppermute(v, BOTH, self.table(lambda x, z, y, c: (x, (z + by) % 4, y, c)))


def after(v, *first):
    return lax.optimization_barrier((v, first))[0]


def spread(v, axis, count):
    return jnp.broadcast_to(jnp.expand_dims(v, axis), v.shape[:axis] + (count,) + v.shape[axis:])


def pair(own, other, at, axis):
    shape = own.shape[:axis] + (2,) + own.shape[axis:]
    here = lax.broadcasted_iota(jnp.int32, shape, axis) == at
    return jnp.where(here, spread(own, axis, 2), spread(other, axis, 2))


def gather_z(g, v, ring):
    out = spread(v, 0, 4)
    place = lax.broadcasted_iota(jnp.int32, out.shape, 0)
    last = v
    for k in range(1, 4):
        last = g.shift(last, 1) if ring else g.shift(v, k)
        out = jnp.where(place == (g.z - k) % 4, spread(last, 0, 4), out)
    return out


def gather_plane(g, a, b):
    a = pair(a, g.swap(a, "x"), g.x, 0)
    b = pair(b, g.swap(b, "y"), g.y, 1)
    yield a, b
    a = pair(a, g.swap(a, "y"), g.y, 2)
    b = pair(b, g.swap(b, "x"), g.x, 0)
    yield a, b


def gather_core(g, v):
    v = pair(v, g.swap(v, "c"), g.c, 3)
    return v.reshape(-1, v.shape[-1])


def keep(v, at, axis):
    return lax.dynamic_index_in_dim(v, at, axis, keepdims=False)


def add(a, b):
    return (a.astype(f32) + b.astype(f32)).astype(bf16)


def split_core(g, v):
    v = v.reshape(2, 4, 2, 2, -1, v.shape[-1])
    return add(keep(v, g.c, 3), g.swap(keep(v, 1 - g.c, 3), "c"))


def split_plane(g, a, b):
    a = add(keep(a, g.x, 0), g.swap(keep(a, 1 - g.x, 0), "x"))
    b = add(keep(b, g.y, 2), g.swap(keep(b, 1 - g.y, 2), "y"))
    yield a, b
    a = add(keep(a, g.y, 1), g.swap(keep(a, 1 - g.y, 1), "y"))
    b = add(keep(b, g.x, 0), g.swap(keep(b, 1 - g.x, 0), "x"))
    yield a, b


def split_z(g, v):
    total = keep(v, g.z, 0).astype(f32)
    for k in range(1, 4):
        total = total + g.shift(keep(v, (g.z + k) % 4, 0), k).astype(f32)
    return total


def scatter_plain(v):
    return lax.psum_scatter(v.astype(f32), BOTH, scatter_dimension=0, tiled=True)


def trade(v, at, rows):
    if rows:
        own = keep(v, at, 0)
        other = swap_seq(keep(v, 1 - at, 0))
        first, second = jnp.where(at == 0, own, other), jnp.where(at == 0, other, own)
        return jnp.concatenate([first, second], axis=0)
    v = v.reshape(2, v.shape[0] // 2, v.shape[1])
    own = keep(v, at, 0)
    other = swap_seq(keep(v, 1 - at, 0))
    return pair(own, other, at, 0)


def swap_seq(v):
    return lax.ppermute(v, "seq", [(0, 1), (1, 0)])


def local(
    inputs, timesteps, boundary, step_table, w_qkv, w_out, w_up, w_down,
    norm1_gain, norm1_shift, norm2_gain, norm2_shift, up_bias, down_bias, cotangent,
):
    seq, row_blocks = lax.axis_size("seq"), lax.axis_size("rows")
    g = Grid(seq, row_blocks)
    at = g.x
    devices = seq * row_blocks
    d = inputs.shape[2]
    shard = w_qkv.shape[0]
    ff = w_up.shape[1]
    steps = step_table.shape[0]
    wide = (ff // devices) // shard

    digits = jnp.stack([timesteps // 128, timesteps % 128], axis=1).astype(bf16)
    digits = jnp.pad(digits, ((0, shard - digits.shape[0]), (0, -(steps + 7 + wide) % 128)))
    short_ones = jnp.stack([norm1_gain, norm1_shift, norm2_gain, norm2_shift, down_bias], axis=1)
    table = jnp.concatenate(
        [step_table.T, short_ones, up_bias.reshape(shard, wide), digits], axis=1
    )
    up_out = jnp.concatenate([w_up, w_out], axis=1)
    x = trade(inputs, at, True)
    if g.known:
        qkv = gather_z(g, w_qkv, False)
        table = gather_z(g, table, False)
        up_out = gather_z(g, after(up_out, qkv), True)
        down = gather_z(g, after(w_down, qkv), True)
        qkv = after(qkv, x)
        w_qk, w_v = qkv[..., : 2 * d], jnp.concatenate([qkv[..., 2 * d :], table], axis=-1)
        plane = gather_plane(g, w_qk, w_v)
        next(plane)
        w_qk, w_v = next(plane)
        up_out, down = after((up_out, down), w_qk, w_v)
        table = gather_core(g, w_v[..., d:])
        w_qk, w_v = gather_core(g, w_qk), gather_core(g, w_v[..., :d])
        plane = gather_plane(g, up_out, down)
        next(plane)
    else:
        w_qk, w_v = w_qkv[:, : 2 * d], w_qkv[:, 2 * d :]
        table, w_qk, w_v, up_out, down = [
            lax.all_gather(v, BOTH, axis=0, tiled=True) for v in (table, w_qk, w_v, up_out, w_down)
        ]

    short = (at < boundary[0]).astype(jnp.int32).reshape(1)
    step = lax.dynamic_index_in_dim(timesteps, at, 0, keepdims=False)
    wanted = jnp.concatenate([step[None], jnp.arange(5 + wide, dtype=jnp.int32) + steps])
    wanted = jnp.pad(wanted, (0, -wanted.shape[0] % 8), constant_values=-1)
    pick = (wanted[:, None] == jnp.arange(table.shape[1], dtype=jnp.int32)[None]).astype(bf16)
    rows = nt(pick, table)
    up_row = rows[6 : 6 + wide].T.reshape(1, ff)
    digits = table[: shard * row_blocks, steps + 5 + wide : steps + 7 + wide]
    digits = digits.reshape(row_blocks, shard, 2)[:, : timesteps.shape[0]].reshape(-1, 2)
    digits = digits.astype(jnp.int32)
    all_steps = digits[:, 0] * 128 + digits[:, 1]

    normed_one = norm_one(x, rows)
    q, k, v, attended, lse = attend(short, normed_one, w_qk, w_v)
    dy = trade(after(cotangent, rows), at, True)
    if g.known:
        up_out, down = [gather_core(g, after(v, attended, dy)) for v in next(plane)]
    middle, normed_two = mix(x, attended, up_out, rows)
    result, d_upper, g_down, g_up_row, g_down_row = ffn(
        normed_two, dy, middle, up_out, down, up_row, rows
    )
    if g.known:
        down_cores = split_core(g, g_down)
    d_middle, d_attended, g_up, g_out, small_two = unffn(
        normed_two, dy, middle, d_upper, up_out, attended, rows
    )
    block_out = trade(result, at, False)
    g_up = jnp.concatenate([g_up, g_out], axis=1)
    half, cut = d // 2, (ff + d) // 2
    if g.known:
        down_plane = split_plane(g, down_cores[..., :half], down_cores[..., half:])
        d_attended = after(d_attended, block_out, down_cores)
    back = attend_back(short, q, k, v, attended, d_attended, lse, 0, 2)
    if g.known:
        up_cores = split_core(g, g_up)
        up_plane = split_plane(g, up_cores[..., :cut], up_cores[..., cut:])
        d_attended = after(d_attended, back, up_cores, next(down_plane))
    more = attend_back(short, q, k, v, attended, d_attended, lse, 1, 2)
    if g.known:
        down = jnp.concatenate(next(down_plane), axis=-1)
        d_middle = after(d_middle, more, down, next(up_plane))
    dq, dk, dv = [jnp.concatenate(both, axis=1) for both in zip(back, more)]
    d_x, g_q, g_k, g_v, small_one = unqkv(x, rows, normed_one, d_middle, w_qk, w_v, dq, dk, dv)
    grad_inputs = trade(d_x, at, False)

    row_count = devices
    mine = at + seq * lax.axis_index("rows")
    own_row = (jnp.arange(row_count, dtype=jnp.int32) == mine).astype(f32)
    small = jnp.concatenate(
        [
            small_one[1:3].T,
            small_two.T,
            g_down_row.T,
            g_up_row.reshape(d, wide),
            small_one[0][:, None] * own_row[None],
        ],
        axis=1,
    ).astype(bf16)
    small = jnp.pad(small, ((0, 0), (0, -small.shape[1] % 128)))
    g_qk = jnp.concatenate([g_q, g_k], axis=1)
    g_v = jnp.concatenate([g_v, small], axis=1)
    if g.known:
        up = jnp.concatenate(next(up_plane), axis=-1)
        sum_down, sum_up = split_z(g, down), split_z(g, up)
        plane = split_plane(g, split_core(g, g_qk), split_core(g, g_v))
        next(plane)
        last = split_z(g, jnp.concatenate(next(plane), axis=-1))
    else:
        sum_up, sum_down = scatter_plain(g_up), scatter_plain(g_down)
        last = scatter_plain(jnp.concatenate([g_qk, g_v], axis=1))
    sum_small = last[:, 3 * d :]
    row_sums = sum_small[:, 5 + wide : 5 + wide + row_count]
    hot = (jnp.arange(steps, dtype=jnp.int32)[:, None] == all_steps[None]).astype(f32)
    g_table = lax.dot_general(
        hot, row_sums, (((1,), (1,)), ((), ())), precision=lax.Precision.HIGHEST,
        preferred_element_type=f32,
    )
    return (
        block_out,
        grad_inputs,
        g_table,
        last[:, : 3 * d],
        sum_up[:, ff:],
        sum_up[:, :ff],
        sum_down,
        sum_small[:, 0],
        sum_small[:, 1],
        sum_small[:, 2],
        sum_small[:, 3],
        sum_small[:, 5 : 5 + wide].reshape(-1),
        sum_small[:, 4],
    )


def solution(mesh):
    tokens, weight, vector = P("rows", "seq", None), P(BOTH, None), P(BOTH)
    table = P(None, BOTH)
    in_specs = (
        (tokens, P("rows"), P("rows"), table) + (weight,) * 4 + (vector,) * 6 + (tokens,)
    )
    out_specs = (tokens, tokens, table) + (weight,) * 4 + (vector,) * 6
    return jax.shard_map(local, mesh=mesh, in_specs=in_specs, out_specs=out_specs, check_vma=False)
```

```python
import functools

import jax
import jax.numpy as jnp
from jax import lax
from jax.experimental import pallas as pl
from jax.experimental.pallas import tpu as pltpu
from jax.sharding import PartitionSpec as P

f32 = jnp.float32
bf16 = jnp.bfloat16
HD = 64
EPS = 1e-5
LOG2E = 1.4426950408889634
VMEM = 56 * 1024 * 1024
BOTH = ("seq", "rows")
WEIGHT = 0.02


def nn(a, b):
    return lax.dot_general(a, b, (((1,), (0,)), ((), ())), preferred_element_type=f32)


def nt(a, b):
    return lax.dot_general(a, b, (((1,), (1,)), ((), ())), preferred_element_type=f32)


def tn(a, b):
    return lax.dot_general(a, b, (((0,), (0,)), ((), ())), preferred_element_type=f32)


def sds(shape, dtype):
    return jax.ShapeDtypeStruct(shape, dtype)


def whole(*shape):
    return pl.BlockSpec(shape, lambda *_: (0,) * len(shape))


def params():
    return pltpu.CompilerParams(vmem_limit_bytes=VMEM, dimension_semantics=("arbitrary",))


def cost(flops, nbytes, trans=0):
    return pl.CostEstimate(
        flops=int(flops * WEIGHT), bytes_accessed=int(nbytes * WEIGHT), transcendentals=int(trans * WEIGHT)
    )


def norm_parts(v):
    c = v - jnp.mean(v, axis=1, keepdims=True)
    s = lax.rsqrt(jnp.mean(c * c, axis=1, keepdims=True) + EPS)
    return c * s, s


def norm_back(e, gain, xhat, s):
    f = e * gain
    return s * (
        f
        - jnp.mean(f, axis=1, keepdims=True)
        - xhat * jnp.mean(f * xhat, axis=1, keepdims=True)
    )


SHORT, SEQ, LAST_A, LAST_B, CORE = range(5)


def choose(flag, a, b):
    return jnp.where(flag == 0, a, b), jnp.where(flag == 0, b, a)


def weave_a(refs, at_ref):
    own, other, own_2, other_2 = [r[...].astype(f32) for r in refs]
    first, second = choose(at_ref[LAST_A], own, other)
    first_2, second_2 = choose(at_ref[LAST_A], own_2, other_2)
    quarters = choose(at_ref[CORE], first, first_2) + choose(at_ref[CORE], second, second_2)
    unit = own.shape[0] // 8
    return jnp.concatenate(
        [q[i * unit : (i + 1) * unit] for i in range(8) for q in quarters], axis=0
    ).astype(bf16)


def weave_b(refs, at_ref):
    own, other, own_2, other_2 = [r[...].astype(f32) for r in refs]
    halves = choose(at_ref[LAST_B], own, other)
    halves_2 = choose(at_ref[LAST_B], own_2, other_2)
    unit = own.shape[0] // 8
    out = []
    for half, half_2 in zip(halves, halves_2):
        even, odd = choose(at_ref[CORE], half, half_2)
        for i in range(8):
            out += [even[i * unit : (i + 1) * unit], odd[i * unit : (i + 1) * unit]]
    return jnp.concatenate(out, axis=0).astype(bf16)


def unweave(v, at_ref, unit):
    own, other = [], []
    for i in range(v.shape[0] // (2 * unit)):
        even, odd = v[2 * i * unit : (2 * i + 1) * unit], v[(2 * i + 1) * unit : (2 * i + 2) * unit]
        mine, theirs = choose(at_ref[CORE], even, odd)
        own.append(mine)
        other.append(theirs)
    return jnp.concatenate(own, axis=0), jnp.concatenate(other, axis=0)


def turn(v, at_ref):
    own, other = unweave(v.T.astype(f32), at_ref, v.shape[1] // 32)
    return own.astype(bf16), other.astype(bf16)


def call(kernel, name, grid, in_specs, out_specs, out_shape, scratch, estimate, at, args, aliases=None):
    return pl.pallas_call(
        kernel,
        grid_spec=pltpu.PrefetchScalarGridSpec(
            num_scalar_prefetch=1,
            grid=grid,
            in_specs=in_specs,
            out_specs=out_specs,
            scratch_shapes=scratch,
        ),
        out_shape=out_shape,
        compiler_params=params(),
        cost_estimate=estimate,
        input_output_aliases=aliases or {},
        name=name,
    )(at, *args)


def norm_one_kernel(at_ref, own_ref, other_ref, row_ref, x_ref, n_ref):
    ahead = pl.program_id(0) // (pl.num_programs(0) // 2) == at_ref[SEQ]
    x = jnp.where(ahead, own_ref[0].astype(f32), other_ref[...].astype(f32))
    x_ref[...] = x.astype(bf16)
    xhat, _ = norm_parts(x + row_ref[0:1, :])
    n_ref[...] = (xhat * row_ref[1:2, :] + row_ref[2:3, :]).astype(bf16)


def norm_one(at, both, other, rows, tb=256):
    half, d = other.shape
    t = 2 * half
    steps = half // tb
    tok = pl.BlockSpec((tb, d), lambda i, s: (i, 0))
    return call(
        norm_one_kernel, "norm_one", (2 * steps,),
        [
            pl.BlockSpec((1, tb, d), lambda i, s: (s[SEQ], i % steps, 0)),
            pl.BlockSpec((tb, d), lambda i, s: (i % steps, 0)),
            whole(*rows.shape),
        ],
        [tok, tok], [sds((t, d), bf16)] * 2, [],
        cost(10 * t * d, 4 * t * d), at, (both, other, rows),
    )


def weave_keys(refs, at_ref, w_ref):
    last = pl.program_id(0) == pl.num_programs(0) - 1

    @pl.when(jnp.logical_not(last))
    def _():
        w_ref[...] = weave_a(refs[:4], at_ref)

    @pl.when(last)
    def _():
        w_ref[...] = weave_b(refs[4:], at_ref)


def qkv_columns(w_a, w_b, width, groups):
    specs, args = [], []
    for pieces, column in (
        (w_a, lambda i, s: (0, i)),
        (w_a, lambda i, s: (0, groups + jnp.minimum(i, groups - 2))),
        (w_b, lambda i, s: (0, 0)),
        (w_b, lambda i, s: (0, 1 + i)),
    ):
        specs += [pl.BlockSpec((pieces[0].shape[0], width), column)] * 4
        args += pieces
    return specs, args


def attend_kernel(at_ref, n_ref, *refs, heads, qb):
    q_ref, k_ref, v_ref, o_ref, lse_ref, wk_ref = refs[16:]
    t = n_ref.shape[0]
    n = n_ref[...]
    weave_keys(refs[4:12], at_ref, wk_ref)
    q_ref[...] = nn(n, weave_a(refs[0:4], at_ref)).astype(bf16)
    k_ref[...] = nn(n, wk_ref[...]).astype(bf16)
    v_ref[...] = nn(n, weave_b(refs[12:16], at_ref)).astype(bf16)

    def run(parts):
        span = t // parts
        for h in range(heads):
            hs = slice(h * HD, (h + 1) * HD)
            for q0 in range(0, t, qb):
                k0 = (q0 // span) * span
                q = q_ref[q0 : q0 + qb, hs] * bf16(0.125)
                s = nt(k_ref[k0 : k0 + span, hs], q)
                top = jnp.max(s, axis=0, keepdims=True)
                p = jnp.exp2((s - top) * f32(LOG2E))
                total = jnp.sum(p, axis=0, keepdims=True)
                probs = (p * (1.0 / total)).astype(bf16)
                o_ref[q0 : q0 + qb, hs] = tn(probs, v_ref[k0 : k0 + span, hs]).astype(bf16)
                lse_ref[0, h : h + 1, q0 : q0 + qb] = top + jnp.log(total)

    short = at_ref[SHORT]

    @pl.when(short == 0)
    def _():
        run(1)

    @pl.when(short != 0)
    def _():
        run(2)


def attend(at, n, w_a, w_b, heads=4, qb=256):
    t, d = n.shape
    c = heads * HD
    groups = d // c
    specs, args = qkv_columns(w_a, w_b, c, groups)
    tok = pl.BlockSpec((t, c), lambda g, s: (0, g))
    return call(
        functools.partial(attend_kernel, heads=heads, qb=qb), "attend", (groups,),
        [whole(t, d)] + specs,
        [tok] * 4 + [pl.BlockSpec((1, heads, t), lambda g, s: (g, 0, 0))],
        [sds((t, d), bf16)] * 4 + [sds((groups, heads, t), f32)], [pltpu.VMEM((d, c), bf16)],
        cost(6 * t * d * d + 16 * t * t * d, 20 * t * d, t * t * d // HD),
        at, (n, *args),
    )


def attend_back_kernel(at_ref, q_ref, k_ref, v_ref, o_ref, do_ref, lse_ref, *refs, heads, qb):
    dq_ref, dk_ref, dv_ref = refs[-3:]
    t = q_ref.shape[0]

    def run(parts):
        span = t // parts
        k_turned = k_ref[...].T
        prod = (do_ref[...].astype(f32) * o_ref[...].astype(f32)).T
        for h in range(heads):
            hs = slice(h * HD, (h + 1) * HD)
            for b in range(parts):
                ks = slice(b * span, (b + 1) * span)
                k = k_ref[ks, hs]
                v = v_ref[ks, hs]
                dk = dv = None
                for q0 in range(b * span, (b + 1) * span, qb):
                    qs = slice(q0, q0 + qb)
                    q = q_ref[qs, hs] * bf16(0.125)
                    do = do_ref[qs, hs]
                    delta = jnp.sum(prod[hs, qs], axis=0, keepdims=True)
                    p = jnp.exp2((nt(k, q) - lse_ref[0, h : h + 1, qs]) * f32(LOG2E))
                    ds = (p * (nt(v, do) - delta)).astype(bf16)
                    dv_part = nn(p.astype(bf16), do)
                    dk_part = nn(ds, q)
                    dv = dv_part if dv is None else dv + dv_part
                    dk = dk_part if dk is None else dk + dk_part
                    dq_ref[qs, hs] = (nn(k_turned[hs, ks], ds) * f32(0.125)).T.astype(bf16)
                dk_ref[ks, hs] = dk.astype(bf16)
                dv_ref[ks, hs] = dv.astype(bf16)

    short = at_ref[SHORT]

    @pl.when(short == 0)
    def _():
        run(1)

    @pl.when(short != 0)
    def _():
        run(2)


def attend_back(at, q, k, v, o, do, lse, part, parts, before=(), heads=2, qb=256):
    t, d = q.shape
    c = heads * HD
    count = d // c // parts
    first = part * count
    tok = pl.BlockSpec((t, c), lambda g, s: (0, first + g))
    return call(
        functools.partial(attend_back_kernel, heads=heads, qb=qb), f"attend_back_{part}", (count,),
        [tok] * 5
        + [pl.BlockSpec((1, heads, t), lambda g, s: (first + g, 0, 0))]
        + [pl.BlockSpec(memory_space=pl.ANY)] * len(before),
        [tok] * 3, [sds((t, d), bf16)] * 3, [],
        cost(40 * t * t * d // parts, 16 * t * d // parts, t * t * d // HD // parts),
        at, (q, k, v, o, do, lse.reshape(-1, heads, t), *before),
        {7 + i: i for i in range(len(before))},
    )


def mix_kernel(
    at_ref, x_ref, o_ref, w0_ref, w1_ref, w2_ref, w3_ref, own_ref, other_ref, row_ref,
    mid_ref, n_ref, dy_ref, w_ref,
):
    @pl.when(pl.program_id(0) == 0)
    def _():
        w_ref[...] = weave_a((w0_ref, w1_ref, w2_ref, w3_ref), at_ref)

    ahead = pl.program_id(0) // (pl.num_programs(0) // 2) == at_ref[SEQ]
    dy_ref[...] = jnp.where(ahead, own_ref[0].astype(f32), other_ref[...].astype(f32)).astype(bf16)
    mid = x_ref[...].astype(f32) + row_ref[0:1, :] + nn(o_ref[...], w_ref[...])
    mid_ref[...] = mid
    xhat, _ = norm_parts(mid)
    n_ref[...] = (xhat * row_ref[3:4, :] + row_ref[4:5, :]).astype(bf16)


def mix(at, x, o, up_out, both, other, rows, tb=256):
    t, d = x.shape
    steps = other.shape[0] // tb
    tok = pl.BlockSpec((tb, d), lambda i, s: (i, 0))
    height, width = up_out[0].shape
    return call(
        mix_kernel, "mix", (t // tb,),
        [tok, tok]
        + [pl.BlockSpec((height, d), lambda i, s: (0, width // d - 1))] * 4
        + [
            pl.BlockSpec((1, tb, d), lambda i, s: (s[SEQ], i % steps, 0)),
            pl.BlockSpec((tb, d), lambda i, s: (i % steps, 0)),
            whole(*rows.shape),
        ],
        [tok] * 3, [sds((t, d), f32), sds((t, d), bf16), sds((t, d), bf16)],
        [pltpu.VMEM((d, d), bf16)], cost(2 * t * d * d, 12 * t * d), at, (x, o, *up_out, both, other, rows),
    )


def gelu_parts(u):
    e = jnp.exp(u * u * f32(-0.5))
    r = pl.reciprocal(1.0 + f32(0.3275911 * 0.7071067811865476) * jnp.abs(u))
    poly = f32(-1.453152027) + r * f32(1.061405429)
    poly = f32(1.421413741) + r * poly
    poly = f32(-0.284496736) + r * poly
    poly = r * (f32(0.254829592) + r * poly)
    tail = f32(0.5) * poly * e
    return jnp.where(u >= 0, 1.0 - tail, tail), e * f32(0.3989422804014327)


def ffn_kernel(at_ref, n_ref, dy_ref, mid_ref, *refs):
    ub_ref, row_ref, own_ref, send_ref, du_ref, keep_ref, give_ref, gub_ref, small_ref, acc, act = refs[8:]
    j = pl.program_id(0)

    @pl.when(j == 0)
    def _():
        acc[...] = mid_ref[...] + row_ref[5:6, :]

    wu = weave_a(refs[:4], at_ref)
    other = (j // (pl.num_programs(0) // 2)) != at_ref[LAST_B]
    even_odd = choose(
        at_ref[CORE],
        jnp.where(other, refs[5][...].astype(f32), refs[4][...].astype(f32)),
        jnp.where(other, refs[7][...].astype(f32), refs[6][...].astype(f32)),
    )
    short, d = refs[4].shape[0] // 4, dy_ref.shape[1]
    wd = jnp.concatenate(
        [
            v[i * short : (i + 1) * short, k * d : (k + 1) * d]
            for i in range(4)
            for v in even_odd
            for k in range(4)
        ],
        axis=0,
    ).astype(bf16)
    unit = 4 * short
    ub = ub_ref[...].astype(f32)
    t, fb = act.shape
    tb = t // 4
    gub = jnp.zeros((1, fb), f32)
    for i in range(4):
        sl = slice(i * tb, (i + 1) * tb)
        u = nn(n_ref[sl, :], wu) + ub
        da = nt(dy_ref[sl, :], wd)
        cdf, pdf = gelu_parts(u)
        active = (u * cdf).astype(bf16)
        act[sl, :] = active
        du = (da * (cdf + u * pdf)).astype(bf16)
        du_ref[sl, :] = du
        gub = gub + jnp.sum(du.astype(f32), axis=0, keepdims=True)
        acc[sl, :] += nn(active, wd)
    gub_ref[...] = gub
    own, theirs = unweave(tn(act[...], dy_ref[...]), at_ref, unit)
    keep_ref[...] = own.astype(bf16)
    give_ref[...] = theirs.astype(bf16)

    @pl.when(j == pl.num_programs(0) - 1)
    def _():
        half = t // 2
        own, theirs = choose(at_ref[SEQ], acc[:half, :], acc[half:, :])
        own_ref[...] = own.astype(bf16)
        send_ref[...] = theirs.astype(bf16)
        small_ref[...] = jnp.sum(dy_ref[...].astype(f32), axis=0, keepdims=True)


def ffn(at, n, dy, mid, up_out, down, up_bias, rows):
    t, d = n.shape
    ff = up_bias.shape[1]
    fb = ff // 4
    high, low = up_out[0].shape[0], down[0].shape[0]
    chunk = pl.BlockSpec((fb // 2, d), lambda j, s: (j, 0))
    return call(
        ffn_kernel, "ffn", (4,),
        [whole(t, d)] * 3
        + [pl.BlockSpec((high, fb), lambda j, s: (0, j))] * 4
        + [pl.BlockSpec((low // 2, 4 * d), lambda j, s: (j % 2, 0))] * 4
        + [pl.BlockSpec((1, fb), lambda j, s: (0, j)), whole(*rows.shape)],
        [whole(t // 2, d)] * 2
        + [pl.BlockSpec((t, fb), lambda j, s: (0, j)), chunk, chunk]
        + [pl.BlockSpec((1, fb), lambda j, s: (0, j)), whole(1, d)],
        [sds((t // 2, d), bf16)] * 2
        + [sds((t, ff), bf16)]
        + [sds((ff // 2, d), bf16)] * 2
        + [sds((1, ff), f32), sds((1, d), f32)],
        [pltpu.VMEM((t, d), f32), pltpu.VMEM((t, fb), bf16)],
        cost(8 * t * d * ff, 20 * t * d + 8 * d * ff, 2 * t * ff),
        at, (n, dy, mid, *up_out, *down, up_bias, rows),
    )


def unffn_kernel(at_ref, n_ref, dy_ref, mid_ref, du_ref, w0_ref, w1_ref, w2_ref, w3_ref, o_ref, row_ref, *refs):
    dmid_ref, do_ref, keep_ref, give_ref, small_ref, acc, turned, turned_2 = refs
    j = pl.program_id(0)
    last = pl.num_programs(0) - 1
    w = weave_a((w0_ref, w1_ref, w2_ref, w3_ref), at_ref)

    @pl.when(j == 0)
    def _():
        acc[...] = jnp.zeros_like(acc)
        turned[...], turned_2[...] = turn(n_ref[...], at_ref)

    @pl.when(j < last)
    def _():
        du = du_ref[...]
        keep_ref[...] = nn(turned[...], du).astype(bf16)
        give_ref[...] = nn(turned_2[...], du).astype(bf16)
        acc[...] += nt(du, w)

    @pl.when(j == last)
    def _():
        xhat, s = norm_parts(mid_ref[...])
        e = acc[...]
        small_ref[...] = jnp.concatenate(
            [jnp.sum(e * xhat, axis=0, keepdims=True), jnp.sum(e, axis=0, keepdims=True)], axis=0
        )
        dmid = dy_ref[...].astype(f32) + norm_back(e, row_ref[3:4, :], xhat, s)
        dmid_ref[...] = dmid
        db = dmid.astype(bf16)
        do_ref[...] = nt(db, w).astype(bf16)
        own, other = unweave(tn(o_ref[...], db), at_ref, w.shape[0] // 32)
        keep_ref[...] = own.astype(bf16)
        give_ref[...] = other.astype(bf16)


def unffn(at, n, dy, mid, du, up_out, o, rows):
    t, d = n.shape
    ff = du.shape[1]
    count = ff // d
    cols = pl.BlockSpec((d // 2, d), lambda j, s: (0, j))
    return call(
        unffn_kernel, "unffn", (count + 1,),
        [whole(t, d)] * 3
        + [pl.BlockSpec((t, d), lambda j, s: (0, jnp.minimum(j, count - 1)))]
        + [pl.BlockSpec((up_out[0].shape[0], d), lambda j, s: (0, j))] * 4
        + [whole(t, d), whole(*rows.shape)],
        [whole(t, d)] * 2 + [cols] * 2 + [whole(2, d)],
        [sds((t, d), f32), sds((t, d), bf16)] + [sds((d // 2, ff + d), bf16)] * 2 + [sds((2, d), f32)],
        [pltpu.VMEM((t, d), f32)] + [pltpu.VMEM((d // 2, t), bf16)] * 2,
        cost(4 * t * d * (ff + d), 20 * t * d + 8 * d * ff),
        at, (n, dy, mid, du, *up_out, o, rows),
    )


def grad_qkv_kernel(at_ref, n_ref, dq_ref, dk_ref, dv_ref, keep_ref, give_ref, turned, turned_2):
    @pl.when(pl.program_id(0) == 0)
    def _():
        turned[...], turned_2[...] = turn(n_ref[...], at_ref)

    for i, d_ref in enumerate((dq_ref, dk_ref, dv_ref)):
        keep_ref[i] = nn(turned[...], d_ref[...]).astype(bf16)
        give_ref[i] = nn(turned_2[...], d_ref[...]).astype(bf16)


def grad_qkv(at, n, dq, dk, dv, cb=256):
    t, d = n.shape
    tok = pl.BlockSpec((t, cb), lambda i, s: (0, i))
    out = pl.BlockSpec((3, d // 2, cb), lambda i, s: (0, 0, i))
    return call(
        grad_qkv_kernel, "grad_qkv", (d // cb,),
        [whole(t, d)] + [tok] * 3, [out] * 2, [sds((3, d // 2, d), bf16)] * 2,
        [pltpu.VMEM((d // 2, t), bf16)] * 2,
        cost(6 * t * d * d, 20 * t * d), at, (n, dq, dk, dv),
    )


def unqkv_kernel(at_ref, x_ref, row_ref, dmid_ref, *refs):
    dq_ref, dk_ref, dv_ref, own_ref, send_ref, small_ref, acc, wk_ref = refs[16:]
    i = pl.program_id(0)
    weave_keys(refs[4:12], at_ref, wk_ref)
    w = [weave_a(refs[0:4], at_ref), wk_ref[...], weave_b(refs[12:16], at_ref)]
    e = nt(
        jnp.concatenate([dq_ref[...], dk_ref[...], dv_ref[...]], axis=1),
        jnp.concatenate(w, axis=1),
    )

    @pl.when(i == 0)
    def _():
        acc[...] = e

    @pl.when(i > 0)
    def _():
        acc[...] += e

    @pl.when(i == pl.num_programs(0) - 1)
    def _():
        e = acc[...]
        xhat, s = norm_parts(x_ref[...].astype(f32) + row_ref[0:1, :])
        d_base = dmid_ref[...] + norm_back(e, row_ref[1:2, :], xhat, s)
        half = d_base.shape[0] // 2
        own, theirs = choose(at_ref[SEQ], d_base[:half], d_base[half:])
        own_ref[...] = own.astype(bf16)
        send_ref[...] = theirs.astype(bf16)
        small_ref[...] = jnp.concatenate(
            [
                jnp.sum(d_base, axis=0, keepdims=True),
                jnp.sum(e * xhat, axis=0, keepdims=True),
                jnp.sum(e, axis=0, keepdims=True),
                jnp.zeros((5, e.shape[1]), f32),
            ],
            axis=0,
        )


def unqkv(at, x, rows, dmid, w_a, w_b, dq, dk, dv, cb=256):
    t, d = x.shape
    count = d // cb
    specs, args = qkv_columns(w_a, w_b, cb, count)
    tok = pl.BlockSpec((t, cb), lambda i, s: (0, i))
    return call(
        unqkv_kernel, "unqkv", (count,),
        [whole(t, d), whole(*rows.shape), whole(t, d)] + specs + [tok] * 3,
        [whole(t // 2, d)] * 2 + [whole(8, d)],
        [sds((t // 2, d), bf16)] * 2 + [sds((8, d), f32)],
        [pltpu.VMEM((t, d), f32), pltpu.VMEM((d, cb), bf16)],
        cost(6 * t * d * d, 30 * t * d), at, (x, rows, dmid, *args, dq, dk, dv),
    )


class Grid:
    def __init__(self, seq, rows):
        self.seq, self.rows = seq, rows
        self.known = seq == 2 and rows == 16
        at = lax.axis_index("rows")
        self.x = lax.axis_index("seq")
        self.z, self.y, self.c = at // 4, (at // 2) % 2, at % 2

    def table(self, move):
        pairs = []
        for x in range(self.seq):
            for z in range(4):
                for y in range(2):
                    for c in range(2):
                        x2, z2, y2, c2 = move(x, z, y, c)
                        pairs.append((x * 16 + z * 4 + y * 2 + c, x2 * 16 + z2 * 4 + y2 * 2 + c2))
        return pairs

    def swap(self, v, axis):
        move = {
            "x": lambda x, z, y, c: (1 - x, z, y, c),
            "y": lambda x, z, y, c: (x, z, 1 - y, c),
            "c": lambda x, z, y, c: (x, z, y, 1 - c),
        }[axis]
        return lax.ppermute(v, BOTH, self.table(move))

    def cross(self, v, bit):
        return lax.ppermute(v, BOTH, self.table(lambda x, z, y, c: (x, z ^ bit, y, c)))

    def shift(self, v, by):
        return lax.ppermute(v, BOTH, self.table(lambda x, z, y, c: (x, (z + by) % 4, y, c)))


def tie(*values):
    return lax.optimization_barrier(values)


def after(v, *first):
    return lax.optimization_barrier((v, first))[0]


def spread(v, axis, count):
    return jnp.broadcast_to(jnp.expand_dims(v, axis), v.shape[:axis] + (count,) + v.shape[axis:])


def pair(own, other, at, axis):
    shape = own.shape[:axis] + (2,) + own.shape[axis:]
    here = lax.broadcasted_iota(jnp.int32, shape, axis) == at
    return jnp.where(here, spread(own, axis, 2), spread(other, axis, 2))


def arrange_z(g, v, shifts):
    out = spread(v, 0, 4)
    place = lax.broadcasted_iota(jnp.int32, out.shape, 0)
    for k, got in enumerate(shifts):
        out = jnp.where(place == (g.z - k - 1) % 4, spread(got, 0, 4), out)
    return out


def gather_z(g, v):
    return arrange_z(g, v, [g.shift(v, k) for k in range(1, 4)])


def flat(v):
    return v.reshape(-1, v.shape[-1])


def quarters(whole_array, kind):
    v = whole_array.reshape(2, 4, 2, 2, -1, whole_array.shape[1])
    pieces = []
    for core in range(2):
        for place in range(2):
            pieces.append(flat(v[:, :, place, core] if kind == "a" else v[place, :, :, core]))
    return pieces


def keep(v, at, axis):
    return lax.dynamic_index_in_dim(v, at, axis, keepdims=False)


def add(a, b):
    return (a.astype(f32) + b.astype(f32)).astype(bf16)


def split_plane(g, a, b):
    a = add(keep(a, g.x, -5), g.swap(keep(a, 1 - g.x, -5), "x"))
    b = add(keep(b, g.y, -3), g.swap(keep(b, 1 - g.y, -3), "y"))
    a, b = yield a, b
    got_a = g.swap(keep(a, 1 - g.y, -3), "y")
    got_b = g.swap(keep(b, 1 - g.x, -4), "x")
    got_a, got_b = yield got_a, got_b
    yield add(keep(a, g.y, -3), got_a), add(keep(b, g.x, -4), got_b)


def split_z(g, v):
    total = keep(v, g.z, -3).astype(f32)
    for k in range(1, 4):
        total = total + g.shift(keep(v, (g.z + k) % 4, -3), k).astype(f32)
    return total


def halve_z(g, v):
    v = v.reshape(*v.shape[:-3], 2, 2, *v.shape[-2:])
    high, low = g.z // 2, g.z % 2
    v = keep(v, low, -3).astype(f32) + g.cross(keep(v, 1 - low, -3), 1).astype(f32)
    got = yield g.cross(keep(v, 1 - high, -3).astype(bf16), 2)
    yield keep(v, high, -3) + got.astype(f32)


def scatter_plain(own, other):
    v = jnp.stack([own.reshape(16, -1, own.shape[1]), other.reshape(16, -1, own.shape[1])], axis=1)
    return lax.psum_scatter(flat(v).astype(f32), BOTH, scatter_dimension=0, tiled=True)


def swap_seq(v):
    return lax.ppermute(v, "seq", [(0, 1), (1, 0)])


def local(
    inputs, timesteps, boundary, step_table, w_qkv, w_out, w_up, w_down,
    norm1_gain, norm1_shift, norm2_gain, norm2_shift, up_bias, down_bias, cotangent,
):
    seq, row_blocks = lax.axis_size("seq"), lax.axis_size("rows")
    g = Grid(seq, row_blocks)
    devices = seq * row_blocks
    d = inputs.shape[2]
    shard = w_qkv.shape[0]
    ff = w_up.shape[1]
    steps = step_table.shape[0]
    wide = (ff // devices) // shard
    short = (g.x < boundary[0]).astype(jnp.int32)
    zero = jnp.zeros_like(short)
    at = jnp.stack([short, g.x] + ([g.y, g.x, g.c] if g.known else [zero] * 3))

    digits = jnp.concatenate([timesteps // 128, timesteps % 128]).astype(bf16)
    shorts = jnp.concatenate(
        [norm1_gain, norm1_shift, norm2_gain, norm2_shift, down_bias, up_bias, digits]
    )
    shorts = jnp.broadcast_to(shorts[None], (devices,) + shorts.shape)
    shorts = lax.all_to_all(shorts, BOTH, split_axis=0, concat_axis=0, tiled=True)
    x_other = swap_seq(keep(inputs, 1 - g.x, 0))
    unit = w_down.shape[0] // 4
    down_wide = w_down.reshape(4, unit, d).transpose(1, 0, 2).reshape(unit, -1)

    def look_up(shorts):
        digits = shorts[:, (5 + wide) * shard :].reshape(seq, row_blocks, 2, -1)[0].astype(jnp.int32)
        all_steps = digits[:, 0] * 128 + digits[:, 1]
        hot = all_steps.T.reshape(-1)[:, None] == jnp.arange(steps, dtype=jnp.int32)[None]
        found = nn(hot.astype(bf16), step_table).astype(bf16)
        found = lax.all_to_all(found, BOTH, split_axis=0, concat_axis=0, tiled=True)
        return all_steps.reshape(-1), found

    def norm_rows(shorts, found):
        rows = jnp.stack([found] + [shorts[:, i * shard : (i + 1) * shard] for i in range(5)])
        return jnp.pad(rows.reshape(6, d).astype(f32), ((0, 2), (0, 0)))

    if g.known:
        shifts = [g.shift(w_qkv, k) for k in range(1, 4)]
        rest = jnp.concatenate([w_up, w_out, down_wide], axis=1)
        rest_2 = g.cross(rest, 2)
        first = arrange_z(g, w_qkv, shifts)
        half = d + 2 * d // 3
        a, b = first[..., :half], first[..., half:]
        a = pair(a, g.swap(a, "x"), g.x, 0)
        b = pair(b, g.swap(b, "y"), g.y, 1)
        a, b, x_other, shorts, rest_2 = tie(a, b, x_other, shorts, rest_2)
        rest = pair(rest, rest_2, g.z // 2, 0)
        rest_1 = g.cross(rest, 1)
        all_steps, found = look_up(shorts)
        a_2, b_2 = g.swap(a, "y"), g.swap(b, "x")
        a_c, b_c = g.swap(a, "c"), g.swap(b, "c")
        w_a = [flat(v) for v in (a, a_2, a_c, g.swap(a_2, "c"))]
        w_b = [flat(v) for v in (b, b_2, b_c, g.swap(b_2, "c"))]
        rest, rest_1, found, a_2, b_2 = tie(rest, rest_1, found, a_2, b_2)
        rest = pair(rest, rest_1, g.z % 2, 1)
        rest = rest.reshape(4, *rest.shape[2:])
        rows = norm_rows(shorts, found)
        x, normed_one = norm_one(at, inputs, x_other, rows)
        a, b = rest[..., : ff + d], rest[..., ff + d :]
        a = pair(a, g.swap(a, "x"), g.x, 0)
        b = pair(b, g.swap(b, "y"), g.y, 1)
        a, b, normed_one = tie(a, b, normed_one)
        a_2, b_2 = g.swap(a, "y"), g.swap(b, "x")
        a_c, b_c = g.swap(a, "c"), g.swap(b, "c")
    else:
        half = d + 2 * d // 3
        w_a, w_b, up_out, down = [
            quarters(lax.all_gather(v, BOTH, axis=0, tiled=True), kind)
            for v, kind in (
                (w_qkv[:, :half], "a"),
                (w_qkv[:, half:], "b"),
                (jnp.concatenate([w_up, w_out], axis=1), "a"),
                (down_wide, "b"),
            )
        ]
        all_steps, found = look_up(shorts)
        rows = norm_rows(shorts, found)
        x, normed_one = norm_one(at, inputs, x_other, rows)

    up_row = shorts[:, 5 * shard : (5 + wide) * shard].reshape(1, ff)
    q, k, v, attended, lse = attend(at, normed_one, w_a, w_b)
    dy_other = swap_seq(keep(cotangent, 1 - g.x, 0))
    if g.known:
        a_2, b_2, attended, dy_other = tie(a_2, b_2, attended, dy_other)
        up_out = [flat(v) for v in (a, a_2, a_c, g.swap(a_2, "c"))]
        down = [flat(v) for v in (b, b_2, b_c, g.swap(b_2, "c"))]
    middle, normed_two, dy = mix(at, x, attended, up_out, cotangent, dy_other, rows)
    block_own, block_send, d_upper, keep_down, give_down, g_up_row, g_down_row = ffn(
        at, normed_two, dy, middle, up_out, down, up_row, rows
    )
    block_other = swap_seq(block_send)
    d_middle, d_attended, keep_up, give_up, small_two = unffn(
        at, normed_two, dy, middle, d_upper, up_out, attended, rows
    )
    six = (2, 4, 2)
    if g.known:
        d_middle, d_attended, keep_up, give_up, small_two, block_other = tie(
            d_middle, d_attended, keep_up, give_up, small_two, block_other
        )
        down = add(keep_down, g.swap(give_down, "c")).reshape(*six, -1, d)
        d_attended, down = tie(d_attended, down)
        down_plane = split_plane(g, down[..., : d // 2], down[..., d // 2 :])
    back = attend_back(at, q, k, v, attended, d_attended, lse, 0, 2)
    if g.known:
        cut = (ff + d) // 2
        up = add(keep_up, g.swap(give_up, "c")).reshape(*six, -1, ff + d)
        down_half = next(down_plane)
        d_attended, up, down_half, *back = tie(d_attended, up, down_half, *back)
        up_plane = split_plane(g, up[..., :cut], up[..., cut:])
        down_got = down_plane.send(down_half)
    dq, dk, dv = attend_back(at, q, k, v, attended, d_attended, lse, 1, 2, tuple(back))
    n = normed_one
    if g.known:
        up_half = next(up_plane)
        n, up_half, dq, down_got = tie(n, up_half, dq, down_got)
        up_got = up_plane.send(up_half)
        down = jnp.concatenate(down_plane.send(down_got), axis=-1)
        down_z = halve_z(g, down)
    keep_qkv, give_qkv = grad_qkv(at, n, dq, dk, dv)
    if g.known:
        qkv = add(keep_qkv, g.swap(give_qkv, "c")).reshape(3, *six, shard, d)
        up = jnp.concatenate(up_plane.send(up_got), axis=-1)
        d_middle, qkv, up = tie(d_middle, qkv, up)
        a = jnp.concatenate([qkv[0], qkv[1, ..., : d // 2]], axis=-1)
        b = jnp.concatenate([qkv[1, ..., d // 2 :], qkv[2]], axis=-1)
        plane = split_plane(g, a, b)
    d_own, d_send, small_one = unqkv(at, x, rows, d_middle, w_a, w_b, dq, dk, dv)
    if g.known:
        ready = next(plane)
        small_one, d_send, ready, down_got = tie(small_one, d_send, ready, next(down_z))
        sum_down = down_z.send(down_got)
        up_z = halve_z(g, up)
        got = plane.send(ready)
    d_other = swap_seq(d_send)

    small = jnp.concatenate([small_one[1:3], small_two, g_down_row, small_one[0:1]], axis=0)
    small = small.reshape(-1, devices, shard).transpose(1, 0, 2).reshape(devices, -1)
    small = jnp.concatenate([small, g_up_row.reshape(devices, -1)], axis=1)
    small = lax.all_to_all(small, BOTH, split_axis=0, concat_axis=0, tiled=True)
    row_sums = small[:, 5 * shard : 6 * shard].reshape(seq, row_blocks, shard).transpose(1, 0, 2)
    row_sums = row_sums.reshape(devices, shard)
    small = jnp.sum(small, axis=0)
    if g.known:
        sum_up = up_z.send(next(up_z))
        last = jnp.concatenate(plane.send(got), axis=-1)
        d_other, last = tie(d_other, split_z(g, last))
    else:
        sum_up, sum_down = scatter_plain(keep_up, give_up), scatter_plain(keep_down, give_down)
        last = [scatter_plain(keep_qkv[i], give_qkv[i]) for i in range(3)]
        last = jnp.concatenate(last, axis=1)
    block_out, grad_inputs = pair(block_own, block_other, g.x, 0), pair(d_own, d_other, g.x, 0)
    hot = (jnp.arange(steps, dtype=jnp.int32)[:, None] == all_steps[None]).astype(f32)
    g_table = lax.dot_general(
        hot, row_sums, (((1,), (0,)), ((), ())), precision=lax.Precision.HIGHEST,
        preferred_element_type=f32,
    )
    return (
        block_out,
        grad_inputs,
        g_table,
        last,
        sum_up[:, ff:],
        sum_up[:, :ff],
        sum_down,
        *[small[i * shard : (i + 1) * shard] for i in range(4)],
        small[6 * shard :],
        small[4 * shard : 5 * shard],
    )


def solution(mesh):
    tokens, weight, vector = P("rows", "seq", None), P(BOTH, None), P(BOTH)
    table = P(None, BOTH)
    in_specs = (
        (tokens, P("rows"), P("rows"), table) + (weight,) * 4 + (vector,) * 6 + (tokens,)
    )
    out_specs = (tokens, tokens, table) + (weight,) * 4 + (vector,) * 6
    return jax.shard_map(local, mesh=mesh, in_specs=in_specs, out_specs=out_specs, check_vma=False)
```

```python
import functools

import jax
import jax.numpy as jnp
from jax import lax
from jax.experimental import pallas as pl
from jax.experimental.pallas import tpu as pltpu
from jax.sharding import PartitionSpec as P

f32 = jnp.float32
bf16 = jnp.bfloat16
HD = 64
EPS = 1e-5
LOG2E = 1.4426950408889634
VMEM = 56 * 1024 * 1024
BOTH = ("seq", "rows")
WEIGHT = 0.02


def nn(a, b):
    return lax.dot_general(a, b, (((1,), (0,)), ((), ())), preferred_element_type=f32)


def nt(a, b):
    return lax.dot_general(a, b, (((1,), (1,)), ((), ())), preferred_element_type=f32)


def tn(a, b):
    return lax.dot_general(a, b, (((0,), (0,)), ((), ())), preferred_element_type=f32)


def sds(shape, dtype):
    return jax.ShapeDtypeStruct(shape, dtype)


def whole(*shape):
    return pl.BlockSpec(shape, lambda *_: (0,) * len(shape))


def params():
    return pltpu.CompilerParams(vmem_limit_bytes=VMEM, dimension_semantics=("arbitrary",))


def cost(flops, nbytes, trans=0):
    return pl.CostEstimate(
        flops=int(flops * WEIGHT), bytes_accessed=int(nbytes * WEIGHT), transcendentals=int(trans * WEIGHT)
    )


def norm_parts(v):
    c = v - jnp.mean(v, axis=1, keepdims=True)
    s = lax.rsqrt(jnp.mean(c * c, axis=1, keepdims=True) + EPS)
    return c * s, s


def norm_back(e, gain, xhat, s):
    f = e * gain
    return s * (
        f
        - jnp.mean(f, axis=1, keepdims=True)
        - xhat * jnp.mean(f * xhat, axis=1, keepdims=True)
    )


SHORT, SEQ, LAST_A, LAST_B, CORE = range(5)


def choose(flag, a, b):
    return jnp.where(flag == 0, a, b), jnp.where(flag == 0, b, a)


def weave_a(refs, at_ref):
    own, other, own_2, other_2 = [r[...].astype(f32) for r in refs]
    first, second = choose(at_ref[LAST_A], own, other)
    first_2, second_2 = choose(at_ref[LAST_A], own_2, other_2)
    quarters = choose(at_ref[CORE], first, first_2) + choose(at_ref[CORE], second, second_2)
    unit = own.shape[0] // 8
    return jnp.concatenate(
        [q[i * unit : (i + 1) * unit] for i in range(8) for q in quarters], axis=0
    ).astype(bf16)


def weave_b(refs, at_ref):
    own, other, own_2, other_2 = [r[...].astype(f32) for r in refs]
    halves = choose(at_ref[LAST_B], own, other)
    halves_2 = choose(at_ref[LAST_B], own_2, other_2)
    unit = own.shape[0] // 8
    out = []
    for half, half_2 in zip(halves, halves_2):
        even, odd = choose(at_ref[CORE], half, half_2)
        for i in range(8):
            out += [even[i * unit : (i + 1) * unit], odd[i * unit : (i + 1) * unit]]
    return jnp.concatenate(out, axis=0).astype(bf16)


def unweave(v, at_ref, unit):
    own, other = [], []
    for i in range(v.shape[0] // (2 * unit)):
        even, odd = v[2 * i * unit : (2 * i + 1) * unit], v[(2 * i + 1) * unit : (2 * i + 2) * unit]
        mine, theirs = choose(at_ref[CORE], even, odd)
        own.append(mine)
        other.append(theirs)
    return jnp.concatenate(own, axis=0), jnp.concatenate(other, axis=0)


def turn(v, at_ref):
    own, other = unweave(v.T.astype(f32), at_ref, v.shape[1] // 32)
    return own.astype(bf16), other.astype(bf16)


def call(kernel, name, grid, in_specs, out_specs, out_shape, scratch, estimate, at, args, aliases=None):
    return pl.pallas_call(
        kernel,
        grid_spec=pltpu.PrefetchScalarGridSpec(
            num_scalar_prefetch=1,
            grid=grid,
            in_specs=in_specs,
            out_specs=out_specs,
            scratch_shapes=scratch,
        ),
        out_shape=out_shape,
        compiler_params=params(),
        cost_estimate=estimate,
        input_output_aliases=aliases or {},
        name=name,
    )(at, *args)


def norm_one_kernel(at_ref, own_ref, other_ref, row_ref, x_ref, n_ref):
    ahead = pl.program_id(0) // (pl.num_programs(0) // 2) == at_ref[SEQ]
    x = jnp.where(ahead, own_ref[0].astype(f32), other_ref[...].astype(f32))
    x_ref[...] = x.astype(bf16)
    xhat, _ = norm_parts(x + row_ref[0:1, :])
    n_ref[...] = (xhat * row_ref[1:2, :] + row_ref[2:3, :]).astype(bf16)


def norm_one(at, both, other, rows, tb=256):
    half, d = other.shape
    t = 2 * half
    steps = half // tb
    tok = pl.BlockSpec((tb, d), lambda i, s: (i, 0))
    return call(
        norm_one_kernel, "norm_one", (2 * steps,),
        [
            pl.BlockSpec((1, tb, d), lambda i, s: (s[SEQ], i % steps, 0)),
            pl.BlockSpec((tb, d), lambda i, s: (i % steps, 0)),
            whole(*rows.shape),
        ],
        [tok, tok], [sds((t, d), bf16)] * 2, [],
        cost(10 * t * d, 4 * t * d), at, (both, other, rows),
    )


def weave_keys(refs, at_ref, w_ref):
    last = pl.program_id(0) == pl.num_programs(0) - 1

    @pl.when(jnp.logical_not(last))
    def _():
        w_ref[...] = weave_a(refs[:4], at_ref)

    @pl.when(last)
    def _():
        w_ref[...] = weave_b(refs[4:], at_ref)


def qkv_columns(w_a, w_b, width, groups):
    specs, args = [], []
    for pieces, column in (
        (w_a, lambda i, s: (0, i)),
        (w_a, lambda i, s: (0, groups + jnp.minimum(i, groups - 2))),
        (w_b, lambda i, s: (0, 0)),
        (w_b, lambda i, s: (0, 1 + i)),
    ):
        specs += [pl.BlockSpec((pieces[0].shape[0], width), column)] * 4
        args += pieces
    return specs, args


def attend_kernel(at_ref, n_ref, *refs, heads, qb):
    q_ref, k_ref, v_ref, o_ref, lse_ref, wk_ref = refs[16:]
    t = n_ref.shape[0]
    n = n_ref[...]
    weave_keys(refs[4:12], at_ref, wk_ref)
    q_ref[...] = nn(n, weave_a(refs[0:4], at_ref)).astype(bf16)
    k_ref[...] = nn(n, wk_ref[...]).astype(bf16)
    v_ref[...] = nn(n, weave_b(refs[12:16], at_ref)).astype(bf16)

    def run(parts):
        span = t // parts
        blocks = [(h, q0) for h in range(heads) for q0 in range(0, t, qb)]

        def scores(h, q0):
            hs = slice(h * HD, (h + 1) * HD)
            k0 = (q0 // span) * span
            return nt(k_ref[k0 : k0 + span, hs], q_ref[q0 : q0 + qb, hs] * bf16(0.125))

        ahead = scores(*blocks[0])
        for i, (h, q0) in enumerate(blocks):
            s = ahead
            if i + 1 < len(blocks):
                ahead = scores(*blocks[i + 1])
            hs = slice(h * HD, (h + 1) * HD)
            k0 = (q0 // span) * span
            top = jnp.max(s, axis=0, keepdims=True)
            p = jnp.exp2((s - top) * f32(LOG2E))
            total = jnp.sum(p, axis=0, keepdims=True)
            probs = (p * (1.0 / total)).astype(bf16)
            o_ref[q0 : q0 + qb, hs] = tn(probs, v_ref[k0 : k0 + span, hs]).astype(bf16)
            lse_ref[0, h : h + 1, q0 : q0 + qb] = top + jnp.log(total)

    short = at_ref[SHORT]

    @pl.when(short == 0)
    def _():
        run(1)

    @pl.when(short != 0)
    def _():
        run(2)


def attend(at, n, w_a, w_b, heads=4, qb=512):
    t, d = n.shape
    c = heads * HD
    groups = d // c
    specs, args = qkv_columns(w_a, w_b, c, groups)
    tok = pl.BlockSpec((t, c), lambda g, s: (0, g))
    return call(
        functools.partial(attend_kernel, heads=heads, qb=qb), "attend", (groups,),
        [whole(t, d)] + specs,
        [tok] * 4 + [pl.BlockSpec((1, heads, t), lambda g, s: (g, 0, 0))],
        [sds((t, d), bf16)] * 4 + [sds((groups, heads, t), f32)], [pltpu.VMEM((d, c), bf16)],
        cost(6 * t * d * d + 16 * t * t * d, 20 * t * d, t * t * d // HD),
        at, (n, *args),
    )


def attend_back_kernel(at_ref, q_ref, k_ref, v_ref, o_ref, do_ref, lse_ref, *refs, heads, qb):
    dq_ref, dk_ref, dv_ref = refs[-3:]
    t = q_ref.shape[0]

    def run(parts):
        span = t // parts
        k_turned = k_ref[...].T
        prod = (do_ref[...].astype(f32) * o_ref[...].astype(f32)).T
        for h in range(heads):
            hs = slice(h * HD, (h + 1) * HD)
            for b in range(parts):
                ks = slice(b * span, (b + 1) * span)
                k = k_ref[ks, hs]
                v = v_ref[ks, hs]
                dk = dv = None
                for q0 in range(b * span, (b + 1) * span, qb):
                    qs = slice(q0, q0 + qb)
                    q = q_ref[qs, hs] * bf16(0.125)
                    do = do_ref[qs, hs]
                    delta = jnp.sum(prod[hs, qs], axis=0, keepdims=True)
                    p = jnp.exp2((nt(k, q) - lse_ref[0, h : h + 1, qs]) * f32(LOG2E))
                    ds = (p * (nt(v, do) - delta)).astype(bf16)
                    dv_part = nn(p.astype(bf16), do)
                    dk_part = nn(ds, q)
                    dv = dv_part if dv is None else dv + dv_part
                    dk = dk_part if dk is None else dk + dk_part
                    dq_ref[qs, hs] = (nn(k_turned[hs, ks], ds) * f32(0.125)).T.astype(bf16)
                dk_ref[ks, hs] = dk.astype(bf16)
                dv_ref[ks, hs] = dv.astype(bf16)

    short = at_ref[SHORT]

    @pl.when(short == 0)
    def _():
        run(1)

    @pl.when(short != 0)
    def _():
        run(2)


def attend_back(at, q, k, v, o, do, lse, part, parts, before=(), heads=2, qb=256):
    t, d = q.shape
    c = heads * HD
    count = d // c // parts
    first = part * count
    tok = pl.BlockSpec((t, c), lambda g, s: (0, first + g))
    return call(
        functools.partial(attend_back_kernel, heads=heads, qb=qb), f"attend_back_{part}", (count,),
        [tok] * 5
        + [pl.BlockSpec((1, heads, t), lambda g, s: (first + g, 0, 0))]
        + [pl.BlockSpec(memory_space=pl.ANY)] * len(before),
        [tok] * 3, [sds((t, d), bf16)] * 3, [],
        cost(40 * t * t * d // parts, 16 * t * d // parts, t * t * d // HD // parts),
        at, (q, k, v, o, do, lse.reshape(-1, heads, t), *before),
        {7 + i: i for i in range(len(before))},
    )


def mix_kernel(
    at_ref, x_ref, o_ref, w0_ref, w1_ref, w2_ref, w3_ref, row_ref, mid_ref, n_ref, w_ref,
):
    @pl.when(pl.program_id(0) == 0)
    def _():
        w_ref[...] = weave_a((w0_ref, w1_ref, w2_ref, w3_ref), at_ref)

    mid = x_ref[...].astype(f32) + row_ref[0:1, :] + nn(o_ref[...], w_ref[...])
    mid_ref[...] = mid
    xhat, _ = norm_parts(mid)
    n_ref[...] = (xhat * row_ref[3:4, :] + row_ref[4:5, :]).astype(bf16)


def last_columns(pieces, width):
    return [
        pl.BlockSpec((p.shape[0], width), (lambda k: lambda i, s: (0, k))(p.shape[1] // width - 1))
        for p in pieces
    ]


def mix(at, x, o, out, rows, tb=256):
    t, d = x.shape
    tok = pl.BlockSpec((tb, d), lambda i, s: (i, 0))
    return call(
        mix_kernel, "mix", (t // tb,),
        [tok, tok] + last_columns(out, d) + [whole(*rows.shape)],
        [tok] * 2, [sds((t, d), f32), sds((t, d), bf16)],
        [pltpu.VMEM((d, d), bf16)], cost(2 * t * d * d, 12 * t * d), at, (x, o, *out, rows),
    )


def gelu_parts(u):
    e = jnp.exp(u * u * f32(-0.5))
    r = pl.reciprocal(1.0 + f32(0.3275911 * 0.7071067811865476) * jnp.abs(u))
    poly = f32(-1.453152027) + r * f32(1.061405429)
    poly = f32(1.421413741) + r * poly
    poly = f32(-0.284496736) + r * poly
    poly = r * (f32(0.254829592) + r * poly)
    tail = f32(0.5) * poly * e
    return jnp.where(u >= 0, 1.0 - tail, tail), e * f32(0.3989422804014327)


def ffn_kernel(at_ref, n_ref, here_ref, there_ref, there_2_ref, mid_ref, *refs):
    ub_ref, row_ref, own_ref, send_ref, du_ref, keep_ref, give_ref, gub_ref, small_ref, dy_ref, acc, act = refs[8:]
    j = pl.program_id(0)

    @pl.when(j == 0)
    def _():
        acc[...] = mid_ref[...] + row_ref[5:6, :]
        there = jnp.concatenate([there_ref[...].astype(f32), there_2_ref[...].astype(f32)], axis=0)
        halves = choose(at_ref[SEQ], here_ref[0].astype(f32), there)
        half = there.shape[0]
        dy_ref[:half, :] = halves[0].astype(bf16)
        dy_ref[half:, :] = halves[1].astype(bf16)

    wu = weave_a(refs[:4], at_ref)
    other = (j // (pl.num_programs(0) // 2)) != at_ref[LAST_B]
    even_odd = choose(
        at_ref[CORE],
        jnp.where(other, refs[5][...].astype(f32), refs[4][...].astype(f32)),
        jnp.where(other, refs[7][...].astype(f32), refs[6][...].astype(f32)),
    )
    short, d = refs[4].shape[0] // 4, dy_ref.shape[1]
    wd = jnp.concatenate(
        [
            v[i * short : (i + 1) * short, k * d : (k + 1) * d]
            for i in range(4)
            for v in even_odd
            for k in range(4)
        ],
        axis=0,
    ).astype(bf16)
    unit = 4 * short
    ub = ub_ref[...].astype(f32)
    t, fb = act.shape
    tb = t // 4
    gub = jnp.zeros((1, fb), f32)
    for i in range(4):
        sl = slice(i * tb, (i + 1) * tb)
        u = nn(n_ref[sl, :], wu) + ub
        da = nt(dy_ref[sl, :], wd)
        cdf, pdf = gelu_parts(u)
        active = (u * cdf).astype(bf16)
        act[sl, :] = active
        du = (da * (cdf + u * pdf)).astype(bf16)
        du_ref[sl, :] = du
        gub = gub + jnp.sum(du.astype(f32), axis=0, keepdims=True)
        acc[sl, :] += nn(active, wd)
    gub_ref[...] = gub
    own, theirs = unweave(tn(act[...], dy_ref[...]), at_ref, unit)
    keep_ref[...] = own.astype(bf16)
    give_ref[...] = theirs.astype(bf16)

    @pl.when(j == pl.num_programs(0) - 1)
    def _():
        half = t // 2
        own, theirs = choose(at_ref[SEQ], acc[:half, :], acc[half:, :])
        own_ref[...] = own.astype(bf16)
        send_ref[...] = theirs.astype(bf16)
        small_ref[...] = jnp.sum(dy_ref[...].astype(f32), axis=0, keepdims=True)


def ffn(at, n, both, other, mid, up_out, down, up_bias, rows):
    t, d = n.shape
    ff = up_bias.shape[1]
    fb = ff // 4
    high, low = up_out[0].shape[0], down[0].shape[0]
    chunk = pl.BlockSpec((fb // 2, d), lambda j, s: (j, 0))
    return call(
        ffn_kernel, "ffn", (4,),
        [whole(t, d), pl.BlockSpec((1, t // 2, d), lambda j, s: (s[SEQ], 0, 0)), whole(t // 4, d), whole(t // 4, d)]
        + [whole(t, d)]
        + [pl.BlockSpec((high, fb), lambda j, s: (0, j))] * 4
        + [pl.BlockSpec((low // 2, 4 * d), lambda j, s: (j % 2, 0))] * 4
        + [pl.BlockSpec((1, fb), lambda j, s: (0, j)), whole(*rows.shape)],
        [whole(t // 2, d)] * 2
        + [pl.BlockSpec((t, fb), lambda j, s: (0, j)), chunk, chunk]
        + [pl.BlockSpec((1, fb), lambda j, s: (0, j)), whole(1, d), whole(t, d)],
        [sds((t // 2, d), bf16)] * 2
        + [sds((t, ff), bf16)]
        + [sds((ff // 2, d), bf16)] * 2
        + [sds((1, ff), f32), sds((1, d), f32), sds((t, d), bf16)],
        [pltpu.VMEM((t, d), f32), pltpu.VMEM((t, fb), bf16)],
        cost(8 * t * d * ff, 20 * t * d + 8 * d * ff, 2 * t * ff),
        at, (n, both, *other, mid, *up_out, *down, up_bias, rows),
    )


def unffn_kernel(at_ref, n_ref, dy_ref, mid_ref, du_ref, o_ref, row_ref, *refs):
    dmid_ref, do_ref, keep_ref, give_ref, small_ref, acc, turned, turned_2 = refs[8:]
    j = pl.program_id(0)
    last = pl.num_programs(0) - 1

    @pl.when(j == 0)
    def _():
        acc[...] = jnp.zeros_like(acc)
        turned[...], turned_2[...] = turn(n_ref[...], at_ref)

    @pl.when(j < last)
    def _():
        du = du_ref[...]
        w = weave_a(refs[:4], at_ref)
        keep_ref[...] = nn(turned[...], du).astype(bf16)
        give_ref[...] = nn(turned_2[...], du).astype(bf16)
        acc[...] += nt(du, w)

    @pl.when(j == last)
    def _():
        xhat, s = norm_parts(mid_ref[...])
        e = acc[...]
        small_ref[...] = jnp.concatenate(
            [jnp.sum(e * xhat, axis=0, keepdims=True), jnp.sum(e, axis=0, keepdims=True)], axis=0
        )
        dmid = dy_ref[...].astype(f32) + norm_back(e, row_ref[3:4, :], xhat, s)
        dmid_ref[...] = dmid
        db = dmid.astype(bf16)
        do_ref[...] = nt(db, weave_a(refs[4:8], at_ref)).astype(bf16)
        own, other = unweave(tn(o_ref[...], db), at_ref, db.shape[1] // 32)
        keep_ref[...] = own.astype(bf16)
        give_ref[...] = other.astype(bf16)


def unffn(at, n, dy, mid, du, up, out, o, rows):
    t, d = n.shape
    ff = du.shape[1]
    count = ff // d
    cols = pl.BlockSpec((d // 2, d), lambda j, s: (0, j))
    return call(
        unffn_kernel, "unffn", (count + 1,),
        [whole(t, d)] * 3
        + [pl.BlockSpec((t, d), lambda j, s: (0, jnp.minimum(j, count - 1)))]
        + [whole(t, d), whole(*rows.shape)]
        + [pl.BlockSpec((p.shape[0], d), lambda j, s: (0, jnp.minimum(j, count - 1))) for p in up]
        + last_columns(out, d),
        [whole(t, d)] * 2 + [cols] * 2 + [whole(2, d)],
        [sds((t, d), f32), sds((t, d), bf16)] + [sds((d // 2, ff + d), bf16)] * 2 + [sds((2, d), f32)],
        [pltpu.VMEM((t, d), f32)] + [pltpu.VMEM((d // 2, t), bf16)] * 2,
        cost(4 * t * d * (ff + d), 20 * t * d + 8 * d * ff),
        at, (n, dy, mid, du, o, rows, *up, *out),
    )


def grad_qkv_kernel(at_ref, n_ref, dq_ref, dk_ref, dv_ref, keep_ref, give_ref, turned, turned_2):
    @pl.when(pl.program_id(0) == 0)
    def _():
        turned[...], turned_2[...] = turn(n_ref[...], at_ref)

    for i, d_ref in enumerate((dq_ref, dk_ref, dv_ref)):
        keep_ref[i] = nn(turned[...], d_ref[...]).astype(bf16)
        give_ref[i] = nn(turned_2[...], d_ref[...]).astype(bf16)


def grad_qkv(at, n, dq, dk, dv, cb=256):
    t, d = n.shape
    tok = pl.BlockSpec((t, cb), lambda i, s: (0, i))
    out = pl.BlockSpec((3, d // 2, cb), lambda i, s: (0, 0, i))
    return call(
        grad_qkv_kernel, "grad_qkv", (d // cb,),
        [whole(t, d)] + [tok] * 3, [out] * 2, [sds((3, d // 2, d), bf16)] * 2,
        [pltpu.VMEM((d // 2, t), bf16)] * 2,
        cost(6 * t * d * d, 20 * t * d), at, (n, dq, dk, dv),
    )


def unqkv_kernel(at_ref, x_ref, row_ref, dmid_ref, *refs):
    dq_ref, dk_ref, dv_ref, own_ref, send_ref, small_ref, acc, wk_ref = refs[16:]
    i = pl.program_id(0)
    weave_keys(refs[4:12], at_ref, wk_ref)
    w = [weave_a(refs[0:4], at_ref), wk_ref[...], weave_b(refs[12:16], at_ref)]
    e = nt(
        jnp.concatenate([dq_ref[...], dk_ref[...], dv_ref[...]], axis=1),
        jnp.concatenate(w, axis=1),
    )

    @pl.when(i == 0)
    def _():
        acc[...] = e

    @pl.when(i > 0)
    def _():
        acc[...] += e

    @pl.when(i == pl.num_programs(0) - 1)
    def _():
        e = acc[...]
        xhat, s = norm_parts(x_ref[...].astype(f32) + row_ref[0:1, :])
        d_base = dmid_ref[...] + norm_back(e, row_ref[1:2, :], xhat, s)
        half = d_base.shape[0] // 2
        own, theirs = choose(at_ref[SEQ], d_base[:half], d_base[half:])
        own_ref[...] = own.astype(bf16)
        send_ref[...] = theirs.astype(bf16)
        small_ref[...] = jnp.concatenate(
            [
                jnp.sum(d_base, axis=0, keepdims=True),
                jnp.sum(e * xhat, axis=0, keepdims=True),
                jnp.sum(e, axis=0, keepdims=True),
                jnp.zeros((5, e.shape[1]), f32),
            ],
            axis=0,
        )


def unqkv(at, x, rows, dmid, w_a, w_b, dq, dk, dv, cb=256):
    t, d = x.shape
    count = d // cb
    specs, args = qkv_columns(w_a, w_b, cb, count)
    tok = pl.BlockSpec((t, cb), lambda i, s: (0, i))
    return call(
        unqkv_kernel, "unqkv", (count,),
        [whole(t, d), whole(*rows.shape), whole(t, d)] + specs + [tok] * 3,
        [whole(t // 2, d)] * 2 + [whole(8, d)],
        [sds((t // 2, d), bf16)] * 2 + [sds((8, d), f32)],
        [pltpu.VMEM((t, d), f32), pltpu.VMEM((d, cb), bf16)],
        cost(6 * t * d * d, 30 * t * d), at, (x, rows, dmid, *args, dq, dk, dv),
    )


class Grid:
    def __init__(self, seq, rows):
        self.seq, self.rows = seq, rows
        self.known = seq == 2 and rows == 16
        at = lax.axis_index("rows")
        self.x = lax.axis_index("seq")
        self.z, self.y, self.c = at // 4, (at // 2) % 2, at % 2

    def table(self, move):
        pairs = []
        for x in range(self.seq):
            for z in range(4):
                for y in range(2):
                    for c in range(2):
                        x2, z2, y2, c2 = move(x, z, y, c)
                        pairs.append((x * 16 + z * 4 + y * 2 + c, x2 * 16 + z2 * 4 + y2 * 2 + c2))
        return pairs

    def swap(self, v, axis):
        move = {
            "x": lambda x, z, y, c: (1 - x, z, y, c),
            "y": lambda x, z, y, c: (x, z, 1 - y, c),
            "c": lambda x, z, y, c: (x, z, y, 1 - c),
        }[axis]
        return lax.ppermute(v, BOTH, self.table(move))

    def cross(self, v, bit):
        return lax.ppermute(v, BOTH, self.table(lambda x, z, y, c: (x, z ^ bit, y, c)))

    def shift(self, v, by):
        return lax.ppermute(v, BOTH, self.table(lambda x, z, y, c: (x, (z + by) % 4, y, c)))


def tie(*values):
    return lax.optimization_barrier(values)


def after(v, *first):
    return lax.optimization_barrier((v, first))[0]


def spread(v, axis, count):
    return jnp.broadcast_to(jnp.expand_dims(v, axis), v.shape[:axis] + (count,) + v.shape[axis:])


def pair(own, other, at, axis):
    shape = own.shape[:axis] + (2,) + own.shape[axis:]
    here = lax.broadcasted_iota(jnp.int32, shape, axis) == at
    return jnp.where(here, spread(own, axis, 2), spread(other, axis, 2))


def arrange_z(g, v, shifts):
    out = spread(v, 0, 4)
    place = lax.broadcasted_iota(jnp.int32, out.shape, 0)
    for k, got in enumerate(shifts):
        out = jnp.where(place == (g.z - k - 1) % 4, spread(got, 0, 4), out)
    return out


def gather_z(g, v):
    return arrange_z(g, v, [g.shift(v, k) for k in range(1, 4)])


def flat(v):
    return v.reshape(-1, v.shape[-1])


def quarters(whole_array, kind):
    v = whole_array.reshape(2, 4, 2, 2, -1, whole_array.shape[1])
    pieces = []
    for core in range(2):
        for place in range(2):
            pieces.append(flat(v[:, :, place, core] if kind == "a" else v[place, :, :, core]))
    return pieces


def keep(v, at, axis):
    return lax.dynamic_index_in_dim(v, at, axis, keepdims=False)


def add(a, b):
    return (a.astype(f32) + b.astype(f32)).astype(bf16)


def split_plane(g, a, b):
    a = add(keep(a, g.x, -5), g.swap(keep(a, 1 - g.x, -5), "x"))
    b = add(keep(b, g.y, -3), g.swap(keep(b, 1 - g.y, -3), "y"))
    a, b = yield a, b
    got_a = g.swap(keep(a, 1 - g.y, -3), "y")
    got_b = g.swap(keep(b, 1 - g.x, -4), "x")
    got_a, got_b = yield got_a, got_b
    yield add(keep(a, g.y, -3), got_a), add(keep(b, g.x, -4), got_b)


def split_z(g, v):
    total = keep(v, g.z, -3).astype(f32)
    for k in range(1, 4):
        total = total + g.shift(keep(v, (g.z + k) % 4, -3), k).astype(f32)
    return total


def halve_z(g, v):
    v = v.reshape(*v.shape[:-3], 2, 2, *v.shape[-2:])
    high, low = g.z // 2, g.z % 2
    v = keep(v, low, -3).astype(f32) + g.cross(keep(v, 1 - low, -3), 1).astype(f32)
    got = yield g.cross(keep(v, 1 - high, -3).astype(bf16), 2)
    yield keep(v, high, -3) + got.astype(f32)


def scatter_plain(own, other):
    v = jnp.stack([own.reshape(16, -1, own.shape[1]), other.reshape(16, -1, own.shape[1])], axis=1)
    return lax.psum_scatter(flat(v).astype(f32), BOTH, scatter_dimension=0, tiled=True)


def swap_seq(v):
    return lax.ppermute(v, "seq", [(0, 1), (1, 0)])


def local(
    inputs, timesteps, boundary, step_table, w_qkv, w_out, w_up, w_down,
    norm1_gain, norm1_shift, norm2_gain, norm2_shift, up_bias, down_bias, cotangent,
):
    seq, row_blocks = lax.axis_size("seq"), lax.axis_size("rows")
    g = Grid(seq, row_blocks)
    devices = seq * row_blocks
    d = inputs.shape[2]
    shard = w_qkv.shape[0]
    ff = w_up.shape[1]
    steps = step_table.shape[0]
    wide = (ff // devices) // shard
    short = (g.x < boundary[0]).astype(jnp.int32)
    zero = jnp.zeros_like(short)
    at = jnp.stack([short, g.x] + ([g.y, g.x, g.c] if g.known else [zero] * 3))

    digits = jnp.concatenate([timesteps // 128, timesteps % 128]).astype(bf16)
    shorts = jnp.concatenate(
        [norm1_gain, norm1_shift, norm2_gain, norm2_shift, down_bias, up_bias, digits]
    )
    shorts = jnp.broadcast_to(shorts[None], (devices,) + shorts.shape)
    shorts = lax.all_to_all(shorts, BOTH, split_axis=0, concat_axis=0, tiled=True)
    x_other = swap_seq(keep(inputs, 1 - g.x, 0))
    unit = w_down.shape[0] // 4
    down_wide = w_down.reshape(4, unit, d).transpose(1, 0, 2).reshape(unit, -1)

    def look_up(shorts):
        digits = shorts[:, (5 + wide) * shard :].reshape(seq, row_blocks, 2, -1)[0].astype(jnp.int32)
        all_steps = digits[:, 0] * 128 + digits[:, 1]
        hot = all_steps.T.reshape(-1)[:, None] == jnp.arange(steps, dtype=jnp.int32)[None]
        found = nn(hot.astype(bf16), step_table).astype(bf16)
        found = lax.all_to_all(found, BOTH, split_axis=0, concat_axis=0, tiled=True)
        return all_steps.reshape(-1), found

    def norm_rows(shorts, found):
        rows = jnp.stack([found] + [shorts[:, i * shard : (i + 1) * shard] for i in range(5)])
        return jnp.pad(rows.reshape(6, d).astype(f32), ((0, 2), (0, 0)))

    if g.known:
        shifts = [g.shift(w_qkv, k) for k in range(1, 4)]
        rest = jnp.concatenate([w_up, w_out, down_wide], axis=1)
        rest_2 = g.cross(rest, 2)
        first = arrange_z(g, w_qkv, shifts)
        half = d + 2 * d // 3
        a, b = first[..., :half], first[..., half:]
        a = pair(a, g.swap(a, "x"), g.x, 0)
        b = pair(b, g.swap(b, "y"), g.y, 1)
        a, b, x_other, shorts, rest_2 = tie(a, b, x_other, shorts, rest_2)
        rest = pair(rest, rest_2, g.z // 2, 0)
        rest_1 = g.cross(rest, 1)
        all_steps, found = look_up(shorts)
        a_2, b_2 = g.swap(a, "y"), g.swap(b, "x")
        a_c, b_c = g.swap(a, "c"), g.swap(b, "c")
        w_a = [flat(v) for v in (a, a_2, a_c, g.swap(a_2, "c"))]
        w_b = [flat(v) for v in (b, b_2, b_c, g.swap(b_2, "c"))]
        rest, rest_1, found, a_2, b_2 = tie(rest, rest_1, found, a_2, b_2)
        rest = pair(rest, rest_1, g.z % 2, 1)
        rest = rest.reshape(4, *rest.shape[2:])
        rows = norm_rows(shorts, found)
        x, normed_one = norm_one(at, inputs, x_other, rows)
        a, b = rest[..., : ff + d], rest[..., ff + d :]
        a = pair(a, g.swap(a, "x"), g.x, 0)
        b = pair(b, g.swap(b, "y"), g.y, 1)
        a, b, normed_one = tie(a, b, normed_one)
        a_2, b_2 = g.swap(a, "y"), g.swap(b, "x")
        a_c, b_c = g.swap(a, "c"), g.swap(b, "c")
    else:
        half = d + 2 * d // 3
        w_a, w_b, up_out, down = [
            quarters(lax.all_gather(v, BOTH, axis=0, tiled=True), kind)
            for v, kind in (
                (w_qkv[:, :half], "a"),
                (w_qkv[:, half:], "b"),
                (jnp.concatenate([w_up, w_out], axis=1), "a"),
                (down_wide, "b"),
            )
        ]
        all_steps, found = look_up(shorts)
        rows = norm_rows(shorts, found)
        x, normed_one = norm_one(at, inputs, x_other, rows)

    up_row = shorts[:, 5 * shard : (5 + wide) * shard].reshape(1, ff)
    q, k, v, attended, lse = attend(at, normed_one, w_a, w_b)
    dy_send = keep(cotangent, 1 - g.x, 0)
    dy_other = [swap_seq(v) for v in jnp.split(dy_send, 2)]
    if g.known:
        q, k, v, lse, attended, dy_other[0] = tie(q, k, v, lse, attended, dy_other[0])
        a_2, b_2, attended = tie(a_2, b_2, attended)
        out = [flat(v) for v in (a, a_2, a_c, g.swap(a_2[..., ff:], "c"))]
        up_out = [flat(v) for v in (a, a_2, a_c, g.swap(a_2, "c"))]
        down = [flat(v) for v in (b, b_2, b_c, g.swap(b_2, "c"))]
    else:
        out = up_out
    middle, normed_two = mix(at, x, attended, out, rows)
    block_own, block_send, d_upper, keep_down, give_down, g_up_row, g_down_row, dy = ffn(
        at, normed_two, cotangent, dy_other, middle, up_out, down, up_row, rows
    )
    block_other = swap_seq(block_send)
    d_middle, d_attended, keep_up, give_up, small_two = unffn(
        at, normed_two, dy, middle, d_upper, up_out, out, attended, rows
    )
    six = (2, 4, 2)
    if g.known:
        d_middle, d_attended, keep_up, give_up, small_two, block_other = tie(
            d_middle, d_attended, keep_up, give_up, small_two, block_other
        )
        down = add(keep_down, g.swap(give_down, "c")).reshape(*six, -1, d)
        block_out = pair(block_own, block_other, g.x, 0)
        d_attended, down, block_out = tie(d_attended, down, block_out)
        down_plane = split_plane(g, down[..., : d // 2], down[..., d // 2 :])
    back = attend_back(at, q, k, v, attended, d_attended, lse, 0, 2)
    if g.known:
        cut = (ff + d) // 2
        up = add(keep_up, g.swap(give_up, "c")).reshape(*six, -1, ff + d)
        down_half = next(down_plane)
        d_attended, up, down_half, *back = tie(d_attended, up, down_half, *back)
        up_plane = split_plane(g, up[..., :cut], up[..., cut:])
        down_got = down_plane.send(down_half)
    dq, dk, dv = attend_back(at, q, k, v, attended, d_attended, lse, 1, 2, tuple(back))
    n = normed_one
    if g.known:
        up_half = next(up_plane)
        n, up_half, dq, down_got = tie(n, up_half, dq, down_got)
        up_got = up_plane.send(up_half)
        down = jnp.concatenate(down_plane.send(down_got), axis=-1)
        down_z = halve_z(g, down)
    keep_qkv, give_qkv = grad_qkv(at, n, dq, dk, dv)
    if g.known:
        keep_qkv, up_got = tie(keep_qkv, up_got)
        qkv = add(keep_qkv, g.swap(give_qkv, "c")).reshape(3, *six, shard, d)
        up = jnp.concatenate(up_plane.send(up_got), axis=-1)
        d_middle, qkv, up = tie(d_middle, qkv, up)
        a = jnp.concatenate([qkv[0], qkv[1, ..., : d // 2]], axis=-1)
        b = jnp.concatenate([qkv[1, ..., d // 2 :], qkv[2]], axis=-1)
        plane = split_plane(g, a, b)
    d_own, d_send, small_one = unqkv(at, x, rows, d_middle, w_a, w_b, dq, dk, dv)
    if g.known:
        ready = next(plane)
        small_one, d_send, ready, down_got = tie(small_one, d_send, ready, next(down_z))
        sum_down = down_z.send(down_got)
        up_z = halve_z(g, up)
        got = plane.send(ready)
    d_other = swap_seq(d_send)

    small = jnp.concatenate([small_one[1:3], small_two, g_down_row, small_one[0:1]], axis=0)
    small = small.reshape(-1, devices, shard).transpose(1, 0, 2).reshape(devices, -1)
    small = jnp.concatenate([small, g_up_row.reshape(devices, -1)], axis=1)
    small = lax.all_to_all(small, BOTH, split_axis=0, concat_axis=0, tiled=True)
    row_sums = small[:, 5 * shard : 6 * shard].reshape(seq, row_blocks, shard).transpose(1, 0, 2)
    row_sums = row_sums.reshape(devices, shard)
    small = jnp.sum(small, axis=0)
    if g.known:
        sum_up = up_z.send(next(up_z))
        last = jnp.concatenate(plane.send(got), axis=-1)
        d_other, last = tie(d_other, split_z(g, last))
    else:
        sum_up, sum_down = scatter_plain(keep_up, give_up), scatter_plain(keep_down, give_down)
        last = [scatter_plain(keep_qkv[i], give_qkv[i]) for i in range(3)]
        last = jnp.concatenate(last, axis=1)
        block_out = pair(block_own, block_other, g.x, 0)
    grad_inputs = pair(d_own, d_other, g.x, 0)
    hot = (jnp.arange(steps, dtype=jnp.int32)[:, None] == all_steps[None]).astype(f32)
    g_table = lax.dot_general(
        hot, row_sums, (((1,), (0,)), ((), ())), precision=lax.Precision.HIGHEST,
        preferred_element_type=f32,
    )
    return (
        block_out,
        grad_inputs,
        g_table,
        last,
        sum_up[:, ff:],
        sum_up[:, :ff],
        sum_down,
        *[small[i * shard : (i + 1) * shard] for i in range(4)],
        small[6 * shard :],
        small[4 * shard : 5 * shard],
    )


def solution(mesh):
    tokens, weight, vector = P("rows", "seq", None), P(BOTH, None), P(BOTH)
    table = P(None, BOTH)
    in_specs = (
        (tokens, P("rows"), P("rows"), table) + (weight,) * 4 + (vector,) * 6 + (tokens,)
    )
    out_specs = (tokens, tokens, table) + (weight,) * 4 + (vector,) * 6
    return jax.shard_map(local, mesh=mesh, in_specs=in_specs, out_specs=out_specs, check_vma=False)
```

```python
import functools

import jax
import jax.numpy as jnp
from jax import lax
from jax.experimental import pallas as pl
from jax.experimental.pallas import tpu as pltpu
from jax.sharding import PartitionSpec as P

f32 = jnp.float32
bf16 = jnp.bfloat16
HD = 64
EPS = 1e-5
LOG2E = 1.4426950408889634
VMEM = 56 * 1024 * 1024
BOTH = ("seq", "rows")
WEIGHT = 0.02


def nn(a, b):
    return lax.dot_general(a, b, (((1,), (0,)), ((), ())), preferred_element_type=f32)


def nt(a, b):
    return lax.dot_general(a, b, (((1,), (1,)), ((), ())), preferred_element_type=f32)


def tn(a, b):
    return lax.dot_general(a, b, (((0,), (0,)), ((), ())), preferred_element_type=f32)


def sds(shape, dtype):
    return jax.ShapeDtypeStruct(shape, dtype)


def whole(*shape):
    return pl.BlockSpec(shape, lambda *_: (0,) * len(shape))


def params():
    return pltpu.CompilerParams(vmem_limit_bytes=VMEM, dimension_semantics=("arbitrary",))


def cost(flops, nbytes, trans=0):
    return pl.CostEstimate(
        flops=int(flops * WEIGHT), bytes_accessed=int(nbytes * WEIGHT), transcendentals=int(trans * WEIGHT)
    )


def norm_parts(v):
    c = v - jnp.mean(v, axis=1, keepdims=True)
    s = lax.rsqrt(jnp.mean(c * c, axis=1, keepdims=True) + EPS)
    return c * s, s


def norm_back(e, gain, xhat, s):
    f = e * gain
    return s * (
        f
        - jnp.mean(f, axis=1, keepdims=True)
        - xhat * jnp.mean(f * xhat, axis=1, keepdims=True)
    )


SHORT, SEQ, LAST_A, LAST_B, CORE = range(5)


def choose(flag, a, b):
    return jnp.where(flag == 0, a, b), jnp.where(flag == 0, b, a)


def weave_a(refs, at_ref):
    own, other, own_2, other_2 = [r[...].astype(f32) for r in refs]
    first, second = choose(at_ref[LAST_A], own, other)
    first_2, second_2 = choose(at_ref[LAST_A], own_2, other_2)
    quarters = choose(at_ref[CORE], first, first_2) + choose(at_ref[CORE], second, second_2)
    unit = own.shape[0] // 8
    return jnp.concatenate(
        [q[i * unit : (i + 1) * unit] for i in range(8) for q in quarters], axis=0
    ).astype(bf16)


def weave_b(refs, at_ref):
    own, other, own_2, other_2 = [r[...].astype(f32) for r in refs]
    halves = choose(at_ref[LAST_B], own, other)
    halves_2 = choose(at_ref[LAST_B], own_2, other_2)
    unit = own.shape[0] // 8
    out = []
    for half, half_2 in zip(halves, halves_2):
        even, odd = choose(at_ref[CORE], half, half_2)
        for i in range(8):
            out += [even[i * unit : (i + 1) * unit], odd[i * unit : (i + 1) * unit]]
    return jnp.concatenate(out, axis=0).astype(bf16)


def unweave(v, at_ref, unit):
    own, other = [], []
    for i in range(v.shape[0] // (2 * unit)):
        even, odd = v[2 * i * unit : (2 * i + 1) * unit], v[(2 * i + 1) * unit : (2 * i + 2) * unit]
        mine, theirs = choose(at_ref[CORE], even, odd)
        own.append(mine)
        other.append(theirs)
    return jnp.concatenate(own, axis=0), jnp.concatenate(other, axis=0)


def turn(v, at_ref):
    own, other = unweave(v.T.astype(f32), at_ref, v.shape[1] // 32)
    return own.astype(bf16), other.astype(bf16)


def call(kernel, name, grid, in_specs, out_specs, out_shape, scratch, estimate, at, args, aliases=None):
    return pl.pallas_call(
        kernel,
        grid_spec=pltpu.PrefetchScalarGridSpec(
            num_scalar_prefetch=1,
            grid=grid,
            in_specs=in_specs,
            out_specs=out_specs,
            scratch_shapes=scratch,
        ),
        out_shape=out_shape,
        compiler_params=params(),
        cost_estimate=estimate,
        input_output_aliases=aliases or {},
        name=name,
    )(at, *args)


def norm_one_kernel(at_ref, own_ref, other_ref, row_ref, x_ref, n_ref):
    ahead = pl.program_id(0) // (pl.num_programs(0) // 2) == at_ref[SEQ]
    x = jnp.where(ahead, own_ref[0].astype(f32), other_ref[...].astype(f32))
    x_ref[...] = x.astype(bf16)
    xhat, _ = norm_parts(x + row_ref[0:1, :])
    n_ref[...] = (xhat * row_ref[1:2, :] + row_ref[2:3, :]).astype(bf16)


def norm_one(at, both, other, rows, tb=256):
    half, d = other.shape
    t = 2 * half
    steps = half // tb
    tok = pl.BlockSpec((tb, d), lambda i, s: (i, 0))
    return call(
        norm_one_kernel, "norm_one", (2 * steps,),
        [
            pl.BlockSpec((1, tb, d), lambda i, s: (s[SEQ], i % steps, 0)),
            pl.BlockSpec((tb, d), lambda i, s: (i % steps, 0)),
            whole(*rows.shape),
        ],
        [tok, tok], [sds((t, d), bf16)] * 2, [],
        cost(10 * t * d, 4 * t * d), at, (both, other, rows),
    )


def weave_keys(refs, at_ref, w_ref):
    last = pl.program_id(0) == pl.num_programs(0) - 1

    @pl.when(jnp.logical_not(last))
    def _():
        w_ref[...] = weave_a(refs[:4], at_ref)

    @pl.when(last)
    def _():
        w_ref[...] = weave_b(refs[4:], at_ref)


def qkv_columns(w_a, w_b, width, groups):
    specs, args = [], []
    for pieces, column in (
        (w_a, lambda i, s: (0, i)),
        (w_a, lambda i, s: (0, groups + jnp.minimum(i, groups - 2))),
        (w_b, lambda i, s: (0, 0)),
        (w_b, lambda i, s: (0, 1 + i)),
    ):
        specs += [pl.BlockSpec((pieces[0].shape[0], width), column)] * 4
        args += pieces
    return specs, args


def attend_kernel(at_ref, n_ref, *refs, heads, qb):
    q_ref, k_ref, v_ref, o_ref, lse_ref, wk_ref = refs[16:]
    t = n_ref.shape[0]
    n = n_ref[...]
    weave_keys(refs[4:12], at_ref, wk_ref)
    q_ref[...] = nn(n, weave_a(refs[0:4], at_ref)).astype(bf16)
    k_ref[...] = nn(n, wk_ref[...]).astype(bf16)
    v_ref[...] = nn(n, weave_b(refs[12:16], at_ref)).astype(bf16)

    def run(parts):
        span = t // parts
        blocks = [(h, q0) for h in range(heads) for q0 in range(0, t, qb)]

        def scores(h, q0):
            hs = slice(h * HD, (h + 1) * HD)
            k0 = (q0 // span) * span
            return nt(k_ref[k0 : k0 + span, hs], q_ref[q0 : q0 + qb, hs] * bf16(0.125))

        ahead = scores(*blocks[0])
        for i, (h, q0) in enumerate(blocks):
            s = ahead
            if i + 1 < len(blocks):
                ahead = scores(*blocks[i + 1])
            hs = slice(h * HD, (h + 1) * HD)
            k0 = (q0 // span) * span
            top = jnp.max(s, axis=0, keepdims=True)
            p = jnp.exp2((s - top) * f32(LOG2E))
            total = jnp.sum(p, axis=0, keepdims=True)
            probs = (p * (1.0 / total)).astype(bf16)
            o_ref[q0 : q0 + qb, hs] = tn(probs, v_ref[k0 : k0 + span, hs]).astype(bf16)
            lse_ref[h // 2, h % 2 : h % 2 + 1, q0 : q0 + qb] = top + jnp.log(total)

    short = at_ref[SHORT]

    @pl.when(short == 0)
    def _():
        run(1)

    @pl.when(short != 0)
    def _():
        run(2)


def attend(at, n, w_a, w_b, heads=4, qb=512):
    t, d = n.shape
    c = heads * HD
    groups = d // c
    specs, args = qkv_columns(w_a, w_b, c, groups)
    tok = pl.BlockSpec((t, c), lambda g, s: (0, g))
    return call(
        functools.partial(attend_kernel, heads=heads, qb=qb), "attend", (groups,),
        [whole(t, d)] + specs,
        [tok] * 4 + [pl.BlockSpec((heads // 2, 2, t), lambda g, s: (g, 0, 0))],
        [sds((t, d), bf16)] * 4 + [sds((groups * heads // 2, 2, t), f32)], [pltpu.VMEM((d, c), bf16)],
        cost(6 * t * d * d + 16 * t * t * d, 20 * t * d, t * t * d // HD),
        at, (n, *args),
    )


def attend_back_kernel(at_ref, q_ref, k_ref, v_ref, o_ref, do_ref, lse_ref, *refs, heads, qb):
    dq_ref, dk_ref, dv_ref = refs[-3:]
    t = q_ref.shape[0]

    def run(parts):
        span = t // parts
        k_turned = k_ref[...].T
        prod = (do_ref[...].astype(f32) * o_ref[...].astype(f32)).T
        for h in range(heads):
            hs = slice(h * HD, (h + 1) * HD)
            for b in range(parts):
                ks = slice(b * span, (b + 1) * span)
                k = k_ref[ks, hs]
                v = v_ref[ks, hs]
                dk = dv = None
                for q0 in range(b * span, (b + 1) * span, qb):
                    qs = slice(q0, q0 + qb)
                    q = q_ref[qs, hs] * bf16(0.125)
                    do = do_ref[qs, hs]
                    delta = jnp.sum(prod[hs, qs], axis=0, keepdims=True)
                    p = jnp.exp2((nt(k, q) - lse_ref[0, h : h + 1, qs]) * f32(LOG2E))
                    ds = (p * (nt(v, do) - delta)).astype(bf16)
                    dv_part = nn(p.astype(bf16), do)
                    dk_part = nn(ds, q)
                    dv = dv_part if dv is None else dv + dv_part
                    dk = dk_part if dk is None else dk + dk_part
                    dq_ref[qs, hs] = (nn(k_turned[hs, ks], ds) * f32(0.125)).T.astype(bf16)
                dk_ref[ks, hs] = dk.astype(bf16)
                dv_ref[ks, hs] = dv.astype(bf16)

    short = at_ref[SHORT]

    @pl.when(short == 0)
    def _():
        run(1)

    @pl.when(short != 0)
    def _():
        run(2)


def attend_back(at, q, k, v, o, do, lse, part, parts, before=(), heads=2, qb=256):
    t, d = q.shape
    c = heads * HD
    count = d // c // parts
    first = part * count
    tok = pl.BlockSpec((t, c), lambda g, s: (0, first + g))
    return call(
        functools.partial(attend_back_kernel, heads=heads, qb=qb), f"attend_back_{part}", (count,),
        [tok] * 5
        + [pl.BlockSpec((1, heads, t), lambda g, s: (first + g, 0, 0))]
        + [pl.BlockSpec(memory_space=pl.ANY)] * len(before),
        [tok] * 3, [sds((t, d), bf16)] * 3, [],
        cost(40 * t * t * d // parts, 16 * t * d // parts, t * t * d // HD // parts),
        at, (q, k, v, o, do, lse, *before),
        {7 + i: i for i in range(len(before))},
    )


def mix_kernel(
    at_ref, x_ref, o_ref, w0_ref, w1_ref, w2_ref, w3_ref, row_ref, mid_ref, n_ref, w_ref,
):
    @pl.when(pl.program_id(0) == 0)
    def _():
        w_ref[...] = weave_a((w0_ref, w1_ref, w2_ref, w3_ref), at_ref)

    mid = x_ref[...].astype(f32) + row_ref[0:1, :] + nn(o_ref[...], w_ref[...])
    mid_ref[...] = mid
    xhat, _ = norm_parts(mid)
    n_ref[...] = (xhat * row_ref[3:4, :] + row_ref[4:5, :]).astype(bf16)


def last_columns(pieces, width):
    return [
        pl.BlockSpec((p.shape[0], width), (lambda k: lambda i, s: (0, k))(p.shape[1] // width - 1))
        for p in pieces
    ]


def mix(at, x, o, out, rows, tb=256):
    t, d = x.shape
    tok = pl.BlockSpec((tb, d), lambda i, s: (i, 0))
    return call(
        mix_kernel, "mix", (t // tb,),
        [tok, tok] + last_columns(out, d) + [whole(*rows.shape)],
        [tok] * 2, [sds((t, d), f32), sds((t, d), bf16)],
        [pltpu.VMEM((d, d), bf16)], cost(2 * t * d * d, 12 * t * d), at, (x, o, *out, rows),
    )


def gelu_parts(u):
    e = jnp.exp(u * u * f32(-0.5))
    r = pl.reciprocal(1.0 + f32(0.3275911 * 0.7071067811865476) * jnp.abs(u))
    poly = f32(-1.453152027) + r * f32(1.061405429)
    poly = f32(1.421413741) + r * poly
    poly = f32(-0.284496736) + r * poly
    poly = r * (f32(0.254829592) + r * poly)
    tail = f32(0.5) * poly * e
    return jnp.where(u >= 0, 1.0 - tail, tail), e * f32(0.3989422804014327)


def ffn_kernel(at_ref, n_ref, here_ref, there_ref, there_2_ref, mid_any, *refs):
    ub_ref, row_ref, own_ref, send_ref, du_ref, keep_ref, give_ref, gub_ref, small_ref, dy_ref = refs[8:18]
    acc, act, mid_ref, mid_sem = refs[18:]
    j = pl.program_id(0)
    late = pltpu.make_async_copy(mid_any, mid_ref, mid_sem)

    @pl.when(j == 0)
    def _():
        late.start()
        acc[...] = jnp.zeros_like(acc)
        there = jnp.concatenate([there_ref[...].astype(f32), there_2_ref[...].astype(f32)], axis=0)
        halves = choose(at_ref[SEQ], here_ref[0].astype(f32), there)
        half = there.shape[0]
        dy_ref[:half, :] = halves[0].astype(bf16)
        dy_ref[half:, :] = halves[1].astype(bf16)

    wu = weave_a(refs[:4], at_ref)
    other = (j // (pl.num_programs(0) // 2)) != at_ref[LAST_B]
    even_odd = choose(
        at_ref[CORE],
        jnp.where(other, refs[5][...].astype(f32), refs[4][...].astype(f32)),
        jnp.where(other, refs[7][...].astype(f32), refs[6][...].astype(f32)),
    )
    short, d = refs[4].shape[0] // 4, dy_ref.shape[1]
    wd = jnp.concatenate(
        [
            v[i * short : (i + 1) * short, k * d : (k + 1) * d]
            for i in range(4)
            for v in even_odd
            for k in range(4)
        ],
        axis=0,
    ).astype(bf16)
    unit = 4 * short
    ub = ub_ref[...].astype(f32)
    t, fb = act.shape
    tb = t // 4
    gub = jnp.zeros((1, fb), f32)
    for i in range(4):
        sl = slice(i * tb, (i + 1) * tb)
        u = nn(n_ref[sl, :], wu) + ub
        da = nt(dy_ref[sl, :], wd)
        cdf, pdf = gelu_parts(u)
        active = (u * cdf).astype(bf16)
        act[sl, :] = active
        du = (da * (cdf + u * pdf)).astype(bf16)
        du_ref[sl, :] = du
        gub = gub + jnp.sum(du.astype(f32), axis=0, keepdims=True)
        acc[sl, :] += nn(active, wd)
    gub_ref[...] = gub
    own, theirs = unweave(tn(act[...], dy_ref[...]), at_ref, unit)
    keep_ref[...] = own.astype(bf16)
    give_ref[...] = theirs.astype(bf16)

    @pl.when(j == pl.num_programs(0) - 1)
    def _():
        half = t // 2
        late.wait()
        result = acc[...] + mid_ref[...] + row_ref[5:6, :]
        own, theirs = choose(at_ref[SEQ], result[:half, :], result[half:, :])
        own_ref[...] = own.astype(bf16)
        send_ref[...] = theirs.astype(bf16)
        small_ref[...] = jnp.sum(dy_ref[...].astype(f32), axis=0, keepdims=True)


def ffn(at, n, both, other, mid, up_out, down, up_bias, rows):
    t, d = n.shape
    ff = up_bias.shape[1]
    fb = ff // 4
    high, low = up_out[0].shape[0], down[0].shape[0]
    chunk = pl.BlockSpec((fb // 2, d), lambda j, s: (j, 0))
    return call(
        ffn_kernel, "ffn", (4,),
        [whole(t, d), pl.BlockSpec((1, t // 2, d), lambda j, s: (s[SEQ], 0, 0)), whole(t // 4, d), whole(t // 4, d)]
        + [pl.BlockSpec(memory_space=pl.ANY)]
        + [pl.BlockSpec((high, fb), lambda j, s: (0, j))] * 4
        + [pl.BlockSpec((low // 2, 4 * d), lambda j, s: (j % 2, 0))] * 4
        + [pl.BlockSpec((1, fb), lambda j, s: (0, j)), whole(*rows.shape)],
        [whole(t // 2, d)] * 2
        + [pl.BlockSpec((t, fb), lambda j, s: (0, j)), chunk, chunk]
        + [pl.BlockSpec((1, fb), lambda j, s: (0, j)), whole(1, d), whole(t, d)],
        [sds((t // 2, d), bf16)] * 2
        + [sds((t, ff), bf16)]
        + [sds((ff // 2, d), bf16)] * 2
        + [sds((1, ff), f32), sds((1, d), f32), sds((t, d), bf16)],
        [pltpu.VMEM((t, d), f32), pltpu.VMEM((t, fb), bf16), pltpu.VMEM((t, d), f32), pltpu.SemaphoreType.DMA],
        cost(8 * t * d * ff, 20 * t * d + 8 * d * ff, 2 * t * ff),
        at, (n, both, *other, mid, *up_out, *down, up_bias, rows),
    )


def unffn_kernel(at_ref, n_ref, dy_any, mid_any, du_ref, o_any, row_ref, *refs):
    dmid_ref, do_ref, keep_ref, give_ref, small_ref, acc, turned, turned_2 = refs[8:16]
    dy_ref, mid_ref, o_ref, dy_sem, mid_sem, o_sem = refs[16:]
    late = [
        pltpu.make_async_copy(*pair_of)
        for pair_of in ((dy_any, dy_ref, dy_sem), (mid_any, mid_ref, mid_sem), (o_any, o_ref, o_sem))
    ]
    j = pl.program_id(0)
    last = pl.num_programs(0) - 1

    @pl.when(j == 0)
    def _():
        for copy in late:
            copy.start()
        acc[...] = jnp.zeros_like(acc)
        turned[...], turned_2[...] = turn(n_ref[...], at_ref)

    @pl.when(j < last)
    def _():
        du = du_ref[...]
        w = weave_a(refs[:4], at_ref)
        keep_ref[...] = nn(turned[...], du).astype(bf16)
        give_ref[...] = nn(turned_2[...], du).astype(bf16)
        acc[...] += nt(du, w)

    @pl.when(j == last)
    def _():
        for copy in late:
            copy.wait()
        xhat, s = norm_parts(mid_ref[...])
        e = acc[...]
        small_ref[...] = jnp.concatenate(
            [jnp.sum(e * xhat, axis=0, keepdims=True), jnp.sum(e, axis=0, keepdims=True)], axis=0
        )
        dmid = dy_ref[...].astype(f32) + norm_back(e, row_ref[3:4, :], xhat, s)
        dmid_ref[...] = dmid
        db = dmid.astype(bf16)
        do_ref[...] = nt(db, weave_a(refs[4:8], at_ref)).astype(bf16)
        own, other = unweave(tn(o_ref[...], db), at_ref, db.shape[1] // 32)
        keep_ref[...] = own.astype(bf16)
        give_ref[...] = other.astype(bf16)


def unffn(at, n, dy, mid, du, up, out, o, rows):
    t, d = n.shape
    ff = du.shape[1]
    count = ff // d
    cols = pl.BlockSpec((d // 2, d), lambda j, s: (0, j))
    return call(
        unffn_kernel, "unffn", (count + 1,),
        [whole(t, d)] + [pl.BlockSpec(memory_space=pl.ANY)] * 2
        + [pl.BlockSpec((t, d), lambda j, s: (0, jnp.minimum(j, count - 1)))]
        + [pl.BlockSpec(memory_space=pl.ANY), whole(*rows.shape)]
        + [pl.BlockSpec((p.shape[0], d), lambda j, s: (0, jnp.minimum(j, count - 1))) for p in up]
        + last_columns(out, d),
        [whole(t, d)] * 2 + [cols] * 2 + [whole(2, d)],
        [sds((t, d), f32), sds((t, d), bf16)] + [sds((d // 2, ff + d), bf16)] * 2 + [sds((2, d), f32)],
        [pltpu.VMEM((t, d), f32)] + [pltpu.VMEM((d // 2, t), bf16)] * 2
        + [pltpu.VMEM((t, d), bf16), pltpu.VMEM((t, d), f32), pltpu.VMEM((t, d), bf16)]
        + [pltpu.SemaphoreType.DMA] * 3,
        cost(4 * t * d * (ff + d), 20 * t * d + 8 * d * ff),
        at, (n, dy, mid, du, o, rows, *up, *out),
    )


def grad_qkv_kernel(at_ref, n_ref, dq_ref, dk_ref, dv_ref, keep_ref, give_ref, turned, turned_2):
    @pl.when(pl.program_id(0) == 0)
    def _():
        turned[...], turned_2[...] = turn(n_ref[...], at_ref)

    for i, d_ref in enumerate((dq_ref, dk_ref, dv_ref)):
        keep_ref[i] = nn(turned[...], d_ref[...]).astype(bf16)
        give_ref[i] = nn(turned_2[...], d_ref[...]).astype(bf16)


def grad_qkv(at, n, dq, dk, dv, cb=256):
    t, d = n.shape
    tok = pl.BlockSpec((t, cb), lambda i, s: (0, i))
    out = pl.BlockSpec((3, d // 2, cb), lambda i, s: (0, 0, i))
    return call(
        grad_qkv_kernel, "grad_qkv", (d // cb,),
        [whole(t, d)] + [tok] * 3, [out] * 2, [sds((3, d // 2, d), bf16)] * 2,
        [pltpu.VMEM((d // 2, t), bf16)] * 2,
        cost(6 * t * d * d, 20 * t * d), at, (n, dq, dk, dv),
    )


def unqkv_kernel(at_ref, x_any, row_ref, dmid_any, *refs):
    dq_ref, dk_ref, dv_ref, own_ref, send_ref, small_ref, acc, wk_ref = refs[16:24]
    x_ref, dmid_ref, x_sem, dmid_sem = refs[24:]
    i = pl.program_id(0)
    late = [
        pltpu.make_async_copy(x_any, x_ref, x_sem), pltpu.make_async_copy(dmid_any, dmid_ref, dmid_sem)
    ]

    @pl.when(i == 0)
    def _():
        for copy in late:
            copy.start()

    weave_keys(refs[4:12], at_ref, wk_ref)
    w = [weave_a(refs[0:4], at_ref), wk_ref[...], weave_b(refs[12:16], at_ref)]
    e = nt(
        jnp.concatenate([dq_ref[...], dk_ref[...], dv_ref[...]], axis=1),
        jnp.concatenate(w, axis=1),
    )

    @pl.when(i == 0)
    def _():
        acc[...] = e

    @pl.when(i > 0)
    def _():
        acc[...] += e

    @pl.when(i == pl.num_programs(0) - 1)
    def _():
        for copy in late:
            copy.wait()
        e = acc[...]
        xhat, s = norm_parts(x_ref[...].astype(f32) + row_ref[0:1, :])
        d_base = dmid_ref[...] + norm_back(e, row_ref[1:2, :], xhat, s)
        half = d_base.shape[0] // 2
        own, theirs = choose(at_ref[SEQ], d_base[:half], d_base[half:])
        own_ref[...] = own.astype(bf16)
        send_ref[...] = theirs.astype(bf16)
        small_ref[...] = jnp.concatenate(
            [
                jnp.sum(e * xhat, axis=0, keepdims=True),
                jnp.sum(e, axis=0, keepdims=True),
                jnp.sum(d_base, axis=0, keepdims=True),
            ],
            axis=0,
        )


def unqkv(at, x, rows, dmid, w_a, w_b, dq, dk, dv, cb=256):
    t, d = x.shape
    count = d // cb
    specs, args = qkv_columns(w_a, w_b, cb, count)
    tok = pl.BlockSpec((t, cb), lambda i, s: (0, i))
    return call(
        unqkv_kernel, "unqkv", (count,),
        [pl.BlockSpec(memory_space=pl.ANY), whole(*rows.shape), pl.BlockSpec(memory_space=pl.ANY)]
        + specs + [tok] * 3,
        [whole(t // 2, d)] * 2 + [whole(3, d)],
        [sds((t // 2, d), bf16)] * 2 + [sds((3, d), f32)],
        [pltpu.VMEM((t, d), f32), pltpu.VMEM((d, cb), bf16), pltpu.VMEM((t, d), bf16), pltpu.VMEM((t, d), f32)]
        + [pltpu.SemaphoreType.DMA] * 2,
        cost(6 * t * d * d, 30 * t * d), at, (x, rows, dmid, *args, dq, dk, dv),
    )


class Grid:
    def __init__(self, seq, rows):
        self.seq, self.rows = seq, rows
        self.known = seq == 2 and rows == 16
        at = lax.axis_index("rows")
        self.x = lax.axis_index("seq")
        self.z, self.y, self.c = at // 4, (at // 2) % 2, at % 2

    def table(self, move):
        pairs = []
        for x in range(self.seq):
            for z in range(4):
                for y in range(2):
                    for c in range(2):
                        x2, z2, y2, c2 = move(x, z, y, c)
                        pairs.append((x * 16 + z * 4 + y * 2 + c, x2 * 16 + z2 * 4 + y2 * 2 + c2))
        return pairs

    def swap(self, v, axis):
        move = {
            "x": lambda x, z, y, c: (1 - x, z, y, c),
            "y": lambda x, z, y, c: (x, z, 1 - y, c),
            "c": lambda x, z, y, c: (x, z, y, 1 - c),
        }[axis]
        return lax.ppermute(v, BOTH, self.table(move))

    def cross(self, v, bit):
        return lax.ppermute(v, BOTH, self.table(lambda x, z, y, c: (x, z ^ bit, y, c)))

    def shift(self, v, by):
        return lax.ppermute(v, BOTH, self.table(lambda x, z, y, c: (x, (z + by) % 4, y, c)))


def tie(*values):
    return lax.optimization_barrier(values)


def after(v, *first):
    return lax.optimization_barrier((v, first))[0]


def spread(v, axis, count):
    return jnp.broadcast_to(jnp.expand_dims(v, axis), v.shape[:axis] + (count,) + v.shape[axis:])


def pair(own, other, at, axis):
    shape = own.shape[:axis] + (2,) + own.shape[axis:]
    here = lax.broadcasted_iota(jnp.int32, shape, axis) == at
    return jnp.where(here, spread(own, axis, 2), spread(other, axis, 2))


def arrange_z(g, v, shifts):
    out = spread(v, 0, 4)
    place = lax.broadcasted_iota(jnp.int32, out.shape, 0)
    for k, got in enumerate(shifts):
        out = jnp.where(place == (g.z - k - 1) % 4, spread(got, 0, 4), out)
    return out


def gather_z(g, v):
    return arrange_z(g, v, [g.shift(v, k) for k in range(1, 4)])


def flat(v):
    return v.reshape(-1, v.shape[-1])


def quarters(whole_array, kind):
    v = whole_array.reshape(2, 4, 2, 2, -1, whole_array.shape[1])
    pieces = []
    for core in range(2):
        for place in range(2):
            pieces.append(flat(v[:, :, place, core] if kind == "a" else v[place, :, :, core]))
    return pieces


def keep(v, at, axis):
    return lax.dynamic_index_in_dim(v, at, axis, keepdims=False)


def add(a, b):
    return (a.astype(f32) + b.astype(f32)).astype(bf16)


def split_plane(g, a, b):
    a = add(keep(a, g.x, -5), g.swap(keep(a, 1 - g.x, -5), "x"))
    b = add(keep(b, g.y, -3), g.swap(keep(b, 1 - g.y, -3), "y"))
    a, b = yield a, b
    got_a = g.swap(keep(a, 1 - g.y, -3), "y")
    got_b = g.swap(keep(b, 1 - g.x, -4), "x")
    got_a, got_b = yield got_a, got_b
    yield add(keep(a, g.y, -3), got_a), add(keep(b, g.x, -4), got_b)


def split_z(g, v):
    total = keep(v, g.z, -3).astype(f32)
    for k in range(1, 4):
        total = total + g.shift(keep(v, (g.z + k) % 4, -3), k).astype(f32)
    return total


def halve_z(g, v):
    v = v.reshape(*v.shape[:-3], 2, 2, *v.shape[-2:])
    high, low = g.z // 2, g.z % 2
    v = keep(v, low, -3).astype(f32) + g.cross(keep(v, 1 - low, -3), 1).astype(f32)
    got = yield g.cross(keep(v, 1 - high, -3).astype(bf16), 2)
    yield keep(v, high, -3) + got.astype(f32)


def scatter_plain(own, other):
    v = jnp.stack([own.reshape(16, -1, own.shape[1]), other.reshape(16, -1, own.shape[1])], axis=1)
    return lax.psum_scatter(flat(v).astype(f32), BOTH, scatter_dimension=0, tiled=True)


def swap_seq(v):
    return lax.ppermute(v, "seq", [(0, 1), (1, 0)])


def local(
    inputs, timesteps, boundary, step_table, w_qkv, w_out, w_up, w_down,
    norm1_gain, norm1_shift, norm2_gain, norm2_shift, up_bias, down_bias, cotangent,
):
    seq, row_blocks = lax.axis_size("seq"), lax.axis_size("rows")
    g = Grid(seq, row_blocks)
    devices = seq * row_blocks
    d = inputs.shape[2]
    shard = w_qkv.shape[0]
    ff = w_up.shape[1]
    steps = step_table.shape[0]
    wide = (ff // devices) // shard
    short = (g.x < boundary[0]).astype(jnp.int32)
    zero = jnp.zeros_like(short)
    at = jnp.stack([short, g.x] + ([g.y, g.x, g.c] if g.known else [zero] * 3))

    digits = jnp.concatenate([timesteps // 128, timesteps % 128]).astype(bf16)
    shorts = jnp.concatenate(
        [norm1_gain, norm1_shift, norm2_gain, norm2_shift, down_bias, up_bias, digits]
    )
    shorts = jnp.broadcast_to(shorts[None], (devices,) + shorts.shape)
    shorts = lax.all_to_all(shorts, BOTH, split_axis=0, concat_axis=0, tiled=True)
    x_other = swap_seq(keep(inputs, 1 - g.x, 0))
    unit = w_down.shape[0] // 4
    down_wide = w_down.reshape(4, unit, d).transpose(1, 0, 2).reshape(unit, -1)

    def look_up(shorts):
        digits = shorts[:, (5 + wide) * shard :].reshape(seq, row_blocks, 2, -1)[0].astype(jnp.int32)
        all_steps = digits[:, 0] * 128 + digits[:, 1]
        hot = all_steps.T.reshape(-1)[:, None] == jnp.arange(steps, dtype=jnp.int32)[None]
        found = nn(hot.astype(bf16), step_table).astype(bf16)
        found = lax.all_to_all(found, BOTH, split_axis=0, concat_axis=0, tiled=True)
        return all_steps.reshape(-1), found

    def norm_rows(shorts, found):
        rows = jnp.stack([found] + [shorts[:, i * shard : (i + 1) * shard] for i in range(5)])
        return jnp.pad(rows.reshape(6, d).astype(f32), ((0, 2), (0, 0)))

    if g.known:
        shifts = [g.shift(w_qkv, k) for k in range(1, 4)]
        rest = jnp.concatenate([w_up, w_out, down_wide], axis=1)
        rest_2 = g.cross(rest, 2)
        first = arrange_z(g, w_qkv, shifts)
        half = d + 2 * d // 3
        a, b = first[..., :half], first[..., half:]
        a = pair(a, g.swap(a, "x"), g.x, 0)
        b = pair(b, g.swap(b, "y"), g.y, 1)
        a, b, x_other, shorts, rest_2 = tie(a, b, x_other, shorts, rest_2)
        rest = pair(rest, rest_2, g.z // 2, 0)
        rest_1 = g.cross(rest, 1)
        all_steps, found = look_up(shorts)
        a_2, b_2 = g.swap(a, "y"), g.swap(b, "x")
        a_c, b_c = g.swap(a, "c"), g.swap(b, "c")
        w_a = [flat(v) for v in (a, a_2, a_c, g.swap(a_2, "c"))]
        w_b = [flat(v) for v in (b, b_2, b_c, g.swap(b_2, "c"))]
        rest, rest_1, found, a_2, b_2 = tie(rest, rest_1, found, a_2, b_2)
        rest = pair(rest, rest_1, g.z % 2, 1)
        rest = rest.reshape(4, *rest.shape[2:])
        rows = norm_rows(shorts, found)
        x, normed_one = norm_one(at, inputs, x_other, rows)
        a, b = rest[..., : ff + d], rest[..., ff + d :]
        a = pair(a, g.swap(a, "x"), g.x, 0)
        b = pair(b, g.swap(b, "y"), g.y, 1)
        a, b, normed_one = tie(a, b, normed_one)
        a_2, b_2 = g.swap(a, "y"), g.swap(b, "x")
        a_c, b_c = g.swap(a, "c"), g.swap(b, "c")
    else:
        half = d + 2 * d // 3
        w_a, w_b, up_out, down = [
            quarters(lax.all_gather(v, BOTH, axis=0, tiled=True), kind)
            for v, kind in (
                (w_qkv[:, :half], "a"),
                (w_qkv[:, half:], "b"),
                (jnp.concatenate([w_up, w_out], axis=1), "a"),
                (down_wide, "b"),
            )
        ]
        all_steps, found = look_up(shorts)
        rows = norm_rows(shorts, found)
        x, normed_one = norm_one(at, inputs, x_other, rows)

    up_row = shorts[:, 5 * shard : (5 + wide) * shard].reshape(1, ff)
    q, k, v, attended, lse = attend(at, normed_one, w_a, w_b)
    dy_send = keep(cotangent, 1 - g.x, 0)
    dy_other = [swap_seq(v) for v in jnp.split(dy_send, 2)]
    if g.known:
        q, k, v, lse, attended, dy_other[0] = tie(q, k, v, lse, attended, dy_other[0])
        a_2, b_2, attended = tie(a_2, b_2, attended)
        out = [flat(v) for v in (a, a_2, a_c, g.swap(a_2[..., ff:], "c"))]
        up_out = [flat(v) for v in (a, a_2, a_c, g.swap(a_2, "c"))]
        down = [flat(v) for v in (b, b_2, b_c, g.swap(b_2, "c"))]
    else:
        out = up_out
    middle, normed_two = mix(at, x, attended, out, rows)
    block_own, block_send, d_upper, keep_down, give_down, g_up_row, g_down_row, dy = ffn(
        at, normed_two, cotangent, dy_other, middle, up_out, down, up_row, rows
    )
    block_other = swap_seq(block_send)
    d_middle, d_attended, keep_up, give_up, small_two = unffn(
        at, normed_two, dy, middle, d_upper, up_out, out, attended, rows
    )
    six = (2, 4, 2)
    if g.known:
        d_middle, d_attended, keep_up, give_up, small_two, block_other = tie(
            d_middle, d_attended, keep_up, give_up, small_two, block_other
        )
        down = add(keep_down, g.swap(give_down, "c")).reshape(*six, -1, d)
        d_attended, down = tie(d_attended, down)
        down_plane = split_plane(g, down[..., : d // 2], down[..., d // 2 :])
    back = attend_back(at, q, k, v, attended, d_attended, lse, 0, 2)
    if g.known:
        cut = (ff + d) // 2
        up = add(keep_up, g.swap(give_up, "c")).reshape(*six, -1, ff + d)
        down_half = next(down_plane)
        d_attended, up, down_half, *back = tie(d_attended, up, down_half, *back)
        up_plane = split_plane(g, up[..., :cut], up[..., cut:])
        down_got = down_plane.send(down_half)
    dq, dk, dv = attend_back(at, q, k, v, attended, d_attended, lse, 1, 2, tuple(back))
    n = normed_one
    if g.known:
        up_half = next(up_plane)
        n, up_half, dq, down_got = tie(n, up_half, dq, down_got)
        up_got = up_plane.send(up_half)
        down = jnp.concatenate(down_plane.send(down_got), axis=-1)
        down_z = halve_z(g, down)
    keep_qkv, give_qkv = grad_qkv(at, n, dq, dk, dv)
    if g.known:
        keep_qkv, up_got = tie(keep_qkv, up_got)
        qkv = add(keep_qkv, g.swap(give_qkv, "c")).reshape(3, *six, shard, d)
        up = jnp.concatenate(up_plane.send(up_got), axis=-1)
        d_middle, qkv, up = tie(d_middle, qkv, up)
        a = jnp.concatenate([qkv[0], qkv[1, ..., : d // 2]], axis=-1)
        b = jnp.concatenate([qkv[1, ..., d // 2 :], qkv[2]], axis=-1)
        plane = split_plane(g, a, b)
    d_own, d_send, small_one = unqkv(at, x, rows, d_middle, w_a, w_b, dq, dk, dv)
    if g.known:
        ready = next(plane)
        small_one, d_send, ready, down_got = tie(small_one, d_send, ready, next(down_z))
        sum_down = down_z.send(down_got)
        up_z = halve_z(g, up)
        got = plane.send(ready)
    d_other = swap_seq(d_send)

    small = jnp.concatenate([small_two, g_down_row, small_one], axis=0)
    small = small.reshape(-1, devices, shard).transpose(1, 0, 2).reshape(devices, -1)
    small = jnp.concatenate([small, g_up_row.reshape(devices, -1)], axis=1)
    small = lax.all_to_all(small, BOTH, split_axis=0, concat_axis=0, tiled=True)
    row_sums = small[:, 5 * shard : 6 * shard].reshape(seq, row_blocks, shard).transpose(1, 0, 2)
    row_sums = row_sums.reshape(devices, shard)
    small = jnp.sum(small, axis=0)
    if g.known:
        sum_up = up_z.send(next(up_z))
        last = jnp.concatenate(plane.send(got), axis=-1)
        block_out = pair(block_own, block_other, g.x, 0)
        d_other, last, block_out = tie(d_other, split_z(g, last), block_out)
    else:
        sum_up, sum_down = scatter_plain(keep_up, give_up), scatter_plain(keep_down, give_down)
        last = [scatter_plain(keep_qkv[i], give_qkv[i]) for i in range(3)]
        last = jnp.concatenate(last, axis=1)
        block_out = pair(block_own, block_other, g.x, 0)
    grad_inputs = pair(d_own, d_other, g.x, 0)
    hot = (jnp.arange(steps, dtype=jnp.int32)[:, None] == all_steps[None]).astype(f32)
    g_table = lax.dot_general(
        hot, row_sums, (((1,), (0,)), ((), ())), precision=lax.Precision.HIGHEST,
        preferred_element_type=f32,
    )
    return (
        block_out,
        grad_inputs,
        g_table,
        last,
        sum_up[:, ff:],
        sum_up[:, :ff],
        sum_down,
        *[small[i * shard : (i + 1) * shard] for i in (3, 4, 0, 1)],
        small[6 * shard :],
        small[2 * shard : 3 * shard],
    )


def solution(mesh):
    tokens, weight, vector = P("rows", "seq", None), P(BOTH, None), P(BOTH)
    table = P(None, BOTH)
    in_specs = (
        (tokens, P("rows"), P("rows"), table) + (weight,) * 4 + (vector,) * 6 + (tokens,)
    )
    out_specs = (tokens, tokens, table) + (weight,) * 4 + (vector,) * 6
    return jax.shard_map(local, mesh=mesh, in_specs=in_specs, out_specs=out_specs, check_vma=False)
```

```python
import functools

import jax
import jax.numpy as jnp
from jax import lax
from jax.experimental import pallas as pl
from jax.experimental.pallas import tpu as pltpu
from jax.sharding import PartitionSpec as P

f32 = jnp.float32
bf16 = jnp.bfloat16
HD = 64
EPS = 1e-5
LOG2E = 1.4426950408889634
VMEM = 56 * 1024 * 1024
BOTH = ("seq", "rows")
WEIGHT = 0.02


def nn(a, b):
    return lax.dot_general(a, b, (((1,), (0,)), ((), ())), preferred_element_type=f32)


def nt(a, b):
    return lax.dot_general(a, b, (((1,), (1,)), ((), ())), preferred_element_type=f32)


def tn(a, b):
    return lax.dot_general(a, b, (((0,), (0,)), ((), ())), preferred_element_type=f32)


def sds(shape, dtype):
    return jax.ShapeDtypeStruct(shape, dtype)


def whole(*shape):
    return pl.BlockSpec(shape, lambda *_: (0,) * len(shape))


def params():
    return pltpu.CompilerParams(vmem_limit_bytes=VMEM, dimension_semantics=("arbitrary",))


def cost(flops, nbytes, trans=0):
    return pl.CostEstimate(
        flops=int(flops * WEIGHT), bytes_accessed=int(nbytes * WEIGHT), transcendentals=int(trans * WEIGHT)
    )


def norm_parts(v):
    c = v - jnp.mean(v, axis=1, keepdims=True)
    s = lax.rsqrt(jnp.mean(c * c, axis=1, keepdims=True) + EPS)
    return c * s, s


def norm_back(e, gain, xhat, s):
    f = e * gain
    return s * (
        f
        - jnp.mean(f, axis=1, keepdims=True)
        - xhat * jnp.mean(f * xhat, axis=1, keepdims=True)
    )


SHORT, SEQ, LAST_A, LAST_B, CORE = range(5)


def choose(flag, a, b):
    return jnp.where(flag == 0, a, b), jnp.where(flag == 0, b, a)


def weave_a(refs, at_ref):
    own, other, own_2, other_2 = [r[...].astype(f32) for r in refs]
    first, second = choose(at_ref[LAST_A], own, other)
    first_2, second_2 = choose(at_ref[LAST_A], own_2, other_2)
    quarters = choose(at_ref[CORE], first, first_2) + choose(at_ref[CORE], second, second_2)
    unit = own.shape[0] // 8
    return jnp.concatenate(
        [q[i * unit : (i + 1) * unit] for i in range(8) for q in quarters], axis=0
    ).astype(bf16)


def weave_b(refs, at_ref):
    own, other, own_2, other_2 = [r[...].astype(f32) for r in refs]
    halves = choose(at_ref[LAST_B], own, other)
    halves_2 = choose(at_ref[LAST_B], own_2, other_2)
    unit = own.shape[0] // 8
    out = []
    for half, half_2 in zip(halves, halves_2):
        even, odd = choose(at_ref[CORE], half, half_2)
        for i in range(8):
            out += [even[i * unit : (i + 1) * unit], odd[i * unit : (i + 1) * unit]]
    return jnp.concatenate(out, axis=0).astype(bf16)


def unweave(v, at_ref, unit):
    own, other = [], []
    for i in range(v.shape[0] // (2 * unit)):
        even, odd = v[2 * i * unit : (2 * i + 1) * unit], v[(2 * i + 1) * unit : (2 * i + 2) * unit]
        mine, theirs = choose(at_ref[CORE], even, odd)
        own.append(mine)
        other.append(theirs)
    return jnp.concatenate(own, axis=0), jnp.concatenate(other, axis=0)


def turn(v, at_ref):
    own, other = unweave(v.T.astype(f32), at_ref, v.shape[1] // 32)
    return own.astype(bf16), other.astype(bf16)


def call(kernel, name, grid, in_specs, out_specs, out_shape, scratch, estimate, at, args, aliases=None):
    return pl.pallas_call(
        kernel,
        grid_spec=pltpu.PrefetchScalarGridSpec(
            num_scalar_prefetch=1,
            grid=grid,
            in_specs=in_specs,
            out_specs=out_specs,
            scratch_shapes=scratch,
        ),
        out_shape=out_shape,
        compiler_params=params(),
        cost_estimate=estimate,
        input_output_aliases=aliases or {},
        name=name,
    )(at, *args)


def norm_one_kernel(at_ref, own_ref, other_ref, row_ref, x_ref, n_ref):
    ahead = pl.program_id(0) // (pl.num_programs(0) // 2) == at_ref[SEQ]
    x = jnp.where(ahead, own_ref[0].astype(f32), other_ref[...].astype(f32))
    x_ref[...] = x.astype(bf16)
    xhat, _ = norm_parts(x + row_ref[0:1, :])
    n_ref[...] = (xhat * row_ref[1:2, :] + row_ref[2:3, :]).astype(bf16)


def norm_one(at, both, other, rows, tb=256):
    half, d = other.shape
    t = 2 * half
    steps = half // tb
    tok = pl.BlockSpec((tb, d), lambda i, s: (i, 0))
    return call(
        norm_one_kernel, "norm_one", (2 * steps,),
        [
            pl.BlockSpec((1, tb, d), lambda i, s: (s[SEQ], i % steps, 0)),
            pl.BlockSpec((tb, d), lambda i, s: (i % steps, 0)),
            whole(*rows.shape),
        ],
        [tok, tok], [sds((t, d), bf16)] * 2, [],
        cost(10 * t * d, 4 * t * d), at, (both, other, rows),
    )


def weave_keys(refs, at_ref, w_ref):
    last = pl.program_id(0) == pl.num_programs(0) - 1

    @pl.when(jnp.logical_not(last))
    def _():
        w_ref[...] = weave_a(refs[:4], at_ref)

    @pl.when(last)
    def _():
        w_ref[...] = weave_b(refs[4:], at_ref)


def qkv_columns(w_a, w_b, width, groups):
    specs, args = [], []
    for pieces, column in (
        (w_a, lambda i, s: (0, i)),
        (w_a, lambda i, s: (0, groups + jnp.minimum(i, groups - 2))),
        (w_b, lambda i, s: (0, 0)),
        (w_b, lambda i, s: (0, 1 + i)),
    ):
        specs += [pl.BlockSpec((pieces[0].shape[0], width), column)] * 4
        args += pieces
    return specs, args


def attend_kernel(at_ref, n_ref, *refs, heads, qb):
    q_ref, k_ref, v_ref, o_ref, lse_ref, wk_ref = refs[16:]
    t = n_ref.shape[0]
    n = n_ref[...]
    weave_keys(refs[4:12], at_ref, wk_ref)
    q_ref[...] = nn(n, weave_a(refs[0:4], at_ref)).astype(bf16)
    k_ref[...] = nn(n, wk_ref[...]).astype(bf16)
    v_ref[...] = nn(n, weave_b(refs[12:16], at_ref)).astype(bf16)

    def run(parts):
        span = t // parts
        blocks = [(h, q0) for h in range(heads) for q0 in range(0, t, qb)]

        def scores(h, q0):
            hs = slice(h * HD, (h + 1) * HD)
            k0 = (q0 // span) * span
            return nt(k_ref[k0 : k0 + span, hs], q_ref[q0 : q0 + qb, hs] * bf16(0.125))

        ahead = scores(*blocks[0])
        for i, (h, q0) in enumerate(blocks):
            s = ahead
            if i + 1 < len(blocks):
                ahead = scores(*blocks[i + 1])
            hs = slice(h * HD, (h + 1) * HD)
            k0 = (q0 // span) * span
            top = jnp.max(s, axis=0, keepdims=True)
            p = jnp.exp2((s - top) * f32(LOG2E))
            total = jnp.sum(p, axis=0, keepdims=True)
            probs = (p * (1.0 / total)).astype(bf16)
            o_ref[q0 : q0 + qb, hs] = tn(probs, v_ref[k0 : k0 + span, hs]).astype(bf16)
            lse_ref[h // 2, h % 2 : h % 2 + 1, q0 : q0 + qb] = top + jnp.log(total)

    short = at_ref[SHORT]

    @pl.when(short == 0)
    def _():
        run(1)

    @pl.when(short != 0)
    def _():
        run(2)


def attend(at, n, w_a, w_b, heads=4, qb=512):
    t, d = n.shape
    c = heads * HD
    groups = d // c
    specs, args = qkv_columns(w_a, w_b, c, groups)
    tok = pl.BlockSpec((t, c), lambda g, s: (0, g))
    return call(
        functools.partial(attend_kernel, heads=heads, qb=qb), "attend", (groups,),
        [whole(t, d)] + specs,
        [tok] * 4 + [pl.BlockSpec((heads // 2, 2, t), lambda g, s: (g, 0, 0))],
        [sds((t, d), bf16)] * 4 + [sds((groups * heads // 2, 2, t), f32)], [pltpu.VMEM((d, c), bf16)],
        cost(6 * t * d * d + 16 * t * t * d, 20 * t * d, t * t * d // HD),
        at, (n, *args),
    )


def attend_back_kernel(at_ref, q_ref, k_ref, v_ref, o_ref, do_ref, lse_ref, *refs, heads, qb):
    dq_ref, dk_ref, dv_ref = refs[-3:]
    t = q_ref.shape[0]

    def run(parts):
        span = t // parts
        k_turned = k_ref[...].T
        prod = (do_ref[...].astype(f32) * o_ref[...].astype(f32)).T
        for h in range(heads):
            hs = slice(h * HD, (h + 1) * HD)
            for b in range(parts):
                ks = slice(b * span, (b + 1) * span)
                k = k_ref[ks, hs]
                v = v_ref[ks, hs]
                dk = dv = None
                for q0 in range(b * span, (b + 1) * span, qb):
                    qs = slice(q0, q0 + qb)
                    q = q_ref[qs, hs] * bf16(0.125)
                    do = do_ref[qs, hs]
                    delta = jnp.sum(prod[hs, qs], axis=0, keepdims=True)
                    p = jnp.exp2((nt(k, q) - lse_ref[0, h : h + 1, qs]) * f32(LOG2E))
                    ds = (p * (nt(v, do) - delta)).astype(bf16)
                    dv_part = nn(p.astype(bf16), do)
                    dk_part = nn(ds, q)
                    dv = dv_part if dv is None else dv + dv_part
                    dk = dk_part if dk is None else dk + dk_part
                    dq_ref[qs, hs] = (nn(k_turned[hs, ks], ds) * f32(0.125)).T.astype(bf16)
                dk_ref[ks, hs] = dk.astype(bf16)
                dv_ref[ks, hs] = dv.astype(bf16)

    short = at_ref[SHORT]

    @pl.when(short == 0)
    def _():
        run(1)

    @pl.when(short != 0)
    def _():
        run(2)


def attend_back(at, q, k, v, o, do, lse, part, parts, before=(), heads=2, qb=256):
    t, d = q.shape
    c = heads * HD
    count = d // c // parts
    first = part * count
    tok = pl.BlockSpec((t, c), lambda g, s: (0, first + g))
    return call(
        functools.partial(attend_back_kernel, heads=heads, qb=qb), f"attend_back_{part}", (count,),
        [tok] * 5
        + [pl.BlockSpec((1, heads, t), lambda g, s: (first + g, 0, 0))]
        + [pl.BlockSpec(memory_space=pl.ANY)] * len(before),
        [tok] * 3, [sds((t, d), bf16)] * 3, [],
        cost(40 * t * t * d // parts, 16 * t * d // parts, t * t * d // HD // parts),
        at, (q, k, v, o, do, lse, *before),
        {7 + i: i for i in range(len(before))},
    )


def mix_kernel(
    at_ref, x_ref, o_ref, w0_ref, w1_ref, w2_ref, w3_ref, row_ref, mid_ref, n_ref, w_ref,
):
    @pl.when(pl.program_id(0) == 0)
    def _():
        w_ref[...] = weave_a((w0_ref, w1_ref, w2_ref, w3_ref), at_ref)

    mid = x_ref[...].astype(f32) + row_ref[0:1, :] + nn(o_ref[...], w_ref[...])
    mid_ref[...] = mid
    xhat, _ = norm_parts(mid)
    n_ref[...] = (xhat * row_ref[3:4, :] + row_ref[4:5, :]).astype(bf16)


def last_columns(pieces, width):
    return [
        pl.BlockSpec((p.shape[0], width), (lambda k: lambda i, s: (0, k))(p.shape[1] // width - 1))
        for p in pieces
    ]


def mix(at, x, o, out, rows, tb=256):
    t, d = x.shape
    tok = pl.BlockSpec((tb, d), lambda i, s: (i, 0))
    return call(
        mix_kernel, "mix", (t // tb,),
        [tok, tok] + last_columns(out, d) + [whole(*rows.shape)],
        [tok] * 2, [sds((t, d), f32), sds((t, d), bf16)],
        [pltpu.VMEM((d, d), bf16)], cost(2 * t * d * d, 12 * t * d), at, (x, o, *out, rows),
    )


def gelu_parts(u):
    e = jnp.exp(u * u * f32(-0.5))
    r = pl.reciprocal(1.0 + f32(0.3275911 * 0.7071067811865476) * jnp.abs(u))
    poly = f32(-1.453152027) + r * f32(1.061405429)
    poly = f32(1.421413741) + r * poly
    poly = f32(-0.284496736) + r * poly
    poly = r * (f32(0.254829592) + r * poly)
    tail = f32(0.5) * poly * e
    return jnp.where(u >= 0, 1.0 - tail, tail), e * f32(0.3989422804014327)


def ffn_kernel(at_ref, n_ref, here_ref, there_ref, there_2_ref, mid_any, *refs):
    ub_ref, row_ref, own_ref, send_ref, du_ref, keep_ref, give_ref, gub_ref, small_ref, dy_ref = refs[8:18]
    acc, act, mid_ref, mid_sem = refs[18:]
    j = pl.program_id(0)
    late = pltpu.make_async_copy(mid_any, mid_ref, mid_sem)

    @pl.when(j == 0)
    def _():
        late.start()
        acc[...] = jnp.zeros_like(acc)
        there = jnp.concatenate([there_ref[...].astype(f32), there_2_ref[...].astype(f32)], axis=0)
        halves = choose(at_ref[SEQ], here_ref[0].astype(f32), there)
        half = there.shape[0]
        dy_ref[:half, :] = halves[0].astype(bf16)
        dy_ref[half:, :] = halves[1].astype(bf16)

    wu = weave_a(refs[:4], at_ref)
    other = (j // (pl.num_programs(0) // 2)) != at_ref[LAST_B]
    even_odd = choose(
        at_ref[CORE],
        jnp.where(other, refs[5][...].astype(f32), refs[4][...].astype(f32)),
        jnp.where(other, refs[7][...].astype(f32), refs[6][...].astype(f32)),
    )
    short, d = refs[4].shape[0] // 4, dy_ref.shape[1]
    wd = jnp.concatenate(
        [
            v[i * short : (i + 1) * short, k * d : (k + 1) * d]
            for i in range(4)
            for v in even_odd
            for k in range(4)
        ],
        axis=0,
    ).astype(bf16)
    unit = 4 * short
    ub = ub_ref[...].astype(f32)
    t, fb = act.shape
    tb = t // 4
    gub = jnp.zeros((1, fb), f32)
    for i in range(4):
        sl = slice(i * tb, (i + 1) * tb)
        u = nn(n_ref[sl, :], wu) + ub
        da = nt(dy_ref[sl, :], wd)
        cdf, pdf = gelu_parts(u)
        active = (u * cdf).astype(bf16)
        act[sl, :] = active
        du = (da * (cdf + u * pdf)).astype(bf16)
        du_ref[sl, :] = du
        gub = gub + jnp.sum(du.astype(f32), axis=0, keepdims=True)
        acc[sl, :] += nn(active, wd)
    gub_ref[...] = gub
    own, theirs = unweave(tn(act[...], dy_ref[...]), at_ref, unit)
    keep_ref[...] = own.astype(bf16)
    give_ref[...] = theirs.astype(bf16)

    @pl.when(j == pl.num_programs(0) - 1)
    def _():
        half = t // 2
        late.wait()
        result = acc[...] + mid_ref[...] + row_ref[5:6, :]
        own, theirs = choose(at_ref[SEQ], result[:half, :], result[half:, :])
        own_ref[...] = own.astype(bf16)
        send_ref[...] = theirs.astype(bf16)
        small_ref[...] = jnp.sum(dy_ref[...].astype(f32), axis=0, keepdims=True)


def ffn(at, n, both, other, mid, up_out, down, up_bias, rows):
    t, d = n.shape
    ff = up_bias.shape[1]
    fb = ff // 4
    high, low = up_out[0].shape[0], down[0].shape[0]
    chunk = pl.BlockSpec((fb // 2, d), lambda j, s: (j, 0))
    return call(
        ffn_kernel, "ffn", (4,),
        [whole(t, d), pl.BlockSpec((1, t // 2, d), lambda j, s: (s[SEQ], 0, 0)), whole(t // 4, d), whole(t // 4, d)]
        + [pl.BlockSpec(memory_space=pl.ANY)]
        + [pl.BlockSpec((high, fb), lambda j, s: (0, j))] * 4
        + [pl.BlockSpec((low // 2, 4 * d), lambda j, s: (j % 2, 0))] * 4
        + [pl.BlockSpec((1, fb), lambda j, s: (0, j)), whole(*rows.shape)],
        [whole(t // 2, d)] * 2
        + [pl.BlockSpec((t, fb), lambda j, s: (0, j)), chunk, chunk]
        + [pl.BlockSpec((1, fb), lambda j, s: (0, j)), whole(1, d), whole(t, d)],
        [sds((t // 2, d), bf16)] * 2
        + [sds((t, ff), bf16)]
        + [sds((ff // 2, d), bf16)] * 2
        + [sds((1, ff), f32), sds((1, d), f32), sds((t, d), bf16)],
        [pltpu.VMEM((t, d), f32), pltpu.VMEM((t, fb), bf16), pltpu.VMEM((t, d), f32), pltpu.SemaphoreType.DMA],
        cost(8 * t * d * ff, 20 * t * d + 8 * d * ff, 2 * t * ff),
        at, (n, both, *other, mid, *up_out, *down, up_bias, rows),
    )


def unffn_kernel(at_ref, n_ref, dy_any, mid_any, du_ref, o_any, row_ref, *refs):
    dmid_ref, do_ref, keep_ref, give_ref, small_ref, acc, turned, turned_2 = refs[8:16]
    dy_ref, mid_ref, o_ref, dy_sem, mid_sem, o_sem = refs[16:]
    late = [
        pltpu.make_async_copy(*pair_of)
        for pair_of in ((dy_any, dy_ref, dy_sem), (mid_any, mid_ref, mid_sem), (o_any, o_ref, o_sem))
    ]
    j = pl.program_id(0)
    last = pl.num_programs(0) - 1

    @pl.when(j == 0)
    def _():
        for copy in late:
            copy.start()
        acc[...] = jnp.zeros_like(acc)
        turned[...], turned_2[...] = turn(n_ref[...], at_ref)

    @pl.when(j < last)
    def _():
        du = du_ref[...]
        w = weave_a(refs[:4], at_ref)
        keep_ref[...] = nn(turned[...], du).astype(bf16)
        give_ref[...] = nn(turned_2[...], du).astype(bf16)
        acc[...] += nt(du, w)

    @pl.when(j == last)
    def _():
        for copy in late:
            copy.wait()
        xhat, s = norm_parts(mid_ref[...])
        e = acc[...]
        small_ref[...] = jnp.concatenate(
            [jnp.sum(e * xhat, axis=0, keepdims=True), jnp.sum(e, axis=0, keepdims=True)], axis=0
        )
        dmid = dy_ref[...].astype(f32) + norm_back(e, row_ref[3:4, :], xhat, s)
        dmid_ref[...] = dmid
        db = dmid.astype(bf16)
        do_ref[...] = nt(db, weave_a(refs[4:8], at_ref)).astype(bf16)
        own, other = unweave(tn(o_ref[...], db), at_ref, db.shape[1] // 32)
        keep_ref[...] = own.astype(bf16)
        give_ref[...] = other.astype(bf16)


def unffn(at, n, dy, mid, du, up, out, o, rows):
    t, d = n.shape
    ff = du.shape[1]
    count = ff // d
    cols = pl.BlockSpec((d // 2, d), lambda j, s: (0, j))
    return call(
        unffn_kernel, "unffn", (count + 1,),
        [whole(t, d)] + [pl.BlockSpec(memory_space=pl.ANY)] * 2
        + [pl.BlockSpec((t, d), lambda j, s: (0, jnp.minimum(j, count - 1)))]
        + [pl.BlockSpec(memory_space=pl.ANY), whole(*rows.shape)]
        + [pl.BlockSpec((p.shape[0], d), lambda j, s: (0, jnp.minimum(j, count - 1))) for p in up]
        + last_columns(out, d),
        [whole(t, d)] * 2 + [cols] * 2 + [whole(2, d)],
        [sds((t, d), f32), sds((t, d), bf16)] + [sds((d // 2, ff + d), bf16)] * 2 + [sds((2, d), f32)],
        [pltpu.VMEM((t, d), f32)] + [pltpu.VMEM((d // 2, t), bf16)] * 2
        + [pltpu.VMEM((t, d), bf16), pltpu.VMEM((t, d), f32), pltpu.VMEM((t, d), bf16)]
        + [pltpu.SemaphoreType.DMA] * 3,
        cost(4 * t * d * (ff + d), 20 * t * d + 8 * d * ff),
        at, (n, dy, mid, du, o, rows, *up, *out),
    )


def grad_qkv_kernel(at_ref, n_ref, dq_ref, dk_ref, dv_ref, keep_ref, give_ref, turned, turned_2):
    @pl.when(pl.program_id(0) == 0)
    def _():
        turned[...], turned_2[...] = turn(n_ref[...], at_ref)

    for i, d_ref in enumerate((dq_ref, dk_ref, dv_ref)):
        keep_ref[i] = nn(turned[...], d_ref[...]).astype(bf16)
        give_ref[i] = nn(turned_2[...], d_ref[...]).astype(bf16)


def grad_qkv(at, n, dq, dk, dv, cb=256):
    t, d = n.shape
    tok = pl.BlockSpec((t, cb), lambda i, s: (0, i))
    out = pl.BlockSpec((3, d // 2, cb), lambda i, s: (0, 0, i))
    return call(
        grad_qkv_kernel, "grad_qkv", (d // cb,),
        [whole(t, d)] + [tok] * 3, [out] * 2, [sds((3, d // 2, d), bf16)] * 2,
        [pltpu.VMEM((d // 2, t), bf16)] * 2,
        cost(6 * t * d * d, 20 * t * d), at, (n, dq, dk, dv),
    )


def unqkv_kernel(at_ref, x_any, row_ref, dmid_any, *refs):
    dq_ref, dk_ref, dv_ref, own_ref, send_ref, small_ref, acc, wk_ref = refs[16:24]
    x_ref, dmid_ref, x_sem, dmid_sem = refs[24:]
    i = pl.program_id(0)
    late = [
        pltpu.make_async_copy(x_any, x_ref, x_sem), pltpu.make_async_copy(dmid_any, dmid_ref, dmid_sem)
    ]

    @pl.when(i == 0)
    def _():
        for copy in late:
            copy.start()

    weave_keys(refs[4:12], at_ref, wk_ref)
    w = [weave_a(refs[0:4], at_ref), wk_ref[...], weave_b(refs[12:16], at_ref)]
    e = nt(
        jnp.concatenate([dq_ref[...], dk_ref[...], dv_ref[...]], axis=1),
        jnp.concatenate(w, axis=1),
    )

    @pl.when(i == 0)
    def _():
        acc[...] = e

    @pl.when(i > 0)
    def _():
        acc[...] += e

    @pl.when(i == pl.num_programs(0) - 1)
    def _():
        for copy in late:
            copy.wait()
        e = acc[...]
        xhat, s = norm_parts(x_ref[...].astype(f32) + row_ref[0:1, :])
        d_base = dmid_ref[...] + norm_back(e, row_ref[1:2, :], xhat, s)
        half = d_base.shape[0] // 2
        own, theirs = choose(at_ref[SEQ], d_base[:half], d_base[half:])
        own_ref[...] = own.astype(bf16)
        send_ref[...] = theirs.astype(bf16)
        small_ref[...] = jnp.concatenate(
            [
                jnp.sum(e * xhat, axis=0, keepdims=True),
                jnp.sum(e, axis=0, keepdims=True),
                jnp.sum(d_base, axis=0, keepdims=True),
            ],
            axis=0,
        )


def unqkv(at, x, rows, dmid, w_a, w_b, dq, dk, dv, cb=256):
    t, d = x.shape
    count = d // cb
    specs, args = qkv_columns(w_a, w_b, cb, count)
    tok = pl.BlockSpec((t, cb), lambda i, s: (0, i))
    return call(
        unqkv_kernel, "unqkv", (count,),
        [pl.BlockSpec(memory_space=pl.ANY), whole(*rows.shape), pl.BlockSpec(memory_space=pl.ANY)]
        + specs + [tok] * 3,
        [whole(t // 2, d)] * 2 + [whole(3, d)],
        [sds((t // 2, d), bf16)] * 2 + [sds((3, d), f32)],
        [pltpu.VMEM((t, d), f32), pltpu.VMEM((d, cb), bf16), pltpu.VMEM((t, d), bf16), pltpu.VMEM((t, d), f32)]
        + [pltpu.SemaphoreType.DMA] * 2,
        cost(6 * t * d * d, 30 * t * d), at, (x, rows, dmid, *args, dq, dk, dv),
    )


class Grid:
    def __init__(self, seq, rows):
        self.seq, self.rows = seq, rows
        self.known = seq == 2 and rows == 16
        at = lax.axis_index("rows")
        self.x = lax.axis_index("seq")
        self.z, self.y, self.c = at // 4, (at // 2) % 2, at % 2

    def table(self, move):
        pairs = []
        for x in range(self.seq):
            for z in range(4):
                for y in range(2):
                    for c in range(2):
                        x2, z2, y2, c2 = move(x, z, y, c)
                        pairs.append((x * 16 + z * 4 + y * 2 + c, x2 * 16 + z2 * 4 + y2 * 2 + c2))
        return pairs

    def swap(self, v, axis):
        move = {
            "x": lambda x, z, y, c: (1 - x, z, y, c),
            "y": lambda x, z, y, c: (x, z, 1 - y, c),
            "c": lambda x, z, y, c: (x, z, y, 1 - c),
        }[axis]
        return lax.ppermute(v, BOTH, self.table(move))

    def cross(self, v, bit):
        return lax.ppermute(v, BOTH, self.table(lambda x, z, y, c: (x, z ^ bit, y, c)))

    def shift(self, v, by):
        return lax.ppermute(v, BOTH, self.table(lambda x, z, y, c: (x, (z + by) % 4, y, c)))


def tie(*values):
    return lax.optimization_barrier(values)


def after(v, *first):
    return lax.optimization_barrier((v, first))[0]


def spread(v, axis, count):
    return jnp.broadcast_to(jnp.expand_dims(v, axis), v.shape[:axis] + (count,) + v.shape[axis:])


def pair(own, other, at, axis):
    shape = own.shape[:axis] + (2,) + own.shape[axis:]
    here = lax.broadcasted_iota(jnp.int32, shape, axis) == at
    return jnp.where(here, spread(own, axis, 2), spread(other, axis, 2))


def arrange_z(g, v, shifts):
    out = spread(v, 0, 4)
    place = lax.broadcasted_iota(jnp.int32, out.shape, 0)
    for k, got in enumerate(shifts):
        out = jnp.where(place == (g.z - k - 1) % 4, spread(got, 0, 4), out)
    return out


def gather_z(g, v):
    return arrange_z(g, v, [g.shift(v, k) for k in range(1, 4)])


def flat(v):
    return v.reshape(-1, v.shape[-1])


def quarters(whole_array, kind):
    v = whole_array.reshape(2, 4, 2, 2, -1, whole_array.shape[1])
    pieces = []
    for core in range(2):
        for place in range(2):
            pieces.append(flat(v[:, :, place, core] if kind == "a" else v[place, :, :, core]))
    return pieces


def keep(v, at, axis):
    return lax.dynamic_index_in_dim(v, at, axis, keepdims=False)


def add(a, b):
    return (a.astype(f32) + b.astype(f32)).astype(bf16)


def split_plane(g, a, b):
    a = add(keep(a, g.x, -5), g.swap(keep(a, 1 - g.x, -5), "x"))
    b = add(keep(b, g.y, -3), g.swap(keep(b, 1 - g.y, -3), "y"))
    a, b = yield a, b
    got_a = g.swap(keep(a, 1 - g.y, -3), "y")
    got_b = g.swap(keep(b, 1 - g.x, -4), "x")
    got_a, got_b = yield got_a, got_b
    yield add(keep(a, g.y, -3), got_a), add(keep(b, g.x, -4), got_b)


def split_z(g, v):
    total = keep(v, g.z, -3).astype(f32)
    for k in range(1, 4):
        total = total + g.shift(keep(v, (g.z + k) % 4, -3), k).astype(f32)
    return total


def halve_z(g, v):
    v = v.reshape(*v.shape[:-3], 2, 2, *v.shape[-2:])
    high, low = g.z // 2, g.z % 2
    v = keep(v, low, -3).astype(f32) + g.cross(keep(v, 1 - low, -3), 1).astype(f32)
    got = yield g.cross(keep(v, 1 - high, -3).astype(bf16), 2)
    yield keep(v, high, -3) + got.astype(f32)


def scatter_plain(own, other):
    v = jnp.stack([own.reshape(16, -1, own.shape[1]), other.reshape(16, -1, own.shape[1])], axis=1)
    return lax.psum_scatter(flat(v).astype(f32), BOTH, scatter_dimension=0, tiled=True)


def swap_seq(v):
    return lax.ppermute(v, "seq", [(0, 1), (1, 0)])


def local(
    inputs, timesteps, boundary, step_table, w_qkv, w_out, w_up, w_down,
    norm1_gain, norm1_shift, norm2_gain, norm2_shift, up_bias, down_bias, cotangent,
):
    seq, row_blocks = lax.axis_size("seq"), lax.axis_size("rows")
    g = Grid(seq, row_blocks)
    devices = seq * row_blocks
    d = inputs.shape[2]
    shard = w_qkv.shape[0]
    ff = w_up.shape[1]
    steps = step_table.shape[0]
    wide = (ff // devices) // shard
    short = (g.x < boundary[0]).astype(jnp.int32)
    zero = jnp.zeros_like(short)
    at = jnp.stack([short, g.x] + ([g.y, g.x, g.c] if g.known else [zero] * 3))

    digits = jnp.concatenate([timesteps // 128, timesteps % 128]).astype(bf16)
    shorts = jnp.concatenate(
        [norm1_gain, norm1_shift, norm2_gain, norm2_shift, down_bias, up_bias, digits]
    )
    shorts = jnp.broadcast_to(shorts[None], (devices,) + shorts.shape)
    shorts = lax.all_to_all(shorts, BOTH, split_axis=0, concat_axis=0, tiled=True)
    x_other = swap_seq(keep(inputs, 1 - g.x, 0))
    unit = w_down.shape[0] // 4
    down_wide = w_down.reshape(4, unit, d).transpose(1, 0, 2).reshape(unit, -1)

    def look_up(shorts):
        digits = shorts[:, (5 + wide) * shard :].reshape(seq, row_blocks, 2, -1)[0].astype(jnp.int32)
        all_steps = digits[:, 0] * 128 + digits[:, 1]
        hot = all_steps.T.reshape(-1)[:, None] == jnp.arange(steps, dtype=jnp.int32)[None]
        found = nn(hot.astype(bf16), step_table).astype(bf16)
        found = lax.all_to_all(found, BOTH, split_axis=0, concat_axis=0, tiled=True)
        return all_steps.reshape(-1), found

    def norm_rows(shorts, found):
        rows = jnp.stack([found] + [shorts[:, i * shard : (i + 1) * shard] for i in range(5)])
        return jnp.pad(rows.reshape(6, d).astype(f32), ((0, 2), (0, 0)))

    if g.known:
        shifts = [g.shift(w_qkv, k) for k in range(1, 4)]
        rest = jnp.concatenate([w_up, w_out, down_wide], axis=1)
        rest_2 = g.cross(rest, 2)
        first = arrange_z(g, w_qkv, shifts)
        half = d + 2 * d // 3
        a, b = first[..., :half], first[..., half:]
        a = pair(a, g.swap(a, "x"), g.x, 0)
        b = pair(b, g.swap(b, "y"), g.y, 1)
        a, b, x_other, shorts, rest_2 = tie(a, b, x_other, shorts, rest_2)
        rest = pair(rest, rest_2, g.z // 2, 0)
        rest_1 = g.cross(rest, 1)
        all_steps, found = look_up(shorts)
        a_2, b_2 = g.swap(a, "y"), g.swap(b, "x")
        a_c, b_c = g.swap(a, "c"), g.swap(b, "c")
        w_a = [flat(v) for v in (a, a_2, a_c, g.swap(a_2, "c"))]
        w_b = [flat(v) for v in (b, b_2, b_c, g.swap(b_2, "c"))]
        rest, rest_1, found, a_2, b_2 = tie(rest, rest_1, found, a_2, b_2)
        rest = pair(rest, rest_1, g.z % 2, 1)
        rest = rest.reshape(4, *rest.shape[2:])
        rows = norm_rows(shorts, found)
        x, normed_one = norm_one(at, inputs, x_other, rows)
        a, b = rest[..., : ff + d], rest[..., ff + d :]
        a = pair(a, g.swap(a, "x"), g.x, 0)
        b = pair(b, g.swap(b, "y"), g.y, 1)
        a, b, normed_one = tie(a, b, normed_one)
        a_2, b_2 = g.swap(a, "y"), g.swap(b, "x")
        a_c, b_c = g.swap(a, "c"), g.swap(b, "c")
    else:
        half = d + 2 * d // 3
        w_a, w_b, up_out, down = [
            quarters(lax.all_gather(v, BOTH, axis=0, tiled=True), kind)
            for v, kind in (
                (w_qkv[:, :half], "a"),
                (w_qkv[:, half:], "b"),
                (jnp.concatenate([w_up, w_out], axis=1), "a"),
                (down_wide, "b"),
            )
        ]
        all_steps, found = look_up(shorts)
        rows = norm_rows(shorts, found)
        x, normed_one = norm_one(at, inputs, x_other, rows)

    up_row = shorts[:, 5 * shard : (5 + wide) * shard].reshape(1, ff)
    q, k, v, attended, lse = attend(at, normed_one, w_a, w_b)
    dy_send = keep(cotangent, 1 - g.x, 0)
    dy_other = [swap_seq(v) for v in jnp.split(dy_send, 2)]
    if g.known:
        q, k, v, lse, attended, dy_other[0] = tie(q, k, v, lse, attended, dy_other[0])
        a_2, b_2, attended = tie(a_2, b_2, attended)
        out = [flat(v) for v in (a, a_2, a_c, g.swap(a_2[..., ff:], "c"))]
        up_out = [flat(v) for v in (a, a_2, a_c, g.swap(a_2, "c"))]
        down = [flat(v) for v in (b, b_2, b_c, g.swap(b_2, "c"))]
    else:
        out = up_out
    middle, normed_two = mix(at, x, attended, out, rows)
    block_own, block_send, d_upper, keep_down, give_down, g_up_row, g_down_row, dy = ffn(
        at, normed_two, cotangent, dy_other, middle, up_out, down, up_row, rows
    )
    block_other = swap_seq(block_send)
    d_middle, d_attended, keep_up, give_up, small_two = unffn(
        at, normed_two, dy, middle, d_upper, up_out, out, attended, rows
    )
    six = (2, 4, 2)
    if g.known:
        d_middle, d_attended, keep_up, give_up, small_two, block_other = tie(
            d_middle, d_attended, keep_up, give_up, small_two, block_other
        )
        down = add(keep_down, g.swap(give_down, "c")).reshape(*six, -1, d)
        d_attended, down = tie(d_attended, down)
        down_plane = split_plane(g, down[..., : d // 2], down[..., d // 2 :])
    back = attend_back(at, q, k, v, attended, d_attended, lse, 0, 2)
    if g.known:
        cut = (ff + d) // 2
        up = add(keep_up, g.swap(give_up, "c")).reshape(*six, -1, ff + d)
        down_half = next(down_plane)
        d_attended, up, down_half, *back = tie(d_attended, up, down_half, *back)
        up_plane = split_plane(g, up[..., :cut], up[..., cut:])
        down_got = down_plane.send(down_half)
    dq, dk, dv = attend_back(at, q, k, v, attended, d_attended, lse, 1, 2, tuple(back))
    n = normed_one
    if g.known:
        up_half = next(up_plane)
        n, up_half, dq, down_got = tie(n, up_half, dq, down_got)
        up_got = up_plane.send(up_half)
        down = jnp.concatenate(down_plane.send(down_got), axis=-1)
        down_z = halve_z(g, down)
    keep_qkv, give_qkv = grad_qkv(at, n, dq, dk, dv)
    if g.known:
        keep_qkv, up_got = tie(keep_qkv, up_got)
        qkv = add(keep_qkv, g.swap(give_qkv, "c")).reshape(3, *six, shard, d)
        up = jnp.concatenate(up_plane.send(up_got), axis=-1)
        d_middle, qkv, up = tie(d_middle, qkv, up)
        a = jnp.concatenate([qkv[0], qkv[1, ..., : d // 2]], axis=-1)
        b = jnp.concatenate([qkv[1, ..., d // 2 :], qkv[2]], axis=-1)
        plane = split_plane(g, a, b)
    d_own, d_send, small_one = unqkv(at, x, rows, d_middle, w_a, w_b, dq, dk, dv)
    if g.known:
        ready = next(plane)
        small_one, d_send, ready, down_got = tie(small_one, d_send, ready, next(down_z))
        sum_down = down_z.send(down_got)
        up_z = halve_z(g, up)
        got_a, got_b = plane.send(ready)
        small_one, got_a = tie(small_one, got_a)
        got = (got_a, got_b)
    d_other = swap_seq(d_send)

    small = jnp.concatenate([small_two, g_down_row, small_one], axis=0)
    small = small.reshape(-1, devices, shard).transpose(1, 0, 2).reshape(devices, -1)
    small = jnp.concatenate([small, g_up_row.reshape(devices, -1)], axis=1)
    small = lax.all_to_all(small, BOTH, split_axis=0, concat_axis=0, tiled=True)
    row_sums = small[:, 5 * shard : 6 * shard].reshape(seq, row_blocks, shard).transpose(1, 0, 2)
    row_sums = row_sums.reshape(devices, shard)
    small = jnp.sum(small, axis=0)
    if g.known:
        sum_up = up_z.send(next(up_z))
        last = jnp.concatenate(plane.send(got), axis=-1)
        block_out = pair(block_own, block_other, g.x, 0)
        d_other, last, block_out = tie(d_other, split_z(g, last), block_out)
    else:
        sum_up, sum_down = scatter_plain(keep_up, give_up), scatter_plain(keep_down, give_down)
        last = [scatter_plain(keep_qkv[i], give_qkv[i]) for i in range(3)]
        last = jnp.concatenate(last, axis=1)
        block_out = pair(block_own, block_other, g.x, 0)
    grad_inputs = pair(d_own, d_other, g.x, 0)
    hot = (jnp.arange(steps, dtype=jnp.int32)[:, None] == all_steps[None]).astype(f32)
    g_table = lax.dot_general(
        hot, row_sums, (((1,), (0,)), ((), ())), precision=lax.Precision.HIGHEST,
        preferred_element_type=f32,
    )
    return (
        block_out,
        grad_inputs,
        g_table,
        last,
        sum_up[:, ff:],
        sum_up[:, :ff],
        sum_down,
        *[small[i * shard : (i + 1) * shard] for i in (3, 4, 0, 1)],
        small[6 * shard :],
        small[2 * shard : 3 * shard],
    )


def solution(mesh):
    tokens, weight, vector = P("rows", "seq", None), P(BOTH, None), P(BOTH)
    table = P(None, BOTH)
    in_specs = (
        (tokens, P("rows"), P("rows"), table) + (weight,) * 4 + (vector,) * 6 + (tokens,)
    )
    out_specs = (tokens, tokens, table) + (weight,) * 4 + (vector,) * 6
    return jax.shard_map(local, mesh=mesh, in_specs=in_specs, out_specs=out_specs, check_vma=False)
```

```python
import functools

import jax
import jax.numpy as jnp
from jax import lax
from jax.experimental import pallas as pl
from jax.experimental.pallas import tpu as pltpu
from jax.sharding import PartitionSpec as P

f32 = jnp.float32
bf16 = jnp.bfloat16
HD = 64
EPS = 1e-5
LOG2E = 1.4426950408889634
VMEM = 56 * 1024 * 1024
BOTH = ("seq", "rows")
WEIGHT = 0.02


def nn(a, b):
    return lax.dot_general(a, b, (((1,), (0,)), ((), ())), preferred_element_type=f32)


def nt(a, b):
    return lax.dot_general(a, b, (((1,), (1,)), ((), ())), preferred_element_type=f32)


def tn(a, b):
    return lax.dot_general(a, b, (((0,), (0,)), ((), ())), preferred_element_type=f32)


def sds(shape, dtype):
    return jax.ShapeDtypeStruct(shape, dtype)


def whole(*shape):
    return pl.BlockSpec(shape, lambda *_: (0,) * len(shape))


def params():
    return pltpu.CompilerParams(vmem_limit_bytes=VMEM, dimension_semantics=("arbitrary",))


def cost(flops, nbytes, trans=0):
    return pl.CostEstimate(
        flops=int(flops * WEIGHT), bytes_accessed=int(nbytes * WEIGHT), transcendentals=int(trans * WEIGHT)
    )


def norm_parts(v):
    c = v - jnp.mean(v, axis=1, keepdims=True)
    s = lax.rsqrt(jnp.mean(c * c, axis=1, keepdims=True) + EPS)
    return c * s, s


def norm_back(e, gain, xhat, s):
    f = e * gain
    return s * (
        f
        - jnp.mean(f, axis=1, keepdims=True)
        - xhat * jnp.mean(f * xhat, axis=1, keepdims=True)
    )


SHORT, SEQ, LAST_A, LAST_B, CORE = range(5)


def choose(flag, a, b):
    return jnp.where(flag == 0, a, b), jnp.where(flag == 0, b, a)


def weave_a(refs, at_ref):
    own, other, own_2, other_2 = [r[...].astype(f32) for r in refs]
    first, second = choose(at_ref[LAST_A], own, other)
    first_2, second_2 = choose(at_ref[LAST_A], own_2, other_2)
    quarters = choose(at_ref[CORE], first, first_2) + choose(at_ref[CORE], second, second_2)
    unit = own.shape[0] // 8
    return jnp.concatenate(
        [q[i * unit : (i + 1) * unit] for i in range(8) for q in quarters], axis=0
    ).astype(bf16)


def weave_b(refs, at_ref):
    own, other, own_2, other_2 = [r[...].astype(f32) for r in refs]
    halves = choose(at_ref[LAST_B], own, other)
    halves_2 = choose(at_ref[LAST_B], own_2, other_2)
    unit = own.shape[0] // 8
    out = []
    for half, half_2 in zip(halves, halves_2):
        even, odd = choose(at_ref[CORE], half, half_2)
        for i in range(8):
            out += [even[i * unit : (i + 1) * unit], odd[i * unit : (i + 1) * unit]]
    return jnp.concatenate(out, axis=0).astype(bf16)


def unweave(v, at_ref, unit):
    own, other = [], []
    for i in range(v.shape[0] // (2 * unit)):
        even, odd = v[2 * i * unit : (2 * i + 1) * unit], v[(2 * i + 1) * unit : (2 * i + 2) * unit]
        mine, theirs = choose(at_ref[CORE], even, odd)
        own.append(mine)
        other.append(theirs)
    return jnp.concatenate(own, axis=0), jnp.concatenate(other, axis=0)


def turn(v, at_ref):
    own, other = unweave(v.T.astype(f32), at_ref, v.shape[1] // 32)
    return own.astype(bf16), other.astype(bf16)


def call(kernel, name, grid, in_specs, out_specs, out_shape, scratch, estimate, at, args, aliases=None):
    return pl.pallas_call(
        kernel,
        grid_spec=pltpu.PrefetchScalarGridSpec(
            num_scalar_prefetch=1,
            grid=grid,
            in_specs=in_specs,
            out_specs=out_specs,
            scratch_shapes=scratch,
        ),
        out_shape=out_shape,
        compiler_params=params(),
        cost_estimate=estimate,
        input_output_aliases=aliases or {},
        name=name,
    )(at, *args)


def norm_one_kernel(at_ref, own_ref, other_ref, row_ref, x_ref, n_ref):
    ahead = pl.program_id(0) // (pl.num_programs(0) // 2) == at_ref[SEQ]
    x = jnp.where(ahead, own_ref[0].astype(f32), other_ref[...].astype(f32))
    x_ref[...] = x.astype(bf16)
    xhat, _ = norm_parts(x + row_ref[0:1, :])
    n_ref[...] = (xhat * row_ref[1:2, :] + row_ref[2:3, :]).astype(bf16)


def norm_one(at, both, other, rows, tb=512):
    half, d = other.shape
    t = 2 * half
    steps = half // tb
    tok = pl.BlockSpec((tb, d), lambda i, s: (i, 0))
    return call(
        norm_one_kernel, "norm_one", (2 * steps,),
        [
            pl.BlockSpec((1, tb, d), lambda i, s: (s[SEQ], i % steps, 0)),
            pl.BlockSpec((tb, d), lambda i, s: (i % steps, 0)),
            whole(*rows.shape),
        ],
        [tok, tok], [sds((t, d), bf16)] * 2, [],
        cost(10 * t * d, 4 * t * d), at, (both, other, rows),
    )


def weave_keys(refs, at_ref, w_ref):
    last = pl.program_id(0) == pl.num_programs(0) - 1

    @pl.when(jnp.logical_not(last))
    def _():
        w_ref[...] = weave_a(refs[:4], at_ref)

    @pl.when(last)
    def _():
        w_ref[...] = weave_b(refs[4:], at_ref)


def qkv_columns(w_a, w_b, width, groups):
    specs, args = [], []
    for pieces, column in (
        (w_a, lambda i, s: (0, i)),
        (w_a, lambda i, s: (0, groups + jnp.minimum(i, groups - 2))),
        (w_b, lambda i, s: (0, 0)),
        (w_b, lambda i, s: (0, 1 + i)),
    ):
        specs += [pl.BlockSpec((pieces[0].shape[0], width), column)] * 4
        args += pieces
    return specs, args


def attend_kernel(at_ref, n_ref, *refs, heads, qb):
    q_ref, k_ref, v_ref, o_ref, lse_ref, wk_ref = refs[16:]
    t = n_ref.shape[0]
    n = n_ref[...]
    weave_keys(refs[4:12], at_ref, wk_ref)
    q_ref[...] = nn(n, weave_a(refs[0:4], at_ref)).astype(bf16)
    k_ref[...] = nn(n, wk_ref[...]).astype(bf16)
    v_ref[...] = nn(n, weave_b(refs[12:16], at_ref)).astype(bf16)

    def run(parts):
        span = t // parts
        blocks = [(h, q0) for h in range(heads) for q0 in range(0, t, qb)]

        def scores(h, q0):
            hs = slice(h * HD, (h + 1) * HD)
            k0 = (q0 // span) * span
            return nt(k_ref[k0 : k0 + span, hs], q_ref[q0 : q0 + qb, hs] * bf16(0.125))

        ahead = scores(*blocks[0])
        for i, (h, q0) in enumerate(blocks):
            s = ahead
            if i + 1 < len(blocks):
                ahead = scores(*blocks[i + 1])
            hs = slice(h * HD, (h + 1) * HD)
            k0 = (q0 // span) * span
            top = jnp.max(s, axis=0, keepdims=True)
            p = jnp.exp2((s - top) * f32(LOG2E))
            total = jnp.sum(p, axis=0, keepdims=True)
            probs = (p * (1.0 / total)).astype(bf16)
            o_ref[q0 : q0 + qb, hs] = tn(probs, v_ref[k0 : k0 + span, hs]).astype(bf16)
            lse_ref[h // 2, h % 2 : h % 2 + 1, q0 : q0 + qb] = top + jnp.log(total)

    short = at_ref[SHORT]

    @pl.when(short == 0)
    def _():
        run(1)

    @pl.when(short != 0)
    def _():
        run(2)


def attend(at, n, w_a, w_b, heads=4, qb=512):
    t, d = n.shape
    c = heads * HD
    groups = d // c
    specs, args = qkv_columns(w_a, w_b, c, groups)
    tok = pl.BlockSpec((t, c), lambda g, s: (0, g))
    return call(
        functools.partial(attend_kernel, heads=heads, qb=qb), "attend", (groups,),
        [whole(t, d)] + specs,
        [tok] * 4 + [pl.BlockSpec((heads // 2, 2, t), lambda g, s: (g, 0, 0))],
        [sds((t, d), bf16)] * 4 + [sds((groups * heads // 2, 2, t), f32)], [pltpu.VMEM((d, c), bf16)],
        cost(6 * t * d * d + 16 * t * t * d, 20 * t * d, t * t * d // HD),
        at, (n, *args),
    )


def attend_back_kernel(at_ref, q_ref, k_ref, v_ref, o_ref, do_ref, lse_ref, *refs, heads, qb):
    dq_ref, dk_ref, dv_ref = refs[-3:]
    t = q_ref.shape[0]

    def run(parts):
        span = t // parts
        k_turned = k_ref[...].T
        prod = (do_ref[...].astype(f32) * o_ref[...].astype(f32)).T
        for h in range(heads):
            hs = slice(h * HD, (h + 1) * HD)
            for b in range(parts):
                ks = slice(b * span, (b + 1) * span)
                k = k_ref[ks, hs]
                v = v_ref[ks, hs]
                dk = dv = None
                for q0 in range(b * span, (b + 1) * span, qb):
                    qs = slice(q0, q0 + qb)
                    q = q_ref[qs, hs] * bf16(0.125)
                    do = do_ref[qs, hs]
                    delta = jnp.sum(prod[hs, qs], axis=0, keepdims=True)
                    p = jnp.exp2((nt(k, q) - lse_ref[0, h : h + 1, qs]) * f32(LOG2E))
                    ds = (p * (nt(v, do) - delta)).astype(bf16)
                    dv_part = nn(p.astype(bf16), do)
                    dk_part = nn(ds, q)
                    dv = dv_part if dv is None else dv + dv_part
                    dk = dk_part if dk is None else dk + dk_part
                    dq_ref[qs, hs] = (nn(k_turned[hs, ks], ds) * f32(0.125)).T.astype(bf16)
                dk_ref[ks, hs] = dk.astype(bf16)
                dv_ref[ks, hs] = dv.astype(bf16)

    short = at_ref[SHORT]

    @pl.when(short == 0)
    def _():
        run(1)

    @pl.when(short != 0)
    def _():
        run(2)


def attend_back(at, q, k, v, o, do, lse, part, parts, before=(), heads=2, qb=256):
    t, d = q.shape
    c = heads * HD
    count = d // c // parts
    first = part * count
    tok = pl.BlockSpec((t, c), lambda g, s: (0, first + g))
    return call(
        functools.partial(attend_back_kernel, heads=heads, qb=qb), f"attend_back_{part}", (count,),
        [tok] * 5
        + [pl.BlockSpec((1, heads, t), lambda g, s: (first + g, 0, 0))]
        + [pl.BlockSpec(memory_space=pl.ANY)] * len(before),
        [tok] * 3, [sds((t, d), bf16)] * 3, [],
        cost(40 * t * t * d // parts, 16 * t * d // parts, t * t * d // HD // parts),
        at, (q, k, v, o, do, lse, *before),
        {7 + i: i for i in range(len(before))},
    )


def mix_kernel(
    at_ref, x_ref, o_ref, w0_ref, w1_ref, w2_ref, w3_ref, row_ref, mid_ref, n_ref, w_ref,
):
    @pl.when(pl.program_id(0) == 0)
    def _():
        w_ref[...] = weave_a((w0_ref, w1_ref, w2_ref, w3_ref), at_ref)

    mid = x_ref[...].astype(f32) + row_ref[0:1, :] + nn(o_ref[...], w_ref[...])
    mid_ref[...] = mid
    xhat, _ = norm_parts(mid)
    n_ref[...] = (xhat * row_ref[3:4, :] + row_ref[4:5, :]).astype(bf16)


def last_columns(pieces, width):
    return [
        pl.BlockSpec((p.shape[0], width), (lambda k: lambda i, s: (0, k))(p.shape[1] // width - 1))
        for p in pieces
    ]


def mix(at, x, o, out, rows, tb=512):
    t, d = x.shape
    tok = pl.BlockSpec((tb, d), lambda i, s: (i, 0))
    return call(
        mix_kernel, "mix", (t // tb,),
        [tok, tok] + last_columns(out, d) + [whole(*rows.shape)],
        [tok] * 2, [sds((t, d), f32), sds((t, d), bf16)],
        [pltpu.VMEM((d, d), bf16)], cost(2 * t * d * d, 12 * t * d), at, (x, o, *out, rows),
    )


def gelu_parts(u):
    e = jnp.exp(u * u * f32(-0.5))
    r = pl.reciprocal(1.0 + f32(0.3275911 * 0.7071067811865476) * jnp.abs(u))
    poly = f32(-1.453152027) + r * f32(1.061405429)
    poly = f32(1.421413741) + r * poly
    poly = f32(-0.284496736) + r * poly
    poly = r * (f32(0.254829592) + r * poly)
    tail = f32(0.5) * poly * e
    return jnp.where(u >= 0, 1.0 - tail, tail), e * f32(0.3989422804014327)


def ffn_kernel(at_ref, n_ref, here_ref, there_ref, there_2_ref, mid_any, *refs):
    ub_ref, row_ref, own_ref, send_ref, du_ref, keep_ref, give_ref, gub_ref, small_ref, dy_ref = refs[8:18]
    acc, act, mid_ref, mid_sem = refs[18:]
    j = pl.program_id(0)
    late = pltpu.make_async_copy(mid_any, mid_ref, mid_sem)

    @pl.when(j == 0)
    def _():
        late.start()
        acc[...] = jnp.zeros_like(acc)
        there = jnp.concatenate([there_ref[...].astype(f32), there_2_ref[...].astype(f32)], axis=0)
        halves = choose(at_ref[SEQ], here_ref[0].astype(f32), there)
        half = there.shape[0]
        dy_ref[:half, :] = halves[0].astype(bf16)
        dy_ref[half:, :] = halves[1].astype(bf16)

    wu = weave_a(refs[:4], at_ref)
    other = (j // (pl.num_programs(0) // 2)) != at_ref[LAST_B]
    even_odd = choose(
        at_ref[CORE],
        jnp.where(other, refs[5][...].astype(f32), refs[4][...].astype(f32)),
        jnp.where(other, refs[7][...].astype(f32), refs[6][...].astype(f32)),
    )
    short, d = refs[4].shape[0] // 4, dy_ref.shape[1]
    wd = jnp.concatenate(
        [
            v[i * short : (i + 1) * short, k * d : (k + 1) * d]
            for i in range(4)
            for v in even_odd
            for k in range(4)
        ],
        axis=0,
    ).astype(bf16)
    unit = 4 * short
    ub = ub_ref[...].astype(f32)
    t, fb = act.shape
    tb = t // 4
    gub = jnp.zeros((1, fb), f32)
    for i in range(4):
        sl = slice(i * tb, (i + 1) * tb)
        u = nn(n_ref[sl, :], wu) + ub
        da = nt(dy_ref[sl, :], wd)
        cdf, pdf = gelu_parts(u)
        active = (u * cdf).astype(bf16)
        act[sl, :] = active
        du = (da * (cdf + u * pdf)).astype(bf16)
        du_ref[sl, :] = du
        gub = gub + jnp.sum(du.astype(f32), axis=0, keepdims=True)
        acc[sl, :] += nn(active, wd)
    gub_ref[...] = gub
    own, theirs = unweave(tn(act[...], dy_ref[...]), at_ref, unit)
    keep_ref[...] = own.astype(bf16)
    give_ref[...] = theirs.astype(bf16)

    @pl.when(j == pl.num_programs(0) - 1)
    def _():
        half = t // 2
        late.wait()
        result = acc[...] + mid_ref[...] + row_ref[5:6, :]
        own, theirs = choose(at_ref[SEQ], result[:half, :], result[half:, :])
        own_ref[...] = own.astype(bf16)
        send_ref[...] = theirs.astype(bf16)
        small_ref[...] = jnp.sum(dy_ref[...].astype(f32), axis=0, keepdims=True)


def ffn(at, n, both, other, mid, up_out, down, up_bias, rows):
    t, d = n.shape
    ff = up_bias.shape[1]
    fb = ff // 4
    high, low = up_out[0].shape[0], down[0].shape[0]
    chunk = pl.BlockSpec((fb // 2, d), lambda j, s: (j, 0))
    return call(
        ffn_kernel, "ffn", (4,),
        [whole(t, d), pl.BlockSpec((1, t // 2, d), lambda j, s: (s[SEQ], 0, 0)), whole(t // 4, d), whole(t // 4, d)]
        + [pl.BlockSpec(memory_space=pl.ANY)]
        + [pl.BlockSpec((high, fb), lambda j, s: (0, j))] * 4
        + [pl.BlockSpec((low // 2, 4 * d), lambda j, s: (j % 2, 0))] * 4
        + [pl.BlockSpec((1, fb), lambda j, s: (0, j)), whole(*rows.shape)],
        [whole(t // 2, d)] * 2
        + [pl.BlockSpec((t, fb), lambda j, s: (0, j)), chunk, chunk]
        + [pl.BlockSpec((1, fb), lambda j, s: (0, j)), whole(1, d), whole(t, d)],
        [sds((t // 2, d), bf16)] * 2
        + [sds((t, ff), bf16)]
        + [sds((ff // 2, d), bf16)] * 2
        + [sds((1, ff), f32), sds((1, d), f32), sds((t, d), bf16)],
        [pltpu.VMEM((t, d), f32), pltpu.VMEM((t, fb), bf16), pltpu.VMEM((t, d), f32), pltpu.SemaphoreType.DMA],
        cost(8 * t * d * ff, 20 * t * d + 8 * d * ff, 2 * t * ff),
        at, (n, both, *other, mid, *up_out, *down, up_bias, rows),
    )


def unffn_kernel(at_ref, n_ref, dy_any, mid_any, du_ref, o_any, row_ref, *refs):
    dmid_ref, do_ref, keep_ref, give_ref, small_ref, acc, turned, turned_2 = refs[8:16]
    dy_ref, mid_ref, o_ref, dy_sem, mid_sem, o_sem = refs[16:]
    late = [
        pltpu.make_async_copy(*pair_of)
        for pair_of in ((dy_any, dy_ref, dy_sem), (mid_any, mid_ref, mid_sem), (o_any, o_ref, o_sem))
    ]
    j = pl.program_id(0)
    last = pl.num_programs(0) - 1

    @pl.when(j == 0)
    def _():
        for copy in late:
            copy.start()
        acc[...] = jnp.zeros_like(acc)
        turned[...], turned_2[...] = turn(n_ref[...], at_ref)

    @pl.when(j < last)
    def _():
        du = du_ref[...]
        w = weave_a(refs[:4], at_ref)
        keep_ref[...] = nn(turned[...], du).astype(bf16)
        give_ref[...] = nn(turned_2[...], du).astype(bf16)
        acc[...] += nt(du, w)

    @pl.when(j == last)
    def _():
        for copy in late:
            copy.wait()
        xhat, s = norm_parts(mid_ref[...])
        e = acc[...]
        small_ref[...] = jnp.concatenate(
            [jnp.sum(e * xhat, axis=0, keepdims=True), jnp.sum(e, axis=0, keepdims=True)], axis=0
        )
        dmid = dy_ref[...].astype(f32) + norm_back(e, row_ref[3:4, :], xhat, s)
        dmid_ref[...] = dmid
        db = dmid.astype(bf16)
        do_ref[...] = nt(db, weave_a(refs[4:8], at_ref)).astype(bf16)
        own, other = unweave(tn(o_ref[...], db), at_ref, db.shape[1] // 32)
        keep_ref[...] = own.astype(bf16)
        give_ref[...] = other.astype(bf16)


def unffn(at, n, dy, mid, du, up, out, o, rows):
    t, d = n.shape
    ff = du.shape[1]
    count = ff // d
    cols = pl.BlockSpec((d // 2, d), lambda j, s: (0, j))
    return call(
        unffn_kernel, "unffn", (count + 1,),
        [whole(t, d)] + [pl.BlockSpec(memory_space=pl.ANY)] * 2
        + [pl.BlockSpec((t, d), lambda j, s: (0, jnp.minimum(j, count - 1)))]
        + [pl.BlockSpec(memory_space=pl.ANY), whole(*rows.shape)]
        + [pl.BlockSpec((p.shape[0], d), lambda j, s: (0, jnp.minimum(j, count - 1))) for p in up]
        + last_columns(out, d),
        [whole(t, d)] * 2 + [cols] * 2 + [whole(2, d)],
        [sds((t, d), f32), sds((t, d), bf16)] + [sds((d // 2, ff + d), bf16)] * 2 + [sds((2, d), f32)],
        [pltpu.VMEM((t, d), f32)] + [pltpu.VMEM((d // 2, t), bf16)] * 2
        + [pltpu.VMEM((t, d), bf16), pltpu.VMEM((t, d), f32), pltpu.VMEM((t, d), bf16)]
        + [pltpu.SemaphoreType.DMA] * 3,
        cost(4 * t * d * (ff + d), 20 * t * d + 8 * d * ff),
        at, (n, dy, mid, du, o, rows, *up, *out),
    )


def grad_qkv_kernel(at_ref, n_ref, dq_ref, dk_ref, dv_ref, keep_ref, give_ref, turned, turned_2):
    @pl.when(pl.program_id(0) == 0)
    def _():
        turned[...], turned_2[...] = turn(n_ref[...], at_ref)

    for i, d_ref in enumerate((dq_ref, dk_ref, dv_ref)):
        keep_ref[i] = nn(turned[...], d_ref[...]).astype(bf16)
        give_ref[i] = nn(turned_2[...], d_ref[...]).astype(bf16)


def grad_qkv(at, n, dq, dk, dv, cb=256):
    t, d = n.shape
    tok = pl.BlockSpec((t, cb), lambda i, s: (0, i))
    out = pl.BlockSpec((3, d // 2, cb), lambda i, s: (0, 0, i))
    return call(
        grad_qkv_kernel, "grad_qkv", (d // cb,),
        [whole(t, d)] + [tok] * 3, [out] * 2, [sds((3, d // 2, d), bf16)] * 2,
        [pltpu.VMEM((d // 2, t), bf16)] * 2,
        cost(6 * t * d * d, 20 * t * d), at, (n, dq, dk, dv),
    )


def unqkv_kernel(at_ref, x_any, row_ref, dmid_any, *refs):
    dq_ref, dk_ref, dv_ref, own_ref, send_ref, small_ref, acc, wk_ref = refs[16:24]
    x_ref, dmid_ref, x_sem, dmid_sem = refs[24:]
    i = pl.program_id(0)
    late = [
        pltpu.make_async_copy(x_any, x_ref, x_sem), pltpu.make_async_copy(dmid_any, dmid_ref, dmid_sem)
    ]

    @pl.when(i == 0)
    def _():
        for copy in late:
            copy.start()

    weave_keys(refs[4:12], at_ref, wk_ref)
    w = [weave_a(refs[0:4], at_ref), wk_ref[...], weave_b(refs[12:16], at_ref)]
    e = nt(
        jnp.concatenate([dq_ref[...], dk_ref[...], dv_ref[...]], axis=1),
        jnp.concatenate(w, axis=1),
    )

    @pl.when(i == 0)
    def _():
        acc[...] = e

    @pl.when(i > 0)
    def _():
        acc[...] += e

    @pl.when(i == pl.num_programs(0) - 1)
    def _():
        for copy in late:
            copy.wait()
        e = acc[...]
        xhat, s = norm_parts(x_ref[...].astype(f32) + row_ref[0:1, :])
        d_base = dmid_ref[...] + norm_back(e, row_ref[1:2, :], xhat, s)
        half = d_base.shape[0] // 2
        own, theirs = choose(at_ref[SEQ], d_base[:half], d_base[half:])
        own_ref[...] = own.astype(bf16)
        send_ref[...] = theirs.astype(bf16)
        small_ref[...] = jnp.concatenate(
            [
                jnp.sum(e * xhat, axis=0, keepdims=True),
                jnp.sum(e, axis=0, keepdims=True),
                jnp.sum(d_base, axis=0, keepdims=True),
            ],
            axis=0,
        )


def unqkv(at, x, rows, dmid, w_a, w_b, dq, dk, dv, cb=256):
    t, d = x.shape
    count = d // cb
    specs, args = qkv_columns(w_a, w_b, cb, count)
    tok = pl.BlockSpec((t, cb), lambda i, s: (0, i))
    return call(
        unqkv_kernel, "unqkv", (count,),
        [pl.BlockSpec(memory_space=pl.ANY), whole(*rows.shape), pl.BlockSpec(memory_space=pl.ANY)]
        + specs + [tok] * 3,
        [whole(t // 2, d)] * 2 + [whole(3, d)],
        [sds((t // 2, d), bf16)] * 2 + [sds((3, d), f32)],
        [pltpu.VMEM((t, d), f32), pltpu.VMEM((d, cb), bf16), pltpu.VMEM((t, d), bf16), pltpu.VMEM((t, d), f32)]
        + [pltpu.SemaphoreType.DMA] * 2,
        cost(6 * t * d * d, 30 * t * d), at, (x, rows, dmid, *args, dq, dk, dv),
    )


class Grid:
    def __init__(self, seq, rows):
        self.seq, self.rows = seq, rows
        self.known = seq == 2 and rows == 16
        at = lax.axis_index("rows")
        self.x = lax.axis_index("seq")
        self.z, self.y, self.c = at // 4, (at // 2) % 2, at % 2

    def table(self, move):
        pairs = []
        for x in range(self.seq):
            for z in range(4):
                for y in range(2):
                    for c in range(2):
                        x2, z2, y2, c2 = move(x, z, y, c)
                        pairs.append((x * 16 + z * 4 + y * 2 + c, x2 * 16 + z2 * 4 + y2 * 2 + c2))
        return pairs

    def swap(self, v, axis):
        move = {
            "x": lambda x, z, y, c: (1 - x, z, y, c),
            "y": lambda x, z, y, c: (x, z, 1 - y, c),
            "c": lambda x, z, y, c: (x, z, y, 1 - c),
        }[axis]
        return lax.ppermute(v, BOTH, self.table(move))

    def cross(self, v, bit):
        return lax.ppermute(v, BOTH, self.table(lambda x, z, y, c: (x, z ^ bit, y, c)))

    def shift(self, v, by):
        return lax.ppermute(v, BOTH, self.table(lambda x, z, y, c: (x, (z + by) % 4, y, c)))


def tie(*values):
    return lax.optimization_barrier(values)


def after(v, *first):
    return lax.optimization_barrier((v, first))[0]


def spread(v, axis, count):
    return jnp.broadcast_to(jnp.expand_dims(v, axis), v.shape[:axis] + (count,) + v.shape[axis:])


def pair(own, other, at, axis):
    shape = own.shape[:axis] + (2,) + own.shape[axis:]
    here = lax.broadcasted_iota(jnp.int32, shape, axis) == at
    return jnp.where(here, spread(own, axis, 2), spread(other, axis, 2))


def arrange_z(g, v, shifts):
    out = spread(v, 0, 4)
    place = lax.broadcasted_iota(jnp.int32, out.shape, 0)
    for k, got in enumerate(shifts):
        out = jnp.where(place == (g.z - k - 1) % 4, spread(got, 0, 4), out)
    return out


def gather_z(g, v):
    return arrange_z(g, v, [g.shift(v, k) for k in range(1, 4)])


def flat(v):
    return v.reshape(-1, v.shape[-1])


def quarters(whole_array, kind):
    v = whole_array.reshape(2, 4, 2, 2, -1, whole_array.shape[1])
    pieces = []
    for core in range(2):
        for place in range(2):
            pieces.append(flat(v[:, :, place, core] if kind == "a" else v[place, :, :, core]))
    return pieces


def keep(v, at, axis):
    return lax.dynamic_index_in_dim(v, at, axis, keepdims=False)


def add(a, b):
    return (a.astype(f32) + b.astype(f32)).astype(bf16)


def split_plane(g, a, b):
    a = add(keep(a, g.x, -5), g.swap(keep(a, 1 - g.x, -5), "x"))
    b = add(keep(b, g.y, -3), g.swap(keep(b, 1 - g.y, -3), "y"))
    a, b = yield a, b
    got_a = g.swap(keep(a, 1 - g.y, -3), "y")
    got_b = g.swap(keep(b, 1 - g.x, -4), "x")
    got_a, got_b = yield got_a, got_b
    yield add(keep(a, g.y, -3), got_a), add(keep(b, g.x, -4), got_b)


def split_z(g, v):
    total = keep(v, g.z, -3).astype(f32)
    for k in range(1, 4):
        total = total + g.shift(keep(v, (g.z + k) % 4, -3), k).astype(f32)
    return total


def halve_z(g, v):
    v = v.reshape(*v.shape[:-3], 2, 2, *v.shape[-2:])
    high, low = g.z // 2, g.z % 2
    v = keep(v, low, -3).astype(f32) + g.cross(keep(v, 1 - low, -3), 1).astype(f32)
    got = yield g.cross(keep(v, 1 - high, -3).astype(bf16), 2)
    yield keep(v, high, -3) + got.astype(f32)


def scatter_plain(own, other):
    v = jnp.stack([own.reshape(16, -1, own.shape[1]), other.reshape(16, -1, own.shape[1])], axis=1)
    return lax.psum_scatter(flat(v).astype(f32), BOTH, scatter_dimension=0, tiled=True)


def swap_seq(v):
    return lax.ppermute(v, "seq", [(0, 1), (1, 0)])


def local(
    inputs, timesteps, boundary, step_table, w_qkv, w_out, w_up, w_down,
    norm1_gain, norm1_shift, norm2_gain, norm2_shift, up_bias, down_bias, cotangent,
):
    seq, row_blocks = lax.axis_size("seq"), lax.axis_size("rows")
    g = Grid(seq, row_blocks)
    devices = seq * row_blocks
    d = inputs.shape[2]
    shard = w_qkv.shape[0]
    ff = w_up.shape[1]
    steps = step_table.shape[0]
    wide = (ff // devices) // shard
    short = (g.x < boundary[0]).astype(jnp.int32)
    zero = jnp.zeros_like(short)
    at = jnp.stack([short, g.x] + ([g.y, g.x, g.c] if g.known else [zero] * 3))

    digits = jnp.concatenate([timesteps // 128, timesteps % 128]).astype(bf16)
    shorts = jnp.concatenate(
        [norm1_gain, norm1_shift, norm2_gain, norm2_shift, down_bias, up_bias, digits]
    )
    shorts = jnp.broadcast_to(shorts[None], (devices,) + shorts.shape)
    shorts = lax.all_to_all(shorts, BOTH, split_axis=0, concat_axis=0, tiled=True)
    x_other = swap_seq(keep(inputs, 1 - g.x, 0))
    unit = w_down.shape[0] // 4
    down_wide = w_down.reshape(4, unit, d).transpose(1, 0, 2).reshape(unit, -1)

    def look_up(shorts):
        digits = shorts[:, (5 + wide) * shard :].reshape(seq, row_blocks, 2, -1)[0].astype(jnp.int32)
        all_steps = digits[:, 0] * 128 + digits[:, 1]
        hot = all_steps.T.reshape(-1)[:, None] == jnp.arange(steps, dtype=jnp.int32)[None]
        found = nn(hot.astype(bf16), step_table).astype(bf16)
        found = lax.all_to_all(found, BOTH, split_axis=0, concat_axis=0, tiled=True)
        return all_steps.reshape(-1), found

    def norm_rows(shorts, found):
        rows = jnp.stack([found] + [shorts[:, i * shard : (i + 1) * shard] for i in range(5)])
        return jnp.pad(rows.reshape(6, d).astype(f32), ((0, 2), (0, 0)))

    if g.known:
        shifts = [g.shift(w_qkv, k) for k in range(1, 4)]
        rest = jnp.concatenate([w_up, w_out, down_wide], axis=1)
        rest_2 = g.cross(rest, 2)
        first = arrange_z(g, w_qkv, shifts)
        half = d + 2 * d // 3
        a, b = first[..., :half], first[..., half:]
        a = pair(a, g.swap(a, "x"), g.x, 0)
        b = pair(b, g.swap(b, "y"), g.y, 1)
        a, b, x_other, shorts, rest_2 = tie(a, b, x_other, shorts, rest_2)
        rest = pair(rest, rest_2, g.z // 2, 0)
        rest_1 = g.cross(rest, 1)
        all_steps, found = look_up(shorts)
        a_2, b_2 = g.swap(a, "y"), g.swap(b, "x")
        a_c, b_c = g.swap(a, "c"), g.swap(b, "c")
        w_a = [flat(v) for v in (a, a_2, a_c, g.swap(a_2, "c"))]
        w_b = [flat(v) for v in (b, b_2, b_c, g.swap(b_2, "c"))]
        rest, rest_1, found, a_2, b_2 = tie(rest, rest_1, found, a_2, b_2)
        rest = pair(rest, rest_1, g.z % 2, 1)
        rest = rest.reshape(4, *rest.shape[2:])
        rows = norm_rows(shorts, found)
        x, normed_one = norm_one(at, inputs, x_other, rows)
        a, b = rest[..., : ff + d], rest[..., ff + d :]
        a = pair(a, g.swap(a, "x"), g.x, 0)
        b = pair(b, g.swap(b, "y"), g.y, 1)
        a, b, normed_one = tie(a, b, normed_one)
        a_2, b_2 = g.swap(a, "y"), g.swap(b, "x")
        a_c, b_c = g.swap(a, "c"), g.swap(b, "c")
    else:
        half = d + 2 * d // 3
        w_a, w_b, up_out, down = [
            quarters(lax.all_gather(v, BOTH, axis=0, tiled=True), kind)
            for v, kind in (
                (w_qkv[:, :half], "a"),
                (w_qkv[:, half:], "b"),
                (jnp.concatenate([w_up, w_out], axis=1), "a"),
                (down_wide, "b"),
            )
        ]
        all_steps, found = look_up(shorts)
        rows = norm_rows(shorts, found)
        x, normed_one = norm_one(at, inputs, x_other, rows)

    up_row = shorts[:, 5 * shard : (5 + wide) * shard].reshape(1, ff)
    q, k, v, attended, lse = attend(at, normed_one, w_a, w_b)
    dy_send = keep(cotangent, 1 - g.x, 0)
    dy_other = [swap_seq(v) for v in jnp.split(dy_send, 2)]
    if g.known:
        q, k, v, lse, attended, dy_other[0] = tie(q, k, v, lse, attended, dy_other[0])
        a_2, b_2, attended = tie(a_2, b_2, attended)
        out = [flat(v) for v in (a, a_2, a_c, g.swap(a_2[..., ff:], "c"))]
        up_out = [flat(v) for v in (a, a_2, a_c, g.swap(a_2, "c"))]
        down = [flat(v) for v in (b, b_2, b_c, g.swap(b_2, "c"))]
    else:
        out = up_out
    middle, normed_two = mix(at, x, attended, out, rows)
    block_own, block_send, d_upper, keep_down, give_down, g_up_row, g_down_row, dy = ffn(
        at, normed_two, cotangent, dy_other, middle, up_out, down, up_row, rows
    )
    block_other = swap_seq(block_send)
    d_middle, d_attended, keep_up, give_up, small_two = unffn(
        at, normed_two, dy, middle, d_upper, up_out, out, attended, rows
    )
    six = (2, 4, 2)
    if g.known:
        d_middle, d_attended, keep_up, give_up, small_two, block_other = tie(
            d_middle, d_attended, keep_up, give_up, small_two, block_other
        )
        down = add(keep_down, g.swap(give_down, "c")).reshape(*six, -1, d)
        d_attended, down = tie(d_attended, down)
        down_plane = split_plane(g, down[..., : d // 2], down[..., d // 2 :])
    back = attend_back(at, q, k, v, attended, d_attended, lse, 0, 2)
    if g.known:
        cut = (ff + d) // 2
        up = add(keep_up, g.swap(give_up, "c")).reshape(*six, -1, ff + d)
        down_half = next(down_plane)
        d_attended, up, down_half, *back = tie(d_attended, up, down_half, *back)
        up_plane = split_plane(g, up[..., :cut], up[..., cut:])
        down_got = down_plane.send(down_half)
    dq, dk, dv = attend_back(at, q, k, v, attended, d_attended, lse, 1, 2, tuple(back))
    n = normed_one
    if g.known:
        up_half = next(up_plane)
        n, up_half, dq, down_got = tie(n, up_half, dq, down_got)
        up_got = up_plane.send(up_half)
        down = jnp.concatenate(down_plane.send(down_got), axis=-1)
        down_z = halve_z(g, down)
    keep_qkv, give_qkv = grad_qkv(at, n, dq, dk, dv)
    if g.known:
        keep_qkv, up_got = tie(keep_qkv, up_got)
        qkv = add(keep_qkv, g.swap(give_qkv, "c")).reshape(3, *six, shard, d)
        up = jnp.concatenate(up_plane.send(up_got), axis=-1)
        d_middle, qkv, up = tie(d_middle, qkv, up)
        a = jnp.concatenate([qkv[0], qkv[1, ..., : d // 2]], axis=-1)
        b = jnp.concatenate([qkv[1, ..., d // 2 :], qkv[2]], axis=-1)
        plane = split_plane(g, a, b)
    d_own, d_send, small_one = unqkv(at, x, rows, d_middle, w_a, w_b, dq, dk, dv)
    if g.known:
        ready = next(plane)
        small_one, d_send, ready, down_got = tie(small_one, d_send, ready, next(down_z))
        sum_down = down_z.send(down_got)
        up_z = halve_z(g, up)
        got_a, got_b = plane.send(ready)
        small_one, got_a = tie(small_one, got_a)
        got = (got_a, got_b)
    d_other = swap_seq(d_send)

    small = jnp.concatenate([small_two, g_down_row, small_one], axis=0)
    small = small.reshape(-1, devices, shard).transpose(1, 0, 2).reshape(devices, -1)
    small = jnp.concatenate([small, g_up_row.reshape(devices, -1)], axis=1)
    small = lax.all_to_all(small, BOTH, split_axis=0, concat_axis=0, tiled=True)
    row_sums = small[:, 5 * shard : 6 * shard].reshape(seq, row_blocks, shard).transpose(1, 0, 2)
    row_sums = row_sums.reshape(devices, shard)
    small = jnp.sum(small, axis=0)
    if g.known:
        sum_up = up_z.send(next(up_z))
        last = jnp.concatenate(plane.send(got), axis=-1)
        block_out = pair(block_own, block_other, g.x, 0)
        d_other, last, block_out = tie(d_other, split_z(g, last), block_out)
    else:
        sum_up, sum_down = scatter_plain(keep_up, give_up), scatter_plain(keep_down, give_down)
        last = [scatter_plain(keep_qkv[i], give_qkv[i]) for i in range(3)]
        last = jnp.concatenate(last, axis=1)
        block_out = pair(block_own, block_other, g.x, 0)
    grad_inputs = pair(d_own, d_other, g.x, 0)
    hot = (jnp.arange(steps, dtype=jnp.int32)[:, None] == all_steps[None]).astype(f32)
    g_table = lax.dot_general(
        hot, row_sums, (((1,), (0,)), ((), ())), precision=lax.Precision.HIGHEST,
        preferred_element_type=f32,
    )
    return (
        block_out,
        grad_inputs,
        g_table,
        last,
        sum_up[:, ff:],
        sum_up[:, :ff],
        sum_down,
        *[small[i * shard : (i + 1) * shard] for i in (3, 4, 0, 1)],
        small[6 * shard :],
        small[2 * shard : 3 * shard],
    )


def solution(mesh):
    tokens, weight, vector = P("rows", "seq", None), P(BOTH, None), P(BOTH)
    table = P(None, BOTH)
    in_specs = (
        (tokens, P("rows"), P("rows"), table) + (weight,) * 4 + (vector,) * 6 + (tokens,)
    )
    out_specs = (tokens, tokens, table) + (weight,) * 4 + (vector,) * 6
    return jax.shard_map(local, mesh=mesh, in_specs=in_specs, out_specs=out_specs, check_vma=False)
```
